512 devices in a mesh: seq: 128 (over z, x, core), row: 2 (over y_hi), col: 2 (over y_lo).
Axes of the slice: x: 4, y: 4 (y_hi: 2, y_lo: 2; y = y_hi * 2 + y_lo), z: 16, core: 2. Of those that a mesh axis runs over, the one named last changes fastest.
Arguments:
- atom_single: bfloat16 [16384, 128], P('seq'), may hold values from -6 to 6
- token_single: bfloat16 [2048, 384], P('seq', 'row'), may hold values from -6 to 6
- pair_band: bfloat16 [2048, 80, 128], P(('seq', 'row'), 'col'), may hold values from -6 to 6
- token_counts: int32 [2048], P('seq'), may hold values from 1 to 23, as said below
- atom_token: int32 [16384], P('seq'), may hold values from 0 to 2047, as said below
- window_starts: int32 [512], P('seq'), may hold values from 0 to 16256, as said below
- single_proj: bfloat16 [384, 128], P('row'), may hold values from -0.3125 to 0.3125
- pair_proj: float32 [128, 12], replicated, may hold values from -6 to 6
- attn_in: bfloat16 [3, 128, 512], replicated, may hold values from -0.5 to 0.5
- attn_out: bfloat16 [3, 128, 128], replicated, may hold values from -0.5 to 0.5
- trans_in: bfloat16 [3, 128, 512], replicated, may hold values from -0.5 to 0.5
- trans_out: bfloat16 [3, 256, 128], replicated, may hold values from -0.375 to 0.375
- agg_proj: bfloat16 [128, 768], P(None, 'row'), may hold values from -0.5 to 0.5
- token_cot: bfloat16 [2048, 768], P('seq', 'row'), may hold values from -6 to 6
Outputs:
- token_act: bfloat16 [2048, 768], P('seq', 'row')
- atom_grad: bfloat16 [16384, 128], P('seq')
- single_grad: bfloat16 [2048, 384], P('seq', 'row')
The draws below stay inside these ranges and needn't reach their ends.
Inputs may be any that keep to these rules, and one draw needn't show every extreme that they name: `token_counts`: the counts of each aligned block of 16 tokens sum to 128 plus a difference of drifts: the first atom of the tokens of block j lies within 32 atoms of atom 8 * 16 * j, and that distance occurs in every draw. Tokens 2k and 2k + 1 together own at least 8 atoms, exactly 8 in some pair of every draw. `atom_token`: atoms are ordered by token: token t owns token_counts[t] consecutive atoms. `window_starts`: the window of query block b starts between 64 and 32 atoms before its first atom, clipped to the atoms; both ends occur in every draw.
All inputs are finite; a program needn't handle non-finite values.
Results may differ from the reference program's by a relative error of at most 0.015.
The reference program's roundings to bfloat16 on the way count: a program that leaves them out, or rounds other values in their place, can miss the bound.
Values may be sent and summed in bfloat16 or wider, within the bound.
A program may use at most 128 MiB of HBM per device.

```python
import jax
import jax.numpy as jnp
from jax import lax

CA = 128
CS = 384
CZ = 128
CT = 768
HEADS = 4
QB = 32
KW = 128
LAYERS = 3
TOK_DEV = 16
ATOM_DEV = 128
NTOK = 2048
ATOMS = 16384
FFA = 256


def token_layout(key):
    key_drift, key_split, key_place = jax.random.split(key, 3)
    block_count = NTOK // TOK_DEV
    drifts = jax.random.randint(key_drift, (block_count + 1,), -4, 5)
    places = jnp.arange(block_count + 1)
    chosen = jax.random.randint(key_place, (), 2, block_count - 1)
    drifts = jnp.where(places == chosen, -4, jnp.where(places == chosen + 1, 4, drifts))
    drifts = jnp.where(places == chosen - 1, 4, drifts)
    drifts = jnp.where((places == 0) | (places == block_count), 0, drifts)
    pair_sums = 16 + drifts[1:] - drifts[:-1]
    pair_count = TOK_DEV // 2
    raw = jax.random.randint(key_split, (block_count, pair_count), 0, 1 << 20)
    first = 1 + raw % (pair_sums[:, None] - 1)
    forced = (jnp.arange(block_count)[:, None] == chosen) & (jnp.arange(pair_count)[None, :] == 0)
    first = jnp.where(forced, 1, first)
    second = pair_sums[:, None] - first
    return jnp.stack([first, second], -1).reshape(NTOK).astype(jnp.int32)


def draw_token_counts(key, part):
    counts = token_layout(key)
    return counts


def draw_atom_token(key, part):
    counts = token_layout(key)
    return jnp.repeat(jnp.arange(NTOK, dtype=jnp.int32), counts, total_repeat_length=ATOMS).astype(jnp.int32)


def draw_window_starts(key, part):
    key = jax.random.fold_in(key, 7)
    key_offset, key_place = jax.random.split(key)
    block_total = ATOMS // QB
    reach = 2 * (KW // 2) + QB - KW
    offsets = jax.random.randint(key_offset, (block_total,), 0, reach + 1)
    chosen = jax.random.randint(key_place, (), ATOM_DEV // QB, block_total - ATOM_DEV // QB - 1)
    places = jnp.arange(block_total)
    offsets = jnp.where(places == chosen, 0, jnp.where(places == chosen + 1, reach, offsets))
    starts = places * QB - KW // 2 + offsets
    return jnp.clip(starts, 0, ATOMS - KW).astype(jnp.int32)


def draw_pair_proj(key, part):
    key = jax.random.fold_in(key, 11)
    return jax.random.normal(key, (CZ, LAYERS * HEADS), jnp.float32) * CZ ** (-0.5)


def shard_levels(stream_key, dims, pieces, low, high):
    level, own = 1.0, jax.random.fold_in(stream_key, 6)
    for axis_at, parts in pieces:
        draws = jnp.exp(jax.random.uniform(jax.random.fold_in(own, axis_at), (parts,), jnp.float32, low / len(pieces), high / len(pieces)))
        level = level * jnp.repeat(draws, dims[axis_at] // parts).reshape([-1 if axis == axis_at else 1 for axis in range(len(dims))])
    return level


def bell_draw(own_key, dims, scale, limit, cuts=(), held_as=jnp.bfloat16):
    values = scale * jax.random.normal(own_key, dims, jnp.float32)
    if cuts:
        values = values * shard_levels(own_key, dims, cuts, -0.22, 0.18)
    return jnp.clip(values, -limit, limit).astype(held_as)


def setup_inputs(seed: int = 0) -> dict:
    streams_of = jax.random.split(jax.random.key(seed), 15)
    return {
        "atom_single": bell_draw(streams_of[0], (ATOMS, CA), 1.0, 6.0, ((0, 128),)),
        "token_single": bell_draw(streams_of[1], (NTOK, CS), 1.0, 6.0, ((0, 128), (1, 2))),
        "pair_band": bell_draw(streams_of[2], (NTOK, 5 * TOK_DEV, CZ), 1.0, 6.0, ((0, 256), (1, 2))),
        "token_counts": draw_token_counts(jax.random.fold_in(streams_of[14], 71), 0),
        "atom_token": draw_atom_token(jax.random.fold_in(streams_of[14], 71), 0),
        "window_starts": draw_window_starts(jax.random.fold_in(streams_of[14], 71), 0),
        "single_proj": bell_draw(streams_of[6], (CS, CA), CS ** -0.5, 0.3125, ((0, 2),)),
        "pair_proj": draw_pair_proj(jax.random.fold_in(streams_of[14], 71), 0),
        "attn_in": bell_draw(streams_of[8], (LAYERS, CA, 4 * CA), CA ** -0.5, 0.5),
        "attn_out": bell_draw(streams_of[9], (LAYERS, CA, CA), CA ** -0.5, 0.5),
        "trans_in": bell_draw(streams_of[10], (LAYERS, CA, 2 * FFA), CA ** -0.5, 0.5),
        "trans_out": bell_draw(streams_of[11], (LAYERS, FFA, CA), FFA ** -0.5, 0.375),
        "agg_proj": bell_draw(streams_of[12], (CA, CT), CA ** -0.5, 0.5, ((1, 2),)),
        "token_cot": bell_draw(streams_of[13], (NTOK, CT), 1.0, 6.0, ((0, 128), (1, 2))),
    }


epsilon = 1e-05
highest = lax.Precision.HIGHEST

def layer_norm(values):
    centre = values - lax.optimization_barrier(jnp.mean(values, axis=-1, keepdims=True))
    spread = lax.optimization_barrier(jnp.mean(centre * centre, axis=-1, keepdims=True))
    return centre * lax.rsqrt(spread + epsilon)

def norm_back(values, upstream):
    centre = values - lax.optimization_barrier(jnp.mean(values, axis=-1, keepdims=True))
    scaling = lax.rsqrt(lax.optimization_barrier(jnp.mean(centre * centre, axis=-1, keepdims=True)) + epsilon)
    normal = centre * scaling
    return scaling * (upstream - lax.optimization_barrier(jnp.mean(upstream, axis=-1, keepdims=True)) - normal * lax.optimization_barrier(jnp.mean(upstream * normal, axis=-1, keepdims=True)))

def silu_grad(values):
    sigmoid_v = jax.nn.sigmoid(values)
    return sigmoid_v * (1.0 + values * (1.0 - sigmoid_v))

def pair_bias(pair_band, pair_proj):
    token_blocks = pair_band.reshape(NTOK // TOK_DEV, TOK_DEV, 5 * TOK_DEV, CZ)

    def one_block(block):
        normal = layer_norm(block.astype(jnp.float32))
        result = jnp.dot(normal.reshape(-1, CZ), pair_proj, precision=highest)
        return result.astype(jnp.bfloat16)
    return lax.map(one_block, token_blocks).reshape(NTOK * 5 * TOK_DEV, LAYERS * HEADS)

def reference(atom_single, token_single, pair_band, token_counts, atom_token, window_starts, single_proj, pair_proj, attn_in, attn_out, trans_in, trans_out, agg_proj, token_cot):
    head_dim = CA // HEADS
    score_scale = head_dim ** (-0.5)
    halo_width = KW // 2
    block_total = ATOMS // QB
    tok_cond = jnp.dot(token_single, single_proj, preferred_element_type=jnp.float32).astype(jnp.bfloat16)
    stream = atom_single.astype(jnp.float32) + tok_cond.astype(jnp.float32)[atom_token]
    bias_table = pair_bias(pair_band, pair_proj)
    key_index = window_starts[:, None] + jnp.arange(KW, dtype=jnp.int32)[None, :]
    query_tokens = atom_token.reshape(block_total, QB)
    key_tokens = atom_token[key_index]
    column = key_tokens[:, None, :] - TOK_DEV * (query_tokens[:, :, None] // TOK_DEV) + 2 * TOK_DEV
    flat_index = query_tokens[:, :, None] * (5 * TOK_DEV) + column
    bias_gathered = bias_table[flat_index]
    saved = []
    for layer in range(LAYERS):
        layer_bias = jnp.transpose(bias_gathered[..., layer * HEADS:(layer + 1) * HEADS], (0, 3, 1, 2)).astype(jnp.float32)
        normed = layer_norm(stream).astype(jnp.bfloat16)
        projected = jnp.dot(normed, attn_in[layer], preferred_element_type=jnp.float32)
        queries = projected[:, :CA].astype(jnp.bfloat16)
        key_value = projected[:, CA:3 * CA].astype(jnp.bfloat16)
        gating = jax.nn.sigmoid(projected[:, 3 * CA:])
        padded = jnp.pad(key_value, ((halo_width, halo_width), (0, 0)))
        windows = padded[key_index + halo_width].astype(jnp.float32).reshape(block_total, KW, 2, HEADS, head_dim)
        query_blocks = queries.astype(jnp.float32).reshape(block_total, QB, HEADS, head_dim)
        scores = jnp.einsum('bqhd,bkhd->bhqk', query_blocks, windows[:, :, 0], precision=highest) * score_scale + layer_bias
        softmaxed = jax.nn.softmax(scores, axis=-1)
        rounded = softmaxed.astype(jnp.bfloat16)
        attended = jnp.einsum('bhqk,bkhd->bqhd', rounded.astype(jnp.float32), windows[:, :, 1], precision=highest).reshape(ATOMS, CA)
        gated = (gating * attended).astype(jnp.bfloat16)
        x_mid = stream + jnp.dot(gated, attn_out[layer], preferred_element_type=jnp.float32)
        normed_mid = layer_norm(x_mid).astype(jnp.bfloat16)
        widened = jnp.dot(normed_mid, trans_in[layer], preferred_element_type=jnp.float32)
        part_a = widened[:, :FFA]
        part_b = widened[:, FFA:]
        transit = (jax.nn.silu(part_a) * part_b).astype(jnp.bfloat16)
        x_next = x_mid + jnp.dot(transit, trans_out[layer], preferred_element_type=jnp.float32)
        saved.append((stream, query_blocks, padded, gating, attended, softmaxed, rounded, x_mid, part_a, part_b))
        stream = x_next
    final_rounded = stream.astype(jnp.bfloat16)
    pre = jnp.dot(final_rounded, agg_proj, preferred_element_type=jnp.float32)
    token_sums = jax.ops.segment_sum(jax.nn.silu(pre), atom_token, num_segments=NTOK)
    counts = token_counts.astype(jnp.float32)
    token_act = (token_sums / counts[:, None]).astype(jnp.bfloat16)
    inverse = (1.0 / counts)[atom_token]
    d_act = token_cot.astype(jnp.float32)[atom_token] * inverse[:, None]
    d_pre = d_act * silu_grad(pre)
    gradient = jnp.dot(d_pre, agg_proj.astype(jnp.float32).T, precision=highest)
    for layer in range(LAYERS - 1, -1, -1):
        stream, query_blocks, padded, gating, attended, softmaxed, rounded, x_mid, part_a, part_b = saved[layer]
        d_transit = jnp.dot(gradient, trans_out[layer].astype(jnp.float32).T, precision=highest)
        d_part_a = d_transit * part_b * silu_grad(part_a)
        d_part_b = d_transit * jax.nn.silu(part_a)
        d_normed_mid = jnp.dot(jnp.concatenate([d_part_a, d_part_b], 1), trans_in[layer].astype(jnp.float32).T, precision=highest)
        d_mid = gradient + norm_back(x_mid, d_normed_mid)
        d_gated = jnp.dot(d_mid, attn_out[layer].astype(jnp.float32).T, precision=highest)
        d_att = (d_gated * gating).reshape(block_total, QB, HEADS, head_dim)
        d_gate = d_gated * attended * gating * (1.0 - gating)
        windows = padded[key_index + halo_width].astype(jnp.float32).reshape(block_total, KW, 2, HEADS, head_dim)
        d_soft = jnp.einsum('bqhd,bkhd->bhqk', d_att, windows[:, :, 1], precision=highest)
        d_scores = softmaxed * (d_soft - lax.optimization_barrier(jnp.sum(softmaxed * d_soft, axis=-1, keepdims=True))) * score_scale
        d_queries = jnp.einsum('bhqk,bkhd->bqhd', d_scores, windows[:, :, 0], precision=highest).reshape(ATOMS, CA)
        d_keys = jnp.einsum('bhqk,bqhd->bkhd', d_scores, query_blocks, precision=highest).reshape(block_total, KW, CA)
        d_values = jnp.einsum('bhqk,bqhd->bkhd', rounded.astype(jnp.float32), d_att, precision=highest).reshape(block_total, KW, CA)
        d_windows = jnp.concatenate([d_keys, d_values], -1).reshape(-1, 2 * CA)
        d_padded = jnp.zeros((ATOMS + 2 * halo_width, 2 * CA), jnp.float32).at[(key_index + halo_width).reshape(-1)].add(d_windows)
        d_key_value = d_padded[halo_width:halo_width + ATOMS]
        d_projected = jnp.concatenate([d_queries, d_key_value, d_gate], 1)
        d_normed = jnp.dot(d_projected, attn_in[layer].astype(jnp.float32).T, precision=highest)
        gradient = d_mid + norm_back(stream, d_normed)
    atom_grad = gradient.astype(jnp.bfloat16)
    d_cond = jax.ops.segment_sum(gradient, atom_token, num_segments=NTOK)
    single_grad = jnp.dot(d_cond, single_proj.astype(jnp.float32).T, precision=highest).astype(jnp.bfloat16)
    return (token_act, atom_grad, single_grad)
```

```python
import functools

import jax
import jax.numpy as jnp
from jax import lax
from jax.experimental import pallas as pl
from jax.experimental.pallas import tpu as pltpu
from jax.sharding import PartitionSpec as P

HEADS = 4
QB = 32
KW = 128
LAYERS = 3
ATOMS = 128
CA = 128
TOK = 16
COND = 192
ACT = 384
FFA = 256
PAIR_ROWS = 8
PAIR_COLS = 40
PAIR_PAD = 48
SPAN = 3 * TOK
HALF = 64
EXT = 256
ALL = HEADS * ATOMS
F32 = jnp.float32
BF16 = jnp.bfloat16
EPS = 1e-05
SCALE = (CA // HEADS) ** (-0.5)
MESH = pl.DeviceIdType.MESH

PARTNERS = [
    (ds, dr, dc)
    for ds in (0, -1, 1)
    for dr in (0, 1)
    for dc in (0, 1)
    if (ds, dr, dc) != (0, 0, 0)
]
COND_PARTNERS = [p for p in PARTNERS if p[2] == 0]
SIDES = (-1, 1)


def nn(a, b):
    return lax.dot_general(a, b, (((1,), (0,)), ((), ())), preferred_element_type=F32)


def nt(a, b):
    return lax.dot_general(a, b, (((1,), (1,)), ((), ())), preferred_element_type=F32)


def flip(values):
    return jnp.transpose(values, (1, 0))


def iota(shape, dim):
    return lax.broadcasted_iota(jnp.int32, shape, dim)


def norm_rows(values):
    centre = values - jnp.mean(values, axis=0, keepdims=True)
    scaling = lax.rsqrt(jnp.mean(centre * centre, axis=0, keepdims=True) + EPS)
    return centre * scaling, scaling


def norm_back(normal, scaling, upstream):
    return scaling * (
        upstream
        - jnp.mean(upstream, axis=0, keepdims=True)
        - normal * jnp.mean(upstream * normal, axis=0, keepdims=True)
    )


def by_head(rows):
    head = iota(rows.shape, 1) // (CA // HEADS)
    return jnp.concatenate(
        [jnp.where(head == h, rows, 0.0).astype(BF16) for h in range(HEADS)], axis=0
    )


def split(values):
    high = values.astype(BF16)
    return high, (values - high.astype(F32)).astype(BF16)


def kernel(
    atom_ref,
    single_ref,
    band_ref,
    counts_ref,
    ids_ref,
    starts_ref,
    proj_ref,
    pair_proj_ref,
    attn_in_ref,
    attn_out_ref,
    trans_in_ref,
    trans_out_ref,
    agg_ref,
    cot_ref,
    act_out,
    grad_out,
    single_out,
    id_buf,
    halo_buf,
    cond_buf,
    pair_buf,
    cot_buf,
    agg_buf,
    kv,
    bias,
    mixed,
    gate_t,
    out_t,
    in_t,
    down_t,
    soft,
    soft_b,
    q_heads,
    key_t,
    normal_x,
    scale_x,
    normal_m,
    scale_m,
    gating,
    gate_back,
    silu_a,
    back_a,
    dkv_send,
    dkv_recv,
    sums_send,
    sums_recv,
    cond_send,
    cond_recv,
    send_sem,
    recv_sem,
):
    seq = lax.axis_index("seq")
    row = lax.axis_index("row")
    col = lax.axis_index("col")
    seqs = lax.axis_size("seq")

    def partner(ds, dr, dc):
        return (
            lax.rem(seq + ds + seqs, seqs),
            lax.rem(row + dr, 2),
            lax.rem(col + dc, 2),
        )

    copies = []

    def send(src, dst, ds, dr=0, dc=0):
        place = len(copies)
        copy = pltpu.make_async_remote_copy(
            src_ref=src,
            dst_ref=dst,
            send_sem=send_sem.at[place],
            recv_sem=recv_sem.at[place],
            device_id=partner(ds, dr, dc),
            device_id_type=MESH,
        )
        copy.start()
        copies.append(copy)
        return copy

    barrier = pltpu.get_barrier_semaphore()
    for ds, dr, dc in PARTNERS:
        pl.semaphore_signal(barrier, inc=1, device_id=partner(ds, dr, dc), device_id_type=MESH)

    cond_buf[1, 0] = nn(single_ref[...], proj_ref[...])
    place_h = (iota((LAYERS * HEADS, CA), 1) == 8 * iota((LAYERS * HEADS, CA), 0)).astype(BF16)
    pp_high, pp_rest = split(pair_proj_ref[...])
    spread_high = nn(pp_high, place_h).astype(BF16)
    spread_rest = nn(pp_rest, place_h).astype(BF16)
    band = band_ref[...].astype(F32).reshape(PAIR_ROWS * PAIR_COLS, CA)
    centre = band - jnp.mean(band, axis=1, keepdims=True)
    normal = centre * lax.rsqrt(jnp.mean(centre * centre, axis=1, keepdims=True) + EPS)
    n_high, n_rest = split(normal)
    pairs = nn(n_high, spread_high) + nn(n_high, spread_rest) + nn(n_rest, spread_high)
    tile = pairs[:PAIR_COLS]
    for i in range(1, PAIR_ROWS):
        tile = tile + pltpu.roll(pairs[PAIR_COLS * i : PAIR_COLS * (i + 1)], i, 1)
    tile = jnp.concatenate([tile, jnp.zeros((PAIR_PAD - PAIR_COLS, CA), F32)], axis=0)
    pair_rows = pl.ds(pl.multiple_of(col * PAIR_PAD, 16), PAIR_PAD)
    pair_lanes = pl.ds(pl.multiple_of(row * CA, CA), CA)
    pair_buf[1, pair_rows, pair_lanes] = tile.astype(BF16)
    cot_buf[1, 0] = cot_ref[...]

    pl.semaphore_wait(barrier, len(PARTNERS))

    cond_copies = [
        send(cond_buf.at[1, 0], cond_buf.at[1 - ds, dr], ds, dr) for ds, dr, dc in COND_PARTNERS
    ]
    id_copies = [send(ids_ref, id_buf.at[1 - ds], ds) for ds in SIDES]
    halo_copies = [
        send(atom_ref.at[pl.ds(0, HALF)], halo_buf.at[pl.ds(0, HALF)], -1),
        send(atom_ref.at[pl.ds(HALF, HALF)], halo_buf.at[pl.ds(HALF, HALF)], 1),
    ]
    pair_copies = [
        send(
            pair_buf.at[1, pair_rows, pair_lanes],
            pair_buf.at[1 - ds, pair_rows, pair_lanes],
            ds,
            dr,
            dc,
        )
        for ds, dr, dc in PARTNERS
    ]
    cot_copies = [
        send(cot_buf.at[1, 0], cot_buf.at[1 - ds, dr], ds, dr) for ds, dr, dc in COND_PARTNERS
    ]
    agg_copy = send(agg_ref, agg_buf, 0, 1)

    for n in range(LAYERS):
        gate_t[n] = flip(attn_in_ref[n, :, 3 * CA :])
        out_t[n] = flip(attn_out_ref[n])
        in_t[n] = flip(trans_in_ref[n])
        down_t[n] = flip(trans_out_ref[n])

    token_base = TOK * (seq - 1)
    own_ids = ids_ref[...] - token_base
    own_id_cols = flip(jnp.broadcast_to(own_ids.astype(F32), (CA, ATOMS))).astype(jnp.int32)
    atom_t = flip(atom_ref[...].astype(F32))
    low = iota((1, ATOMS), 1) < HALF

    for copy in id_copies + halo_copies + cond_copies:
        copy.wait_recv()
    halo_ids = jnp.where(low, id_buf[2], id_buf[0]) - token_base
    halo_id_cols = flip(jnp.broadcast_to(halo_ids.astype(F32), (CA, ATOMS))).astype(jnp.int32)
    id_rows = jnp.concatenate([own_ids, halo_ids], axis=1)
    id_cols = jnp.concatenate([own_id_cols, halo_id_cols], axis=0)
    pick_ext = (iota((SPAN, EXT), 0) == id_rows).astype(F32).astype(BF16)
    pick = pick_ext[:, :ATOMS]
    at_token = id_cols == iota((EXT, CA), 1)
    pick_t = at_token[:ATOMS].astype(F32).astype(BF16)[:, :SPAN]
    token_atoms = jnp.sum(at_token.astype(F32), axis=0, keepdims=True)
    atom_counts = jnp.sum(
        jnp.where(at_token[:ATOMS], token_atoms, 0.0), axis=1, keepdims=True
    )
    inverse = 1.0 / jnp.maximum(atom_counts, 1.0)
    cond = (cond_buf[:, 0] + cond_buf[:, 1]).astype(BF16).reshape(SPAN, CA)
    cond_t = flip(cond.astype(F32)).astype(BF16)
    stream_ext = jnp.concatenate([atom_t, flip(halo_buf[...].astype(F32))], axis=1) + nn(
        cond_t, pick_ext
    )

    position = iota((EXT, ATOMS), 0)
    position = jnp.where(position < ATOMS + HALF, position, position - EXT)
    lane = iota((1, ATOMS), 1)
    first = jnp.zeros((1, ATOMS), jnp.int32)
    for b in range(ATOMS // QB):
        first = jnp.where(lane // QB == b, starts_ref[b] - seq * ATOMS, first)
    inside = (position >= first) & (position < first + KW)
    outside = jnp.where(inside, 0.0, -1e30)
    outside = jnp.concatenate([outside] * HEADS, axis=1)

    def bias_mixed():
        lanes = iota((EXT, 2 * PAIR_PAD), 1)
        column = jnp.where(
            lanes < PAIR_PAD,
            jnp.where(lanes < PAIR_COLS, lanes, -4096),
            jnp.where(lanes < PAIR_PAD + PAIR_COLS, lanes - (PAIR_PAD - PAIR_COLS), -4096),
        )
        for s in range(3):
            take = (id_cols[:, : 2 * PAIR_PAD] + (2 - s) * TOK == column).astype(F32).astype(BF16)
            mixed[:, 2 * CA * s : 2 * CA * (s + 1)] = nn(take, pair_buf[s]).astype(BF16)

    wide = 3 * 2 * CA
    place = iota((wide, ATOMS), 0)
    head_of = (place // PAIR_ROWS) % (CA // PAIR_ROWS)
    token_of = TOK * (place // (2 * CA)) + PAIR_ROWS * ((place // CA) % 2) + place % PAIR_ROWS
    token_hit = token_of == own_ids

    def bias_layer(n):
        picks = jnp.concatenate(
            [
                (token_hit & (head_of == HEADS * n + h)).astype(F32).astype(BF16)
                for h in range(HEADS)
            ],
            axis=1,
        )
        bias[n] = nn(mixed[...], picks) + outside

    stream = stream_ext[:, :ATOMS]
    for n in range(LAYERS):
        wait_for = []
        if n == 0:
            normal_ext, scale_ext = norm_rows(stream_ext)
            normal_x[n] = normal_ext[:, :ATOMS]
            scale_x[n] = scale_ext[:, :ATOMS]
            normed = normal_ext[:, :ATOMS].astype(BF16)
            rows_ext = flip(normal_ext).astype(BF16)
            rows = rows_ext[:ATOMS]
            kv[n] = nn(rows_ext, attn_in_ref[n, :, CA : 3 * CA]).astype(BF16)
        else:
            normal, scaling = norm_rows(stream)
            normal_x[n] = normal
            scale_x[n] = scaling
            normed = normal.astype(BF16)
            rows = flip(normal).astype(BF16)
            kv[n, :ATOMS] = nn(rows, attn_in_ref[n, :, CA : 3 * CA]).astype(BF16)
            wait_for = [
                send(kv.at[n, pl.ds(0, HALF)], kv.at[n, pl.ds(ATOMS, HALF)], -1),
                send(kv.at[n, pl.ds(HALF, HALF)], kv.at[n, pl.ds(ATOMS + HALF, HALF)], 1),
            ]
        queries = nn(rows, attn_in_ref[n, :, :CA]).astype(BF16).astype(F32)
        q_heads[n] = by_head(queries)
        gates = jax.nn.sigmoid(nn(gate_t[n], normed))
        if n == 0:
            for copy in pair_copies:
                copy.wait_recv()
            bias_mixed()
        bias_layer(n)
        own_scores = nt(kv[n, :ATOMS, :CA], q_heads[n]) * SCALE + bias[n, :ATOMS]
        own_values = flip(kv[n, :ATOMS, CA:])
        for copy in wait_for:
            copy.wait_recv()
        halo_scores = nt(kv[n, ATOMS:, :CA], q_heads[n]) * SCALE + bias[n, ATOMS:]
        halo_values = flip(kv[n, ATOMS:, CA:])
        most = jnp.maximum(
            jnp.max(own_scores, axis=0, keepdims=True), jnp.max(halo_scores, axis=0, keepdims=True)
        )
        own_exp = jnp.exp(own_scores - most)
        halo_exp = jnp.exp(halo_scores - most)
        total = jnp.sum(own_exp, axis=0, keepdims=True) + jnp.sum(halo_exp, axis=0, keepdims=True)
        share = 1.0 / total
        own_soft = own_exp * share
        halo_soft = halo_exp * share
        soft[n, :ATOMS] = own_soft
        soft[n, ATOMS:] = halo_soft
        soft_b[n, :ATOMS] = own_soft.astype(BF16)
        soft_b[n, ATOMS:] = halo_soft.astype(BF16)
        values_t = jnp.concatenate([own_values, halo_values], axis=1)
        width = CA // HEADS
        attended = jnp.concatenate(
            [
                nn(
                    values_t[width * h : width * (h + 1)],
                    soft_b[n, :, ATOMS * h : ATOMS * (h + 1)],
                )
                for h in range(HEADS)
            ],
            axis=0,
        )
        gated = gates * attended
        gating[n] = gates
        gate_back[n] = gated * (1.0 - gates)
        x_mid = stream + nn(out_t[n], gated.astype(BF16))
        normal, scaling = norm_rows(x_mid)
        normal_m[n] = normal
        scale_m[n] = scaling
        widened = nn(in_t[n], normal.astype(BF16))
        part_a = widened[:FFA]
        part_b = widened[FFA:]
        sig = jax.nn.sigmoid(part_a)
        act = part_a * sig
        silu_a[n] = act
        back_a[n] = part_b * (sig * (1.0 + part_a * (1.0 - sig)))
        stream = x_mid + nn(down_t[n], (act * part_b).astype(BF16))
        key_t[n, :, :ATOMS] = flip(kv[n, :ATOMS, :CA])
        key_t[n, :, ATOMS:] = flip(kv[n, ATOMS:, :CA])

    final = flip(stream).astype(BF16)
    agg_copy.wait_recv()
    for copy in cot_copies:
        copy.wait_recv()
    gradient = None
    for part in range(2):
        weights = agg_ref[...] if part == 0 else agg_buf[...]
        pre = nn(final, weights)
        sig = jax.nn.sigmoid(pre)
        d_act = nn(pick_t, cot_buf[:, part].reshape(SPAN, ACT)) * inverse
        d_pre = (d_act * (sig * (1.0 + pre * (1.0 - sig)))).astype(BF16)
        term = nt(weights, d_pre)
        gradient = term if part == 0 else gradient + term
        if part == 0:
            high, rest = split(pre * sig)
            sums = nn(pick, high) + nn(pick, rest)
            sums_send[0] = sums[:TOK].astype(BF16)
            sums_send[1] = sums[2 * TOK :].astype(BF16)
            own_sums = sums[TOK : 2 * TOK]
            sums_copies = [
                send(sums_send.at[(ds + 1) // 2], sums_recv.at[(ds + 1) // 2], ds) for ds in SIDES
            ]

    for n in range(LAYERS - 1, -1, -1):
        d_transit = nn(trans_out_ref[n], gradient.astype(BF16))
        d_wide = jnp.concatenate(
            [(d_transit * back_a[n]).astype(BF16), (d_transit * silu_a[n]).astype(BF16)], axis=0
        )
        d_mid = gradient + norm_back(normal_m[n], scale_m[n], nn(trans_in_ref[n], d_wide))
        d_gated = nn(attn_out_ref[n], d_mid.astype(BF16))
        d_att = by_head(flip(d_gated * gating[n]))
        d_gate = (d_gated * gate_back[n]).astype(BF16)
        dkv_send[n, 1] = nn(soft_b[n, ATOMS:], d_att).astype(BF16)
        wait_for = [
            send(dkv_send.at[n, 1, pl.ds(0, HALF)], dkv_recv.at[n, 1, pl.ds(0, HALF)], 1),
            send(dkv_send.at[n, 1, pl.ds(HALF, HALF)], dkv_recv.at[n, 1, pl.ds(HALF, HALF)], -1),
        ]
        own_d = nt(kv[n, :ATOMS, CA:], d_att)
        halo_d = nt(kv[n, ATOMS:, CA:], d_att)
        own_prod = soft[n, :ATOMS] * own_d
        halo_prod = soft[n, ATOMS:] * halo_d
        inner = jnp.sum(own_prod, axis=0, keepdims=True) + jnp.sum(
            halo_prod, axis=0, keepdims=True
        )
        halo_ds = ((halo_prod - soft[n, ATOMS:] * inner) * SCALE).astype(BF16)
        own_ds = ((own_prod - soft[n, :ATOMS] * inner) * SCALE).astype(BF16)
        dkv_send[n, 0] = nn(halo_ds, q_heads[n]).astype(BF16)
        wait_for += [
            send(dkv_send.at[n, 0, pl.ds(0, HALF)], dkv_recv.at[n, 0, pl.ds(0, HALF)], 1),
            send(dkv_send.at[n, 0, pl.ds(HALF, HALF)], dkv_recv.at[n, 0, pl.ds(HALF, HALF)], -1),
        ]
        d_queries = jnp.concatenate(
            [
                nn(
                    key_t[n, width * h : width * (h + 1), :ATOMS],
                    own_ds[:, ATOMS * h : ATOMS * (h + 1)],
                )
                + nn(
                    key_t[n, width * h : width * (h + 1), ATOMS:],
                    halo_ds[:, ATOMS * h : ATOMS * (h + 1)],
                )
                for h in range(HEADS)
            ],
            axis=0,
        ).astype(BF16)
        own_keys = nn(own_ds, q_heads[n])
        own_vals = nn(soft_b[n, :ATOMS], d_att)
        d_normed = nn(attn_in_ref[n, :, :CA], d_queries) + nn(attn_in_ref[n, :, 3 * CA :], d_gate)
        for copy in wait_for:
            copy.wait_recv()
        d_keys = (own_keys + dkv_recv[n, 0].astype(F32)).astype(BF16)
        d_vals = (own_vals + dkv_recv[n, 1].astype(F32)).astype(BF16)
        d_normed = (
            d_normed
            + nt(attn_in_ref[n, :, CA : 2 * CA], d_keys)
            + nt(attn_in_ref[n, :, 2 * CA : 3 * CA], d_vals)
        )
        gradient = d_mid + norm_back(normal_x[n], scale_x[n], d_normed)

    grad_rows = flip(gradient)
    high, rest = split(grad_rows)
    grad_out[...] = high
    d_cond = nn(pick, high) + nn(pick, rest)
    cond_send[0] = d_cond[:TOK].astype(BF16)
    cond_send[1] = d_cond[2 * TOK :].astype(BF16)
    cond_copies = [send(cond_send.at[(ds + 1) // 2], cond_recv.at[(ds + 1) // 2], ds) for ds in SIDES]
    for copy in sums_copies:
        copy.wait_recv()
    token_sums = own_sums + (sums_recv[0].astype(F32) + sums_recv[1].astype(F32))
    diagonal = iota((TOK, TOK), 0) == iota((TOK, TOK), 1)
    counts = jnp.sum(
        jnp.where(diagonal, counts_ref[...].astype(F32), 0.0), axis=1, keepdims=True
    )
    act_out[...] = (token_sums / counts).astype(BF16)
    for copy in cond_copies:
        copy.wait_recv()
    d_cond = d_cond[TOK : 2 * TOK] + (cond_recv[0].astype(F32) + cond_recv[1].astype(F32))
    high, rest = split(d_cond)
    single_out[...] = (nt(high, proj_ref[...]) + nt(rest, proj_ref[...])).astype(BF16)
    for copy in copies:
        copy.wait_send()


N_COPIES = 5 + 2 + 2 + 11 + 5 + 1 + 2 * (LAYERS - 1) + 2 + 4 * LAYERS + 2


def local(
    atom_single,
    token_single,
    pair_band,
    token_counts,
    atom_token,
    window_starts,
    single_proj,
    pair_proj,
    attn_in,
    attn_out,
    trans_in,
    trans_out,
    agg_proj,
    token_cot,
):
    vmem = pl.BlockSpec(memory_space=pltpu.VMEM)
    smem = pl.BlockSpec(memory_space=pltpu.SMEM)

    def scratch(dtype, *shape):
        return pltpu.VMEM(shape, dtype)

    return pl.pallas_call(
        kernel,
        out_shape=(
            jax.ShapeDtypeStruct((TOK, ACT), BF16),
            jax.ShapeDtypeStruct((ATOMS, CA), BF16),
            jax.ShapeDtypeStruct((TOK, COND), BF16),
        ),
        in_specs=[vmem] * 5 + [smem] + [vmem] * 8,
        out_specs=(vmem, vmem, vmem),
        scratch_shapes=[
            scratch(jnp.int32, 3, 1, ATOMS),
            scratch(BF16, ATOMS, CA),
            scratch(F32, 3, 2, TOK, CA),
            scratch(BF16, 3, 2 * PAIR_PAD, 2 * CA),
            scratch(BF16, 3, 2, TOK, ACT),
            scratch(BF16, CA, ACT),
            scratch(BF16, LAYERS, EXT, 2 * CA),
            scratch(F32, LAYERS, EXT, ALL),
            scratch(BF16, EXT, 6 * CA),
            scratch(BF16, LAYERS, CA, CA),
            scratch(BF16, LAYERS, CA, CA),
            scratch(BF16, LAYERS, 2 * FFA, CA),
            scratch(BF16, LAYERS, CA, FFA),
            scratch(F32, LAYERS, EXT, ALL),
            scratch(BF16, LAYERS, EXT, ALL),
            scratch(BF16, LAYERS, ALL, CA),
            scratch(BF16, LAYERS, CA, EXT),
            scratch(F32, LAYERS, CA, ATOMS),
            scratch(F32, LAYERS, 1, ATOMS),
            scratch(F32, LAYERS, CA, ATOMS),
            scratch(F32, LAYERS, 1, ATOMS),
            scratch(F32, LAYERS, CA, ATOMS),
            scratch(F32, LAYERS, CA, ATOMS),
            scratch(F32, LAYERS, FFA, ATOMS),
            scratch(F32, LAYERS, FFA, ATOMS),
            scratch(BF16, LAYERS, 2, ATOMS, CA),
            scratch(BF16, LAYERS, 2, ATOMS, CA),
            scratch(BF16, 2, TOK, ACT),
            scratch(BF16, 2, TOK, ACT),
            scratch(BF16, 2, TOK, CA),
            scratch(BF16, 2, TOK, CA),
            pltpu.SemaphoreType.DMA((N_COPIES,)),
            pltpu.SemaphoreType.DMA((N_COPIES,)),
        ],
        compiler_params=pltpu.CompilerParams(
            collective_id=0, has_side_effects=True, vmem_limit_bytes=48 * 1024 * 1024
        ),
        cost_estimate=pl.CostEstimate(
            flops=2_000_000_000, bytes_accessed=2_000_000, transcendentals=1_000_000
        ),
        name="atoms",
    )(
        atom_single,
        token_single,
        pair_band,
        token_counts.reshape(1, TOK),
        atom_token.reshape(1, ATOMS),
        window_starts,
        single_proj,
        pair_proj,
        attn_in,
        attn_out,
        trans_in,
        trans_out,
        agg_proj,
        token_cot,
    )


def solution(mesh):
    return jax.shard_map(
        local,
        mesh=mesh,
        in_specs=(
            P("seq", None),
            P("seq", "row"),
            P(("seq", "row"), "col", None),
            P("seq"),
            P("seq"),
            P("seq"),
            P("row", None),
            P(),
            P(),
            P(),
            P(),
            P(),
            P(None, "row"),
            P("seq", "row"),
        ),
        out_specs=(P("seq", "row"), P("seq", None), P("seq", "row")),
        check_vma=False,
    )
```

```python
import functools

import jax
import jax.numpy as jnp
from jax import lax
from jax.experimental import pallas as pl
from jax.experimental.pallas import tpu as pltpu
from jax.sharding import PartitionSpec as P

HEADS = 4
QB = 32
KW = 128
LAYERS = 3
ATOMS = 128
CA = 128
TOK = 16
COND = 192
ACT = 384
FFA = 256
PAIR_ROWS = 8
PAIR_COLS = 40
PAIR_PAD = 48
SPAN = 3 * TOK
HALF = 64
EXT = 256
ALL = HEADS * ATOMS
F32 = jnp.float32
BF16 = jnp.bfloat16
EPS = 1e-05
SCALE = (CA // HEADS) ** (-0.5)
MESH = pl.DeviceIdType.MESH

PARTNERS = [
    (ds, dr, dc)
    for ds in (0, -1, 1)
    for dr in (0, 1)
    for dc in (0, 1)
    if (ds, dr, dc) != (0, 0, 0)
]
COND_PARTNERS = [p for p in PARTNERS if p[2] == 0]
SIDES = (-1, 1)


def nn(a, b):
    return lax.dot_general(a, b, (((1,), (0,)), ((), ())), preferred_element_type=F32)


def nt(a, b):
    return lax.dot_general(a, b, (((1,), (1,)), ((), ())), preferred_element_type=F32)


def tn(a, b):
    return lax.dot_general(a, b, (((0,), (0,)), ((), ())), preferred_element_type=F32)


def flip(values):
    return jnp.transpose(values, (1, 0))


def iota(shape, dim):
    return lax.broadcasted_iota(jnp.int32, shape, dim)


def norm_rows(values):
    centre = values - jnp.mean(values, axis=0, keepdims=True)
    scaling = lax.rsqrt(jnp.mean(centre * centre, axis=0, keepdims=True) + EPS)
    return centre * scaling, scaling


def norm_back(normal, scaling, upstream):
    return scaling * (
        upstream
        - jnp.mean(upstream, axis=0, keepdims=True)
        - normal * jnp.mean(upstream * normal, axis=0, keepdims=True)
    )


def by_head(rows):
    head = iota(rows.shape, 1) // (CA // HEADS)
    return jnp.concatenate(
        [jnp.where(head == h, rows, 0.0).astype(BF16) for h in range(HEADS)], axis=0
    )


def split(values):
    high = values.astype(BF16)
    return high, (values - high.astype(F32)).astype(BF16)


def kernel(
    atom_hbm,
    single_hbm,
    band_hbm,
    counts_hbm,
    ids_hbm,
    starts_hbm,
    proj_hbm,
    pair_proj_hbm,
    attn_in_hbm,
    attn_out_hbm,
    trans_in_hbm,
    trans_out_hbm,
    agg_hbm,
    cot_hbm,
    act_out,
    grad_out,
    single_out,
    atom_ref,
    single_ref,
    band_ref,
    counts_ref,
    ids_ref,
    starts_ref,
    proj_ref,
    pair_proj_ref,
    attn_in_ref,
    attn_out_ref,
    trans_in_ref,
    trans_out_ref,
    agg_ref,
    id_buf,
    halo_buf,
    cond_buf,
    pair_buf,
    cot_buf,
    agg_buf,
    rows_buf,
    stream_buf,
    kv,
    kv_wide,
    bias,
    bias_rim,
    mixed,
    gate_t,
    out_t,
    in_t,
    down_t,
    soft,
    soft_b,
    soft_rim,
    soft_rim_own,
    q_heads,
    q_rim,
    key_t,
    normal_x,
    scale_x,
    normal_m,
    scale_m,
    gating,
    gate_back,
    silu_a,
    back_a,
    dkv_send,
    dkv_recv,
    part_send,
    part_recv,
    sums_send,
    sums_recv,
    cond_send,
    cond_recv,
    local_sem,
    send_sem,
    recv_sem,
):
    seq = lax.axis_index("seq")
    row = lax.axis_index("row")
    col = lax.axis_index("col")
    seqs = lax.axis_size("seq")
    width = CA // HEADS

    def partner(ds, dr, dc):
        return (
            lax.rem(seq + ds + seqs, seqs),
            lax.rem(row + dr, 2),
            lax.rem(col + dc, 2),
        )

    copies = []

    def send(src, dst, ds, dr=0, dc=0):
        place = len(copies)
        copy = pltpu.make_async_remote_copy(
            src_ref=src,
            dst_ref=dst,
            send_sem=send_sem.at[place],
            recv_sem=recv_sem.at[place],
            device_id=partner(ds, dr, dc),
            device_id_type=MESH,
        )
        copy.start()
        copies.append(copy)
        return copy

    def arrive(group):
        for copy in group:
            copy.wait_recv()

    barrier = pltpu.get_barrier_semaphore()
    for ds, dr, dc in PARTNERS:
        pl.semaphore_signal(barrier, inc=1, device_id=partner(ds, dr, dc), device_id_type=MESH)

    fetches = []

    def fetch(src, dst):
        copy = pltpu.make_async_copy(src, dst, local_sem.at[len(fetches)])
        copy.start()
        fetches.append(copy)
        return copy

    first_fetch = [fetch(single_hbm, single_ref), fetch(proj_hbm, proj_ref)]
    pair_fetch = [fetch(band_hbm, band_ref), fetch(pair_proj_hbm, pair_proj_ref)]
    id_fetch = [fetch(ids_hbm, ids_ref), fetch(starts_hbm, starts_ref)]
    atom_fetch = [fetch(atom_hbm, atom_ref)]
    weight_fetch = [
        fetch(attn_in_hbm, attn_in_ref),
        fetch(attn_out_hbm, attn_out_ref),
        fetch(trans_in_hbm, trans_in_ref),
        fetch(trans_out_hbm, trans_out_ref),
        fetch(agg_hbm, agg_ref),
        fetch(cot_hbm, cot_buf.at[1, 0]),
        fetch(counts_hbm, counts_ref),
    ]

    for copy in first_fetch:
        copy.wait()
    cond_buf[1, 0] = nn(single_ref[...], proj_ref[...])
    for copy in id_fetch:
        copy.wait()
    lane = iota((1, ATOMS), 1)
    own_first = jnp.zeros((1, ATOMS), jnp.int32)
    for b in range(ATOMS // QB):
        own_first = jnp.where(lane // QB == b, starts_ref[b], own_first)
    id_buf[1, 0:1] = ids_ref[...]
    id_buf[1, 1:2] = own_first
    for copy in pair_fetch:
        copy.wait()
    place_h = (iota((LAYERS * HEADS, CA), 1) == 8 * iota((LAYERS * HEADS, CA), 0)).astype(BF16)
    pp_high, pp_rest = split(pair_proj_ref[...])
    spread_high = tn(pp_high, place_h).astype(BF16)
    spread_rest = tn(pp_rest, place_h).astype(BF16)
    band = band_ref[...].astype(F32).reshape(PAIR_ROWS * PAIR_COLS, CA)
    centre = band - jnp.mean(band, axis=1, keepdims=True)
    normal = centre * lax.rsqrt(jnp.mean(centre * centre, axis=1, keepdims=True) + EPS)
    n_high, n_rest = split(normal)
    pairs = nn(n_high, spread_high) + nn(n_high, spread_rest) + nn(n_rest, spread_high)
    tile = pairs[:PAIR_COLS]
    for i in range(1, PAIR_ROWS):
        tile = tile + pltpu.roll(pairs[PAIR_COLS * i : PAIR_COLS * (i + 1)], i, 1)
    tile = jnp.concatenate([tile, jnp.zeros((PAIR_PAD - PAIR_COLS, CA), F32)], axis=0)
    pair_rows = pl.ds(pl.multiple_of(col * PAIR_PAD, 16), PAIR_PAD)
    pair_lanes = pl.ds(pl.multiple_of(row * CA, CA), CA)
    pair_buf[1, pair_rows, pair_lanes] = tile.astype(BF16)

    pl.semaphore_wait(barrier, len(PARTNERS))

    cond_copies = [
        send(cond_buf.at[1, 0], cond_buf.at[1 - ds, dr], ds, dr) for ds, dr, dc in COND_PARTNERS
    ]
    id_copies = [send(id_buf.at[1], id_buf.at[1 - ds], ds) for ds in SIDES]
    halo_copies = [
        send(atom_hbm.at[pl.ds(0, HALF)], halo_buf.at[pl.ds(0, HALF)], -1),
        send(atom_hbm.at[pl.ds(HALF, HALF)], halo_buf.at[pl.ds(HALF, HALF)], 1),
    ]
    pair_copies = [
        send(
            pair_buf.at[1, pair_rows, pair_lanes],
            pair_buf.at[1 - ds, pair_rows, pair_lanes],
            ds,
            dr,
            dc,
        )
        for ds, dr, dc in PARTNERS
    ]
    cot_copies = [
        send(cot_hbm, cot_buf.at[1 - ds, dr], ds, dr) for ds, dr, dc in COND_PARTNERS
    ]
    agg_copy = send(agg_hbm, agg_buf, 0, 1)

    for copy in atom_fetch + weight_fetch:
        copy.wait()
    for n in range(LAYERS):
        gate_t[n] = flip(attn_in_ref[n, :, 3 * CA :])
        out_t[n] = flip(attn_out_ref[n])
        in_t[n] = flip(trans_in_ref[n])
        down_t[n] = flip(trans_out_ref[n])

    token_base = TOK * (seq - 1)
    atom_base = seq * ATOMS
    low = lane < HALF

    def as_cols(ids):
        return flip(jnp.broadcast_to(ids.astype(F32), (CA, ATOMS))).astype(jnp.int32)

    own_ids = ids_ref[...] - token_base
    own_id_cols = as_cols(own_ids)
    atom_t = flip(atom_ref[...].astype(F32))

    arrive(id_copies + halo_copies + cond_copies)
    left_ids = id_buf[0, 0:1] - token_base
    right_ids = id_buf[2, 0:1] - token_base
    halo_ids = jnp.where(low, right_ids, left_ids)
    halo_id_cols = as_cols(halo_ids)
    pick_ext = (iota((SPAN, EXT), 0) == jnp.concatenate([own_ids, halo_ids], axis=1)).astype(
        F32
    ).astype(BF16)
    pick = pick_ext[:, :ATOMS]
    cond = (cond_buf[:, 0] + cond_buf[:, 1]).astype(BF16).reshape(SPAN, CA)
    cond_t = flip(cond.astype(F32)).astype(BF16)
    stream_ext = jnp.concatenate([atom_t, flip(halo_buf[...].astype(F32))], axis=1) + nn(
        cond_t, pick_ext
    )

    position = iota((EXT, ATOMS), 0)
    position = jnp.where(position < ATOMS + HALF, position, position - EXT)
    first = own_first - atom_base
    outside = jnp.where((position >= first) & (position < first + KW), 0.0, -1e30)
    outside = jnp.concatenate([outside] * HEADS, axis=1)

    wide = 3 * 2 * CA
    place = iota((wide, ATOMS), 0)
    head_of = (place // PAIR_ROWS) % (CA // PAIR_ROWS)
    token_of = TOK * (place // (2 * CA)) + PAIR_ROWS * ((place // CA) % 2) + place % PAIR_ROWS

    def mix_bias(at, id_cols):
        rows = id_cols.shape[0]
        lanes = iota((rows, 2 * PAIR_PAD), 1)
        column = jnp.where(
            lanes < PAIR_PAD,
            jnp.where(lanes < PAIR_COLS, lanes, -4096),
            jnp.where(lanes < PAIR_PAD + PAIR_COLS, lanes - (PAIR_PAD - PAIR_COLS), -4096),
        )
        for s in range(3):
            take = (id_cols[:, : 2 * PAIR_PAD] + (2 - s) * TOK == column).astype(F32).astype(BF16)
            mixed[at : at + rows, 2 * CA * s : 2 * CA * (s + 1)] = nn(take, pair_buf[s]).astype(
                BF16
            )

    def bias_picks(n, ids):
        hit = token_of == ids
        return jnp.concatenate(
            [
                (hit & (head_of == HEADS * n + h)).astype(F32).astype(BF16)
                for h in range(HEADS)
            ],
            axis=1,
        )

    def bias_layer(n):
        bias[n] = nn(mixed[:EXT], bias_picks(n, own_ids)) + outside

    def right_rows(values):
        return jnp.concatenate(
            [values[HALF:ATOMS], values[ATOMS : ATOMS + HALF], values[EXT : EXT + HALF]], axis=0
        )

    def left_rows(values):
        return jnp.concatenate(
            [values[:HALF], values[ATOMS + HALF : EXT], values[EXT + HALF :]], axis=0
        )

    low_all = jnp.concatenate([low] * HEADS, axis=1)

    def attend_own(n, kv_n, wait_for):
        own_scores = nt(kv_n[:ATOMS, :CA], q_heads[n]) * SCALE + bias[n, :ATOMS]
        own_values = flip(kv_n[:ATOMS, CA:])
        arrive(wait_for)
        halo_scores = nt(kv_n[ATOMS:EXT, :CA], q_heads[n]) * SCALE + bias[n, ATOMS:]
        halo_values = flip(kv_n[ATOMS:EXT, CA:])
        most = jnp.maximum(
            jnp.max(own_scores, axis=0, keepdims=True), jnp.max(halo_scores, axis=0, keepdims=True)
        )
        own_exp = jnp.exp(own_scores - most)
        halo_exp = jnp.exp(halo_scores - most)
        total = jnp.sum(own_exp, axis=0, keepdims=True) + jnp.sum(halo_exp, axis=0, keepdims=True)
        share = 1.0 / total
        own_soft = own_exp * share
        halo_soft = halo_exp * share
        soft[n, :ATOMS] = own_soft
        soft[n, ATOMS:] = halo_soft
        soft_b[n, :ATOMS] = own_soft.astype(BF16)
        soft_b[n, ATOMS:] = halo_soft.astype(BF16)
        values_t = jnp.concatenate([own_values, halo_values], axis=1)
        key_t[n, :, :ATOMS] = flip(kv_n[:ATOMS, :CA])
        key_t[n, :, ATOMS:] = flip(kv_n[ATOMS:EXT, :CA])
        return jnp.concatenate(
            [
                nn(
                    values_t[width * h : width * (h + 1)],
                    soft_b[n, :, ATOMS * h : ATOMS * (h + 1)],
                )
                for h in range(HEADS)
            ],
            axis=0,
        )

    def attend_rim(n, kv_n):
        right_kv = right_rows(kv_n)
        left_kv = left_rows(kv_n)
        scores = jnp.where(
            low_all, nt(right_kv[:, :CA], q_rim[...]), nt(left_kv[:, :CA], q_rim[...])
        )
        scores = scores * SCALE + bias_rim[...]
        most = jnp.maximum(jnp.max(scores, axis=0, keepdims=True), -1e29)
        exps = jnp.exp(scores - most)
        weights = exps * (1.0 / jnp.maximum(jnp.sum(exps, axis=0, keepdims=True), 1e-30))
        soft_rim[...] = weights
        rounded = weights.astype(BF16)
        near = weights[:HALF]
        soft_rim_own[:HALF] = jnp.where(low_all, 0.0, near).astype(BF16)
        soft_rim_own[HALF:] = jnp.where(low_all, near, 0.0).astype(BF16)
        right_t = flip(right_kv[:, CA:])
        left_t = flip(left_kv[:, CA:])
        parts = []
        for h in range(HEADS):
            here = rounded[:, ATOMS * h : ATOMS * (h + 1)]
            parts.append(
                jnp.where(
                    low,
                    nn(right_t[width * h : width * (h + 1)], here),
                    nn(left_t[width * h : width * (h + 1)], here),
                )
            )
        return jnp.concatenate(parts, axis=0)

    def transition(n, stream, gates, attended, lanes):
        gated = gates * attended
        gating[n, :, :lanes] = gates
        gate_back[n] = gated[:, :ATOMS] * (1.0 - gates[:, :ATOMS])
        x_mid = stream + nn(out_t[n], gated.astype(BF16))
        normal, scaling = norm_rows(x_mid)
        normal_m[n, :, :lanes] = normal
        scale_m[n, :, :lanes] = scaling
        widened = nn(in_t[n], normal.astype(BF16))
        part_a = widened[:FFA]
        part_b = widened[FFA:]
        sig = jax.nn.sigmoid(part_a)
        act = part_a * sig
        silu_a[n, :, :lanes] = act
        back_a[n, :, :lanes] = part_b * (sig * (1.0 + part_a * (1.0 - sig)))
        return x_mid + nn(down_t[n], (act * part_b).astype(BF16))

    def local_layer(n, stream_ext):
        normal_ext, scale_ext = norm_rows(stream_ext)
        normal_x[n] = normal_ext
        scale_x[n] = scale_ext
        rows_ext = flip(normal_ext).astype(BF16)
        kv[n // 2] = nn(rows_ext, attn_in_ref[n, :, CA : 3 * CA]).astype(BF16)
        queries = nn(rows_ext[:ATOMS], attn_in_ref[n, :, :CA]).astype(BF16).astype(F32)
        q_heads[n] = by_head(queries)
        gates = jax.nn.sigmoid(nn(gate_t[n], normal_ext[:, :ATOMS].astype(BF16)))
        if n == 0:
            arrive(pair_copies)
            mix_bias(0, jnp.concatenate([own_id_cols, halo_id_cols], axis=0))
            bias_layer(n)
        attended = attend_own(n, kv[n // 2], [])
        return transition(n, stream_ext[:, :ATOMS], gates, attended, ATOMS)

    stream = local_layer(0, stream_ext)

    normal, scaling = norm_rows(stream)
    normal_x[1, :, :ATOMS] = normal
    scale_x[1, :, :ATOMS] = scaling
    rows_buf[:ATOMS] = flip(normal).astype(BF16)
    lower, upper = pl.ds(0, HALF), pl.ds(HALF, HALF)
    inner_copies = [
        send(rows_buf.at[lower], rows_buf.at[pl.ds(ATOMS, HALF)], -1),
        send(rows_buf.at[upper], rows_buf.at[pl.ds(ATOMS + HALF, HALF)], 1),
    ]
    outer_copies = [
        send(rows_buf.at[upper], rows_buf.at[pl.ds(EXT, HALF)], -1),
        send(rows_buf.at[lower], rows_buf.at[pl.ds(EXT + HALF, HALF)], 1),
    ]
    stream_buf[0] = flip(stream)
    stream_copies = [
        send(stream_buf.at[0, lower], stream_buf.at[1, lower], -1),
        send(stream_buf.at[0, upper], stream_buf.at[1, upper], 1),
    ]
    kv_wide[:ATOMS] = nn(rows_buf[:ATOMS], attn_in_ref[1, :, CA : 3 * CA]).astype(BF16)
    q_heads[1] = by_head(nn(rows_buf[:ATOMS], attn_in_ref[1, :, :CA]).astype(BF16).astype(F32))
    bias_layer(1)
    outer_ids = pltpu.roll(jnp.where(low, left_ids, right_ids), HALF, 1)
    mix_bias(EXT, as_cols(outer_ids))
    rim_full = nn(mixed[...], bias_picks(1, halo_ids))
    rim_rows = iota((3 * HALF, ATOMS), 0)
    left_position = jnp.where(
        rim_rows < HALF,
        rim_rows,
        jnp.where(rim_rows < ATOMS, rim_rows - ATOMS, rim_rows - EXT),
    )
    rim_position = jnp.where(low, HALF + rim_rows, left_position)
    rim_first = jnp.where(low, id_buf[2, 1:2], id_buf[0, 1:2]) - atom_base
    rim_outside = jnp.where(
        (rim_position >= rim_first) & (rim_position < rim_first + KW), 0.0, -1e30
    )
    bias_rim[...] = jnp.where(low_all, right_rows(rim_full), left_rows(rim_full)) + jnp.concatenate(
        [rim_outside] * HEADS, axis=1
    )
    bias_layer(2)
    at_token = jnp.concatenate([own_id_cols, halo_id_cols], axis=0) == iota((EXT, CA), 1)
    pick_t = at_token[:ATOMS].astype(F32).astype(BF16)[:, :SPAN]
    token_atoms = jnp.sum(at_token.astype(F32), axis=0, keepdims=True)
    atom_counts = jnp.sum(jnp.where(at_token[:ATOMS], token_atoms, 0.0), axis=1, keepdims=True)
    inverse = 1.0 / jnp.maximum(atom_counts, 1.0)
    arrive(inner_copies)
    kv_wide[ATOMS:EXT] = nn(rows_buf[ATOMS:EXT], attn_in_ref[1, :, CA : 3 * CA]).astype(BF16)
    attended = attend_own(1, kv_wide, [])
    gates = jax.nn.sigmoid(nt(gate_t[1], rows_buf[:EXT]))
    q_rim[...] = by_head(nn(rows_buf[ATOMS:EXT], attn_in_ref[1, :, :CA]).astype(BF16).astype(F32))
    arrive(outer_copies)
    kv_wide[EXT:] = nn(rows_buf[EXT:], attn_in_ref[1, :, CA : 3 * CA]).astype(BF16)
    attended = jnp.concatenate([attended, attend_rim(1, kv_wide)], axis=1)
    arrive(stream_copies)
    stream_ext = jnp.concatenate([stream, flip(stream_buf[1])], axis=1)
    stream_ext = transition(1, stream_ext, gates, attended, EXT)

    stream = local_layer(2, stream_ext)

    final = flip(stream).astype(BF16)
    arrive([agg_copy] + cot_copies)
    gradient = None
    for part in range(2):
        weights = agg_ref[...] if part == 0 else agg_buf[...]
        pre = nn(final, weights)
        sig = jax.nn.sigmoid(pre)
        d_act = nn(pick_t, cot_buf[:, part].reshape(SPAN, ACT)) * inverse
        d_pre = (d_act * (sig * (1.0 + pre * (1.0 - sig)))).astype(BF16)
        term = nt(weights, d_pre)
        gradient = term if part == 0 else gradient + term
        if part == 0:
            high, rest = split(pre * sig)
            sums = nn(pick, high) + nn(pick, rest)
            sums_send[0] = sums[:TOK].astype(BF16)
            sums_send[1] = sums[2 * TOK :].astype(BF16)
            own_sums = sums[TOK : 2 * TOK]
            sums_copies = [
                send(sums_send.at[(ds + 1) // 2], sums_recv.at[(ds + 1) // 2], ds) for ds in SIDES
            ]

    def d_middle(n, upstream, lanes):
        d_transit = nn(trans_out_ref[n], upstream.astype(BF16))
        d_wide = jnp.concatenate(
            [
                (d_transit * back_a[n, :, :lanes]).astype(BF16),
                (d_transit * silu_a[n, :, :lanes]).astype(BF16),
            ],
            axis=0,
        )
        d_mid = upstream + norm_back(
            normal_m[n, :, :lanes], scale_m[n, :, :lanes], nn(trans_in_ref[n], d_wide)
        )
        return d_mid, nn(attn_out_ref[n], d_mid.astype(BF16))

    def d_own(n, kv_n, d_att, sent):
        own_d = nt(kv_n[:ATOMS, CA:], d_att)
        halo_d = nt(kv_n[ATOMS:EXT, CA:], d_att)
        own_prod = soft[n, :ATOMS] * own_d
        halo_prod = soft[n, ATOMS:] * halo_d
        inner = jnp.sum(own_prod, axis=0, keepdims=True) + jnp.sum(
            halo_prod, axis=0, keepdims=True
        )
        halo_ds = ((halo_prod - soft[n, ATOMS:] * inner) * SCALE).astype(BF16)
        own_ds = ((own_prod - soft[n, :ATOMS] * inner) * SCALE).astype(BF16)
        if sent is not None:
            sent(halo_ds)
        d_queries = jnp.concatenate(
            [
                nn(
                    key_t[n, width * h : width * (h + 1), :ATOMS],
                    own_ds[:, ATOMS * h : ATOMS * (h + 1)],
                )
                + nn(
                    key_t[n, width * h : width * (h + 1), ATOMS:],
                    halo_ds[:, ATOMS * h : ATOMS * (h + 1)],
                )
                for h in range(HEADS)
            ],
            axis=0,
        ).astype(BF16)
        return d_queries, nn(own_ds, q_heads[n]), nn(soft_b[n, :ATOMS], d_att)

    def weigh_kv(n, d_keys, d_vals):
        return nt(attn_in_ref[n, :, CA : 2 * CA], d_keys) + nt(
            attn_in_ref[n, :, 2 * CA : 3 * CA], d_vals
        )

    def local_back(n, upstream):
        slot = n // 2
        d_mid, d_gated = d_middle(n, upstream, ATOMS)
        d_att = by_head(flip(d_gated * gating[n, :, :ATOMS]))
        d_gate = (d_gated * gate_back[n]).astype(BF16)
        group = []

        def give(kind, values):
            dkv_send[slot, kind] = values.astype(BF16)
            group.append(
                send(dkv_send.at[slot, kind, lower], dkv_recv.at[slot, kind, lower], 1)
            )
            group.append(
                send(dkv_send.at[slot, kind, upper], dkv_recv.at[slot, kind, upper], -1)
            )

        give(1, nn(soft_b[n, ATOMS:], d_att))
        d_queries, d_keys, d_vals = d_own(
            n, kv[slot], d_att, lambda halo_ds: give(0, nn(halo_ds, q_heads[n]))
        )
        d_normed = (
            nn(attn_in_ref[n, :, :CA], d_queries)
            + nn(attn_in_ref[n, :, 3 * CA :], d_gate)
            + weigh_kv(n, d_keys.astype(BF16), d_vals.astype(BF16))
        )
        part = d_mid + norm_back(normal_x[n, :, :ATOMS], scale_x[n, :, :ATOMS], d_normed)
        return part, group

    def beside(n):
        slot = n // 2
        return norm_back(
            normal_x[n, :, ATOMS:],
            scale_x[n, :, ATOMS:],
            weigh_kv(n, dkv_send[slot, 0], dkv_send[slot, 1]),
        )

    def from_beside(n):
        slot = n // 2
        return norm_back(
            normal_x[n, :, :ATOMS],
            scale_x[n, :, :ATOMS],
            weigh_kv(n, dkv_recv[slot, 0], dkv_recv[slot, 1]),
        )

    part, group = local_back(2, gradient)
    part_send[...] = part.astype(BF16)
    part_copies = [send(part_send, part_recv.at[(ds + 1) // 2], ds) for ds in SIDES]
    halo_gradient = beside(2)
    arrive(group)
    gradient = part + from_beside(2)
    arrive(part_copies)
    halo_gradient = halo_gradient + jnp.where(low, part_recv[0], part_recv[1]).astype(F32)
    gradient = jnp.concatenate([gradient, halo_gradient], axis=1)

    d_mid, d_gated = d_middle(1, gradient, EXT)
    d_att_t = d_gated * gating[1]
    d_att = by_head(flip(d_att_t[:, :ATOMS]))
    d_att_rim = by_head(flip(d_att_t[:, ATOMS:]))
    d_gate = (d_gated[:, :ATOMS] * gate_back[1]).astype(BF16)
    d_queries, d_keys, d_vals = d_own(1, kv_wide, d_att, None)
    rim_d = jnp.where(
        low_all,
        nt(right_rows(kv_wide[:, CA:]), d_att_rim),
        nt(left_rows(kv_wide[:, CA:]), d_att_rim),
    )
    rim_prod = soft_rim[...] * rim_d
    rim_inner = jnp.sum(rim_prod, axis=0, keepdims=True)
    rim_ds = (rim_prod[:HALF] - soft_rim[:HALF] * rim_inner) * SCALE
    rim_ds = jnp.concatenate(
        [jnp.where(low_all, 0.0, rim_ds), jnp.where(low_all, rim_ds, 0.0)], axis=0
    ).astype(BF16)
    d_keys = d_keys + nn(rim_ds, q_rim[...])
    d_vals = d_vals + nn(soft_rim_own[...], d_att_rim)
    d_normed = (
        nn(attn_in_ref[1, :, :CA], d_queries)
        + nn(attn_in_ref[1, :, 3 * CA :], d_gate)
        + weigh_kv(1, d_keys.astype(BF16), d_vals.astype(BF16))
    )
    gradient = d_mid[:, :ATOMS] + norm_back(
        normal_x[1, :, :ATOMS], scale_x[1, :, :ATOMS], d_normed
    )

    def per_token(picks, values):
        high, rest = split(values)
        return nt(picks, high) + nt(picks, rest)

    part, group = local_back(0, gradient)
    d_cond = per_token(pick, part)
    cond_send[0] = d_cond[:TOK].astype(BF16)
    cond_send[1] = d_cond[2 * TOK :].astype(BF16)
    last_copies = [send(cond_send.at[(ds + 1) // 2], cond_recv.at[(ds + 1) // 2], ds) for ds in SIDES]
    d_cond = d_cond[TOK : 2 * TOK] + per_token(pick_ext[TOK : 2 * TOK, ATOMS:], beside(0))
    arrive(sums_copies)
    token_sums = own_sums + (sums_recv[0].astype(F32) + sums_recv[1].astype(F32))
    diagonal = iota((TOK, TOK), 0) == iota((TOK, TOK), 1)
    counts = jnp.sum(
        jnp.where(diagonal, counts_ref[...].astype(F32), 0.0), axis=1, keepdims=True
    )
    act_out[...] = (token_sums / counts).astype(BF16)
    arrive(group)
    rest_gradient = from_beside(0)
    grad_out[...] = flip(part + rest_gradient).astype(BF16)
    d_cond = d_cond + per_token(pick[TOK : 2 * TOK], rest_gradient)
    arrive(last_copies)
    d_cond = d_cond + (cond_recv[0].astype(F32) + cond_recv[1].astype(F32))
    high, rest = split(d_cond)
    single_out[...] = (nt(high, proj_ref[...]) + nt(rest, proj_ref[...])).astype(BF16)
    for copy in copies:
        copy.wait_send()


N_COPIES = 5 + 2 + 2 + 11 + 5 + 1 + 6 + 2 + 4 + 2 + 4 + 2


def hand_on(act, grad, single, act_out, grad_out, single_out):
    act_out[...] = act[...]
    grad_out[...] = grad[...]
    single_out[...] = single[...]


def local(
    atom_single,
    token_single,
    pair_band,
    token_counts,
    atom_token,
    window_starts,
    single_proj,
    pair_proj,
    attn_in,
    attn_out,
    trans_in,
    trans_out,
    agg_proj,
    token_cot,
):
    vmem = pl.BlockSpec(memory_space=pltpu.VMEM)
    hbm = pl.BlockSpec(memory_space=pltpu.HBM)

    def scratch(dtype, *shape):
        return pltpu.VMEM(shape, dtype)

    results = (
        jax.ShapeDtypeStruct((TOK, ACT), BF16),
        jax.ShapeDtypeStruct((ATOMS, CA), BF16),
        jax.ShapeDtypeStruct((TOK, COND), BF16),
    )
    results_here = pl.pallas_call(
        kernel,
        out_shape=results,
        in_specs=[hbm] * 14,
        out_specs=(vmem, vmem, vmem),
        scratch_shapes=[
            scratch(BF16, ATOMS, CA),
            scratch(BF16, TOK, COND),
            scratch(BF16, PAIR_ROWS, PAIR_COLS, CA),
            scratch(jnp.int32, 1, TOK),
            scratch(jnp.int32, 1, ATOMS),
            pltpu.SMEM((ATOMS // QB,), jnp.int32),
            scratch(BF16, COND, CA),
            scratch(F32, LAYERS * HEADS, CA),
            scratch(BF16, LAYERS, CA, 4 * CA),
            scratch(BF16, LAYERS, CA, CA),
            scratch(BF16, LAYERS, CA, 2 * FFA),
            scratch(BF16, LAYERS, FFA, CA),
            scratch(BF16, CA, ACT),
            scratch(jnp.int32, 3, 2, ATOMS),
            scratch(BF16, ATOMS, CA),
            scratch(F32, 3, 2, TOK, CA),
            scratch(BF16, 3, 2 * PAIR_PAD, 2 * CA),
            scratch(BF16, 3, 2, TOK, ACT),
            scratch(BF16, CA, ACT),
            scratch(BF16, 3 * ATOMS, CA),
            scratch(F32, 2, ATOMS, CA),
            scratch(BF16, 2, EXT, 2 * CA),
            scratch(BF16, 3 * ATOMS, 2 * CA),
            scratch(F32, LAYERS, EXT, ALL),
            scratch(F32, 3 * HALF, ALL),
            scratch(BF16, 3 * ATOMS, 6 * CA),
            scratch(BF16, LAYERS, CA, CA),
            scratch(BF16, LAYERS, CA, CA),
            scratch(BF16, LAYERS, 2 * FFA, CA),
            scratch(BF16, LAYERS, CA, FFA),
            scratch(F32, LAYERS, EXT, ALL),
            scratch(BF16, LAYERS, EXT, ALL),
            scratch(F32, 3 * HALF, ALL),
            scratch(BF16, ATOMS, ALL),
            scratch(BF16, LAYERS, ALL, CA),
            scratch(BF16, ALL, CA),
            scratch(BF16, LAYERS, CA, EXT),
            scratch(F32, LAYERS, CA, EXT),
            scratch(F32, LAYERS, 1, EXT),
            scratch(F32, LAYERS, CA, EXT),
            scratch(F32, LAYERS, 1, EXT),
            scratch(F32, LAYERS, CA, EXT),
            scratch(F32, LAYERS, CA, ATOMS),
            scratch(F32, LAYERS, FFA, EXT),
            scratch(F32, LAYERS, FFA, EXT),
            scratch(BF16, 2, 2, ATOMS, CA),
            scratch(BF16, 2, 2, ATOMS, CA),
            scratch(BF16, CA, ATOMS),
            scratch(BF16, 2, CA, ATOMS),
            scratch(BF16, 2, TOK, ACT),
            scratch(BF16, 2, TOK, ACT),
            scratch(BF16, 2, TOK, CA),
            scratch(BF16, 2, TOK, CA),
            pltpu.SemaphoreType.DMA((14,)),
            pltpu.SemaphoreType.DMA((N_COPIES,)),
            pltpu.SemaphoreType.DMA((N_COPIES,)),
        ],
        compiler_params=pltpu.CompilerParams(
            collective_id=0, has_side_effects=True, vmem_limit_bytes=64 * 1024 * 1024
        ),
        cost_estimate=pl.CostEstimate(
            flops=2_000_000_000, bytes_accessed=2_000_000, transcendentals=1_000_000
        ),
        name="atoms",
    )(
        atom_single,
        token_single,
        pair_band,
        token_counts.reshape(1, TOK),
        atom_token.reshape(1, ATOMS),
        window_starts,
        single_proj,
        pair_proj.T,
        attn_in,
        attn_out,
        trans_in,
        trans_out,
        agg_proj,
        token_cot,
    )
    return pl.pallas_call(
        hand_on,
        out_shape=results,
        in_specs=[vmem] * 3,
        out_specs=(vmem,) * 3,
        name="results",
    )(*results_here)


def solution(mesh):
    return jax.shard_map(
        local,
        mesh=mesh,
        in_specs=(
            P("seq", None),
            P("seq", "row"),
            P(("seq", "row"), "col", None),
            P("seq"),
            P("seq"),
            P("seq"),
            P("row", None),
            P(),
            P(),
            P(),
            P(),
            P(),
            P(None, "row"),
            P("seq", "row"),
        ),
        out_specs=(P("seq", "row"), P("seq", None), P("seq", "row")),
        check_vma=False,
    )
```

```python
import functools

import jax
import jax.numpy as jnp
from jax import lax
from jax.experimental import pallas as pl
from jax.experimental.pallas import tpu as pltpu
from jax.sharding import PartitionSpec as P

HEADS = 4
QB = 32
KW = 128
LAYERS = 3
ATOMS = 128
CA = 128
TOK = 16
COND = 192
ACT = 384
FFA = 256
PAIR_ROWS = 8
PAIR_COLS = 40
PAIR_PAD = 48
SPAN = 3 * TOK
HALF = 64
EXT = 256
ALL = HEADS * ATOMS
F32 = jnp.float32
BF16 = jnp.bfloat16
EPS = 1e-05
SCALE = (CA // HEADS) ** (-0.5)
MESH = pl.DeviceIdType.MESH

PARTNERS = [
    (ds, dr, dc)
    for ds in (0, -1, 1)
    for dr in (0, 1)
    for dc in (0, 1)
    if (ds, dr, dc) != (0, 0, 0)
]
COND_PARTNERS = [p for p in PARTNERS if p[2] == 0]
SIDES = (-1, 1)


def nn(a, b):
    return lax.dot_general(a, b, (((1,), (0,)), ((), ())), preferred_element_type=F32)


def nt(a, b):
    return lax.dot_general(a, b, (((1,), (1,)), ((), ())), preferred_element_type=F32)


def tn(a, b):
    return lax.dot_general(a, b, (((0,), (0,)), ((), ())), preferred_element_type=F32)


def flip(values):
    return jnp.transpose(values, (1, 0))


def iota(shape, dim):
    return lax.broadcasted_iota(jnp.int32, shape, dim)


def norm_rows(values):
    centre = values - jnp.mean(values, axis=0, keepdims=True)
    scaling = lax.rsqrt(jnp.mean(centre * centre, axis=0, keepdims=True) + EPS)
    return centre * scaling, scaling


def norm_back(normal, scaling, upstream):
    return scaling * (
        upstream
        - jnp.mean(upstream, axis=0, keepdims=True)
        - normal * jnp.mean(upstream * normal, axis=0, keepdims=True)
    )


def by_head(rows):
    head = iota(rows.shape, 1) // (CA // HEADS)
    return jnp.concatenate(
        [jnp.where(head == h, rows, 0.0).astype(BF16) for h in range(HEADS)], axis=0
    )


def split(values):
    high = values.astype(BF16)
    return high, (values - high.astype(F32)).astype(BF16)


def kernel(
    atom_hbm,
    single_hbm,
    band_hbm,
    counts_hbm,
    ids_hbm,
    starts_hbm,
    proj_hbm,
    pair_proj_hbm,
    attn_in_hbm,
    attn_out_hbm,
    trans_in_hbm,
    trans_out_hbm,
    agg_hbm,
    cot_hbm,
    act_out,
    grad_out,
    single_out,
    atom_ref,
    single_ref,
    band_ref,
    counts_ref,
    ids_ref,
    starts_ref,
    proj_ref,
    pair_proj_ref,
    attn_in_ref,
    attn_out_ref,
    trans_in_ref,
    trans_out_ref,
    agg_ref,
    id_buf,
    halo_buf,
    cond_buf,
    pair_buf,
    cot_buf,
    agg_buf,
    rows_buf,
    stream_buf,
    kv,
    kv_wide,
    bias,
    bias_rim,
    mixed,
    gate_t,
    out_t,
    in_t,
    down_t,
    soft,
    soft_b,
    soft_rim,
    soft_rim_own,
    q_heads,
    q_rim,
    key_t,
    normal_x,
    scale_x,
    normal_m,
    scale_m,
    gating,
    gate_back,
    silu_a,
    back_a,
    dkv_send,
    dkv_recv,
    part_send,
    part_recv,
    sums_send,
    sums_recv,
    cond_send,
    cond_recv,
    local_sem,
    send_sem,
    recv_sem,
):
    seq = lax.axis_index("seq")
    row = lax.axis_index("row")
    col = lax.axis_index("col")
    seqs = lax.axis_size("seq")
    width = CA // HEADS

    def partner(ds, dr, dc):
        return (
            lax.rem(seq + ds + seqs, seqs),
            lax.rem(row + dr, 2),
            lax.rem(col + dc, 2),
        )

    has = {-1: seq > 0, 1: seq < seqs - 1}

    def toward(ds, act):
        if ds == 0:
            act()
        else:
            pl.when(has[ds])(act)

    copies = []

    def send_all(wanted):
        group = []
        for src, dst, ds, dr, dc in wanted:
            place = len(copies)
            copy = pltpu.make_async_remote_copy(
                src_ref=src,
                dst_ref=dst,
                send_sem=send_sem.at[place],
                recv_sem=recv_sem.at[place],
                device_id=partner(ds, dr, dc),
                device_id_type=MESH,
            )
            copies.append((copy, ds))
            group.append((copy, ds))
        for side in (-1, 1, 0):
            mine = [copy for copy, ds in group if ds == side]
            if mine:
                toward(side, lambda mine=mine: [copy.start() for copy in mine] and None)
        return group

    def arrive(group):
        for side in (0, -1, 1):
            mine = [copy for copy, ds in group if ds == side]
            if mine:
                toward(-side, lambda mine=mine: [copy.wait_recv() for copy in mine] and None)

    barrier = pltpu.get_barrier_semaphore()

    def greet(side):
        for ds, dr, dc in PARTNERS:
            if ds == side:
                pl.semaphore_signal(
                    barrier, inc=1, device_id=partner(ds, dr, dc), device_id_type=MESH
                )

    for side in (-1, 1, 0):
        toward(side, functools.partial(greet, side))

    fetches = []

    def fetch(src, dst):
        copy = pltpu.make_async_copy(src, dst, local_sem.at[len(fetches)])
        copy.start()
        fetches.append(copy)
        return copy

    first_fetch = [fetch(single_hbm, single_ref), fetch(proj_hbm, proj_ref)]
    pair_fetch = [fetch(band_hbm, band_ref), fetch(pair_proj_hbm, pair_proj_ref)]
    id_fetch = [fetch(ids_hbm, ids_ref), fetch(starts_hbm, starts_ref)]
    atom_fetch = [fetch(atom_hbm, atom_ref)]
    weight_fetch = [
        fetch(attn_in_hbm, attn_in_ref),
        fetch(attn_out_hbm, attn_out_ref),
        fetch(trans_in_hbm, trans_in_ref),
        fetch(trans_out_hbm, trans_out_ref),
        fetch(agg_hbm, agg_ref),
        fetch(cot_hbm, cot_buf.at[1, 0]),
        fetch(counts_hbm, counts_ref),
    ]

    near, far = pl.ds(0, HALF), pl.ds(HALF, HALF)

    def close(slot, half):
        id_buf[slot, 0:1] = jnp.full((1, ATOMS), -(2**20), jnp.int32)
        id_buf[slot, 1:2] = jnp.full((1, ATOMS), 2**20, jnp.int32)
        cond_buf[slot] = jnp.zeros(cond_buf.shape[1:], F32)
        pair_buf[slot] = jnp.zeros(pair_buf.shape[1:], BF16)
        cot_buf[slot] = jnp.zeros(cot_buf.shape[1:], BF16)
        halo_buf[half] = jnp.zeros((HALF, CA), BF16)
        for at in (ATOMS, EXT):
            other = (half.start + at - ATOMS) % ATOMS
            rows_buf[at + other : at + other + HALF] = jnp.zeros((HALF, CA), BF16)
        stream_buf[1, half] = jnp.zeros((HALF, CA), F32)
        opposite = pl.ds(HALF - half.start, HALF)
        for slot_kv in range(2):
            for kind in range(2):
                dkv_recv[slot_kv, kind, opposite] = jnp.zeros((HALF, CA), BF16)
        side = 1 if slot == 0 else 0
        part_recv[side] = jnp.zeros((CA, ATOMS), BF16)
        sums_recv[side] = jnp.zeros((TOK, ACT), BF16)
        cond_recv[side] = jnp.zeros((TOK, CA), BF16)

    pl.when(seq == 0)(lambda: close(0, far))
    pl.when(seq == seqs - 1)(lambda: close(2, near))

    for copy in first_fetch:
        copy.wait()
    cond_buf[1, 0] = nn(single_ref[...], proj_ref[...])
    for copy in id_fetch:
        copy.wait()
    lane = iota((1, ATOMS), 1)
    own_first = jnp.zeros((1, ATOMS), jnp.int32)
    for b in range(ATOMS // QB):
        own_first = jnp.where(lane // QB == b, starts_ref[b], own_first)
    id_buf[1, 0:1] = ids_ref[...]
    id_buf[1, 1:2] = own_first
    for copy in pair_fetch:
        copy.wait()
    place_h = (iota((LAYERS * HEADS, CA), 1) == 8 * iota((LAYERS * HEADS, CA), 0)).astype(BF16)
    pp_high, pp_rest = split(pair_proj_ref[...])
    spread_high = tn(pp_high, place_h).astype(BF16)
    spread_rest = tn(pp_rest, place_h).astype(BF16)
    band = band_ref[...].astype(F32).reshape(PAIR_ROWS * PAIR_COLS, CA)
    centre = band - jnp.mean(band, axis=1, keepdims=True)
    normal = centre * lax.rsqrt(jnp.mean(centre * centre, axis=1, keepdims=True) + EPS)
    n_high, n_rest = split(normal)
    pairs = nn(n_high, spread_high) + nn(n_high, spread_rest) + nn(n_rest, spread_high)
    tile = pairs[:PAIR_COLS]
    for i in range(1, PAIR_ROWS):
        tile = tile + pltpu.roll(pairs[PAIR_COLS * i : PAIR_COLS * (i + 1)], i, 1)
    tile = jnp.concatenate([tile, jnp.zeros((PAIR_PAD - PAIR_COLS, CA), F32)], axis=0)
    pair_rows = pl.ds(pl.multiple_of(col * PAIR_PAD, 16), PAIR_PAD)
    pair_lanes = pl.ds(pl.multiple_of(row * CA, CA), CA)
    pair_buf[1, pair_rows, pair_lanes] = tile.astype(BF16)

    beyond = len(PARTNERS) // 3 + 1
    pl.semaphore_wait(
        barrier, beyond - 1 + beyond * (has[-1].astype(jnp.int32) + has[1].astype(jnp.int32))
    )

    cond_copies = send_all(
        [
            (cond_buf.at[1, 0], cond_buf.at[1 - ds, dr], ds, dr, dc)
            for ds, dr, dc in COND_PARTNERS
        ]
        + [(id_buf.at[1], id_buf.at[1 - ds], ds, 0, 0) for ds in SIDES]
        + [
            (atom_hbm.at[near], halo_buf.at[near], -1, 0, 0),
            (atom_hbm.at[far], halo_buf.at[far], 1, 0, 0),
        ]
    )
    pair_copies = send_all(
        [
            (
                pair_buf.at[1, pair_rows, pair_lanes],
                pair_buf.at[1 - ds, pair_rows, pair_lanes],
                ds,
                dr,
                dc,
            )
            for ds, dr, dc in PARTNERS
        ]
    )
    late_copies = send_all(
        [(cot_hbm, cot_buf.at[1 - ds, dr], ds, dr, dc) for ds, dr, dc in COND_PARTNERS]
        + [(agg_hbm, agg_buf, 0, 1, 0)]
    )

    for copy in atom_fetch + weight_fetch:
        copy.wait()
    for n in range(LAYERS):
        gate_t[n] = flip(attn_in_ref[n, :, 3 * CA :])
        out_t[n] = flip(attn_out_ref[n])
        in_t[n] = flip(trans_in_ref[n])
        down_t[n] = flip(trans_out_ref[n])

    token_base = TOK * (seq - 1)
    atom_base = seq * ATOMS
    low = lane < HALF

    def as_cols(ids):
        return flip(jnp.broadcast_to(ids.astype(F32), (CA, ATOMS))).astype(jnp.int32)

    own_ids = ids_ref[...] - token_base
    own_id_cols = as_cols(own_ids)
    atom_t = flip(atom_ref[...].astype(F32))

    arrive(cond_copies)
    left_ids = id_buf[0, 0:1] - token_base
    right_ids = id_buf[2, 0:1] - token_base
    halo_ids = jnp.where(low, right_ids, left_ids)
    halo_id_cols = as_cols(halo_ids)
    pick_ext = (iota((SPAN, EXT), 0) == jnp.concatenate([own_ids, halo_ids], axis=1)).astype(
        F32
    ).astype(BF16)
    pick = pick_ext[:, :ATOMS]
    cond = (cond_buf[:, 0] + cond_buf[:, 1]).astype(BF16).reshape(SPAN, CA)
    cond_t = flip(cond.astype(F32)).astype(BF16)
    stream_ext = jnp.concatenate([atom_t, flip(halo_buf[...].astype(F32))], axis=1) + nn(
        cond_t, pick_ext
    )

    position = iota((EXT, ATOMS), 0)
    position = jnp.where(position < ATOMS + HALF, position, position - EXT)
    first = own_first - atom_base
    outside = jnp.where((position >= first) & (position < first + KW), 0.0, -1e30)
    outside = jnp.concatenate([outside] * HEADS, axis=1)

    wide = 3 * 2 * CA
    place = iota((wide, ATOMS), 0)
    head_of = (place // PAIR_ROWS) % (CA // PAIR_ROWS)
    token_of = TOK * (place // (2 * CA)) + PAIR_ROWS * ((place // CA) % 2) + place % PAIR_ROWS

    def mix_bias(at, id_cols):
        rows = id_cols.shape[0]
        lanes = iota((rows, 2 * PAIR_PAD), 1)
        column = jnp.where(
            lanes < PAIR_PAD,
            jnp.where(lanes < PAIR_COLS, lanes, -4096),
            jnp.where(lanes < PAIR_PAD + PAIR_COLS, lanes - (PAIR_PAD - PAIR_COLS), -4096),
        )
        for s in range(3):
            take = (id_cols[:, : 2 * PAIR_PAD] + (2 - s) * TOK == column).astype(F32).astype(BF16)
            mixed[at : at + rows, 2 * CA * s : 2 * CA * (s + 1)] = nn(take, pair_buf[s]).astype(
                BF16
            )

    def bias_picks(n, ids):
        hit = token_of == ids
        return jnp.concatenate(
            [
                (hit & (head_of == HEADS * n + h)).astype(F32).astype(BF16)
                for h in range(HEADS)
            ],
            axis=1,
        )

    def bias_layer(n):
        bias[n] = nn(mixed[:EXT], bias_picks(n, own_ids)) + outside

    def right_rows(values):
        return jnp.concatenate(
            [values[HALF:ATOMS], values[ATOMS : ATOMS + HALF], values[EXT : EXT + HALF]], axis=0
        )

    def left_rows(values):
        return jnp.concatenate(
            [values[:HALF], values[ATOMS + HALF : EXT], values[EXT + HALF :]], axis=0
        )

    low_all = jnp.concatenate([low] * HEADS, axis=1)

    def attend_own(n, kv_n, wait_for):
        own_scores = nt(kv_n[:ATOMS, :CA], q_heads[n]) * SCALE + bias[n, :ATOMS]
        own_values = flip(kv_n[:ATOMS, CA:])
        arrive(wait_for)
        halo_scores = nt(kv_n[ATOMS:EXT, :CA], q_heads[n]) * SCALE + bias[n, ATOMS:]
        halo_values = flip(kv_n[ATOMS:EXT, CA:])
        most = jnp.maximum(
            jnp.max(own_scores, axis=0, keepdims=True), jnp.max(halo_scores, axis=0, keepdims=True)
        )
        own_exp = jnp.exp(own_scores - most)
        halo_exp = jnp.exp(halo_scores - most)
        total = jnp.sum(own_exp, axis=0, keepdims=True) + jnp.sum(halo_exp, axis=0, keepdims=True)
        share = 1.0 / total
        own_soft = own_exp * share
        halo_soft = halo_exp * share
        soft[n, :ATOMS] = own_soft
        soft[n, ATOMS:] = halo_soft
        soft_b[n, :ATOMS] = own_soft.astype(BF16)
        soft_b[n, ATOMS:] = halo_soft.astype(BF16)
        values_t = jnp.concatenate([own_values, halo_values], axis=1)
        key_t[n, :, :ATOMS] = flip(kv_n[:ATOMS, :CA])
        key_t[n, :, ATOMS:] = flip(kv_n[ATOMS:EXT, :CA])
        return jnp.concatenate(
            [
                nn(
                    values_t[width * h : width * (h + 1)],
                    soft_b[n, :, ATOMS * h : ATOMS * (h + 1)],
                )
                for h in range(HEADS)
            ],
            axis=0,
        )

    def attend_rim(n, kv_n):
        right_kv = right_rows(kv_n)
        left_kv = left_rows(kv_n)
        scores = jnp.where(
            low_all, nt(right_kv[:, :CA], q_rim[...]), nt(left_kv[:, :CA], q_rim[...])
        )
        scores = scores * SCALE + bias_rim[...]
        most = jnp.maximum(jnp.max(scores, axis=0, keepdims=True), -1e29)
        exps = jnp.exp(scores - most)
        weights = exps * (1.0 / jnp.maximum(jnp.sum(exps, axis=0, keepdims=True), 1e-30))
        soft_rim[...] = weights
        rounded = weights.astype(BF16)
        near = weights[:HALF]
        soft_rim_own[:HALF] = jnp.where(low_all, 0.0, near).astype(BF16)
        soft_rim_own[HALF:] = jnp.where(low_all, near, 0.0).astype(BF16)
        right_t = flip(right_kv[:, CA:])
        left_t = flip(left_kv[:, CA:])
        parts = []
        for h in range(HEADS):
            here = rounded[:, ATOMS * h : ATOMS * (h + 1)]
            parts.append(
                jnp.where(
                    low,
                    nn(right_t[width * h : width * (h + 1)], here),
                    nn(left_t[width * h : width * (h + 1)], here),
                )
            )
        return jnp.concatenate(parts, axis=0)

    def transition(n, stream, gates, attended, lanes):
        gated = gates * attended
        gating[n, :, :lanes] = gates
        gate_back[n] = gated[:, :ATOMS] * (1.0 - gates[:, :ATOMS])
        x_mid = stream + nn(out_t[n], gated.astype(BF16))
        normal, scaling = norm_rows(x_mid)
        normal_m[n, :, :lanes] = normal
        scale_m[n, :, :lanes] = scaling
        widened = nn(in_t[n], normal.astype(BF16))
        part_a = widened[:FFA]
        part_b = widened[FFA:]
        sig = jax.nn.sigmoid(part_a)
        act = part_a * sig
        silu_a[n, :, :lanes] = act
        back_a[n, :, :lanes] = part_b * (sig * (1.0 + part_a * (1.0 - sig)))
        return x_mid + nn(down_t[n], (act * part_b).astype(BF16))

    def local_layer(n, stream_ext):
        normal_ext, scale_ext = norm_rows(stream_ext)
        normal_x[n] = normal_ext
        scale_x[n] = scale_ext
        rows_ext = flip(normal_ext).astype(BF16)
        kv[n // 2] = nn(rows_ext, attn_in_ref[n, :, CA : 3 * CA]).astype(BF16)
        queries = nn(rows_ext[:ATOMS], attn_in_ref[n, :, :CA]).astype(BF16).astype(F32)
        q_heads[n] = by_head(queries)
        gates = jax.nn.sigmoid(nn(gate_t[n], normal_ext[:, :ATOMS].astype(BF16)))
        if n == 0:
            arrive(pair_copies)
            mix_bias(0, jnp.concatenate([own_id_cols, halo_id_cols], axis=0))
            bias_layer(n)
        attended = attend_own(n, kv[n // 2], [])
        return transition(n, stream_ext[:, :ATOMS], gates, attended, ATOMS)

    stream = local_layer(0, stream_ext)

    normal, scaling = norm_rows(stream)
    normal_x[1, :, :ATOMS] = normal
    scale_x[1, :, :ATOMS] = scaling
    rows_buf[:ATOMS] = flip(normal).astype(BF16)
    lower, upper = near, far
    inner_copies = send_all(
        [
            (rows_buf.at[lower], rows_buf.at[pl.ds(ATOMS, HALF)], -1, 0, 0),
            (rows_buf.at[upper], rows_buf.at[pl.ds(ATOMS + HALF, HALF)], 1, 0, 0),
        ]
    )
    outer_copies = send_all(
        [
            (rows_buf.at[upper], rows_buf.at[pl.ds(EXT, HALF)], -1, 0, 0),
            (rows_buf.at[lower], rows_buf.at[pl.ds(EXT + HALF, HALF)], 1, 0, 0),
        ]
    )
    stream_buf[0] = flip(stream)
    stream_copies = send_all(
        [
            (stream_buf.at[0, lower], stream_buf.at[1, lower], -1, 0, 0),
            (stream_buf.at[0, upper], stream_buf.at[1, upper], 1, 0, 0),
        ]
    )
    kv_wide[:ATOMS] = nn(rows_buf[:ATOMS], attn_in_ref[1, :, CA : 3 * CA]).astype(BF16)
    q_heads[1] = by_head(nn(rows_buf[:ATOMS], attn_in_ref[1, :, :CA]).astype(BF16).astype(F32))
    bias_layer(1)
    outer_ids = pltpu.roll(jnp.where(low, left_ids, right_ids), HALF, 1)
    mix_bias(EXT, as_cols(outer_ids))
    rim_full = nn(mixed[...], bias_picks(1, halo_ids))
    rim_rows = iota((3 * HALF, ATOMS), 0)
    left_position = jnp.where(
        rim_rows < HALF,
        rim_rows,
        jnp.where(rim_rows < ATOMS, rim_rows - ATOMS, rim_rows - EXT),
    )
    rim_position = jnp.where(low, HALF + rim_rows, left_position)
    rim_first = jnp.where(low, id_buf[2, 1:2], id_buf[0, 1:2]) - atom_base
    rim_outside = jnp.where(
        (rim_position >= rim_first) & (rim_position < rim_first + KW), 0.0, -1e30
    )
    bias_rim[...] = jnp.where(low_all, right_rows(rim_full), left_rows(rim_full)) + jnp.concatenate(
        [rim_outside] * HEADS, axis=1
    )
    bias_layer(2)
    at_token = jnp.concatenate([own_id_cols, halo_id_cols], axis=0) == iota((EXT, CA), 1)
    pick_t = at_token[:ATOMS].astype(F32).astype(BF16)[:, :SPAN]
    token_atoms = jnp.sum(at_token.astype(F32), axis=0, keepdims=True)
    atom_counts = jnp.sum(jnp.where(at_token[:ATOMS], token_atoms, 0.0), axis=1, keepdims=True)
    inverse = 1.0 / jnp.maximum(atom_counts, 1.0)
    arrive(inner_copies)
    kv_wide[ATOMS:EXT] = nn(rows_buf[ATOMS:EXT], attn_in_ref[1, :, CA : 3 * CA]).astype(BF16)
    attended = attend_own(1, kv_wide, [])
    gates = jax.nn.sigmoid(nt(gate_t[1], rows_buf[:EXT]))
    q_rim[...] = by_head(nn(rows_buf[ATOMS:EXT], attn_in_ref[1, :, :CA]).astype(BF16).astype(F32))
    arrive(outer_copies)
    kv_wide[EXT:] = nn(rows_buf[EXT:], attn_in_ref[1, :, CA : 3 * CA]).astype(BF16)
    attended = jnp.concatenate([attended, attend_rim(1, kv_wide)], axis=1)
    arrive(stream_copies)
    stream_ext = jnp.concatenate([stream, flip(stream_buf[1])], axis=1)
    stream_ext = transition(1, stream_ext, gates, attended, EXT)

    stream = local_layer(2, stream_ext)

    final = flip(stream).astype(BF16)
    arrive(late_copies)
    gradient = None
    for part in range(2):
        weights = agg_ref[...] if part == 0 else agg_buf[...]
        pre = nn(final, weights)
        sig = jax.nn.sigmoid(pre)
        d_act = nn(pick_t, cot_buf[:, part].reshape(SPAN, ACT)) * inverse
        d_pre = (d_act * (sig * (1.0 + pre * (1.0 - sig)))).astype(BF16)
        term = nt(weights, d_pre)
        gradient = term if part == 0 else gradient + term
        if part == 0:
            high, rest = split(pre * sig)
            sums = nn(pick, high) + nn(pick, rest)
            sums_send[0] = sums[:TOK].astype(BF16)
            sums_send[1] = sums[2 * TOK :].astype(BF16)
            own_sums = sums[TOK : 2 * TOK]
            sums_copies = send_all(
                [
                    (sums_send.at[(ds + 1) // 2], sums_recv.at[(ds + 1) // 2], ds, 0, 0)
                    for ds in SIDES
                ]
            )

    def d_middle(n, upstream, lanes):
        d_transit = nn(trans_out_ref[n], upstream.astype(BF16))
        d_wide = jnp.concatenate(
            [
                (d_transit * back_a[n, :, :lanes]).astype(BF16),
                (d_transit * silu_a[n, :, :lanes]).astype(BF16),
            ],
            axis=0,
        )
        d_mid = upstream + norm_back(
            normal_m[n, :, :lanes], scale_m[n, :, :lanes], nn(trans_in_ref[n], d_wide)
        )
        return d_mid, nn(attn_out_ref[n], d_mid.astype(BF16))

    def d_own(n, kv_n, d_att, sent):
        own_d = nt(kv_n[:ATOMS, CA:], d_att)
        halo_d = nt(kv_n[ATOMS:EXT, CA:], d_att)
        own_prod = soft[n, :ATOMS] * own_d
        halo_prod = soft[n, ATOMS:] * halo_d
        inner = jnp.sum(own_prod, axis=0, keepdims=True) + jnp.sum(
            halo_prod, axis=0, keepdims=True
        )
        halo_ds = ((halo_prod - soft[n, ATOMS:] * inner) * SCALE).astype(BF16)
        own_ds = ((own_prod - soft[n, :ATOMS] * inner) * SCALE).astype(BF16)
        if sent is not None:
            sent(halo_ds)
        d_queries = jnp.concatenate(
            [
                nn(
                    key_t[n, width * h : width * (h + 1), :ATOMS],
                    own_ds[:, ATOMS * h : ATOMS * (h + 1)],
                )
                + nn(
                    key_t[n, width * h : width * (h + 1), ATOMS:],
                    halo_ds[:, ATOMS * h : ATOMS * (h + 1)],
                )
                for h in range(HEADS)
            ],
            axis=0,
        ).astype(BF16)
        return d_queries, nn(own_ds, q_heads[n]), nn(soft_b[n, :ATOMS], d_att)

    def weigh_kv(n, d_keys, d_vals):
        return nt(attn_in_ref[n, :, CA : 2 * CA], d_keys) + nt(
            attn_in_ref[n, :, 2 * CA : 3 * CA], d_vals
        )

    def local_back(n, upstream):
        slot = n // 2
        d_mid, d_gated = d_middle(n, upstream, ATOMS)
        d_att = by_head(flip(d_gated * gating[n, :, :ATOMS]))
        d_gate = (d_gated * gate_back[n]).astype(BF16)
        group = []

        def give(kind, values):
            dkv_send[slot, kind] = values.astype(BF16)
            group.extend(
                send_all(
                    [
                        (
                            dkv_send.at[slot, kind, half],
                            dkv_recv.at[slot, kind, half],
                            ds,
                            0,
                            0,
                        )
                        for half, ds in ((lower, 1), (upper, -1))
                    ]
                )
            )

        give(1, nn(soft_b[n, ATOMS:], d_att))
        d_queries, d_keys, d_vals = d_own(
            n, kv[slot], d_att, lambda halo_ds: give(0, nn(halo_ds, q_heads[n]))
        )
        d_normed = (
            nn(attn_in_ref[n, :, :CA], d_queries)
            + nn(attn_in_ref[n, :, 3 * CA :], d_gate)
            + weigh_kv(n, d_keys.astype(BF16), d_vals.astype(BF16))
        )
        part = d_mid + norm_back(normal_x[n, :, :ATOMS], scale_x[n, :, :ATOMS], d_normed)
        return part, group

    def beside(n):
        slot = n // 2
        return norm_back(
            normal_x[n, :, ATOMS:],
            scale_x[n, :, ATOMS:],
            weigh_kv(n, dkv_send[slot, 0], dkv_send[slot, 1]),
        )

    def from_beside(n):
        slot = n // 2
        return norm_back(
            normal_x[n, :, :ATOMS],
            scale_x[n, :, :ATOMS],
            weigh_kv(n, dkv_recv[slot, 0], dkv_recv[slot, 1]),
        )

    part, group = local_back(2, gradient)
    part_send[...] = part.astype(BF16)
    part_copies = send_all([(part_send, part_recv.at[(ds + 1) // 2], ds, 0, 0) for ds in SIDES])
    halo_gradient = beside(2)
    arrive(group)
    gradient = part + from_beside(2)
    arrive(part_copies)
    halo_gradient = halo_gradient + jnp.where(low, part_recv[0], part_recv[1]).astype(F32)
    gradient = jnp.concatenate([gradient, halo_gradient], axis=1)

    d_mid, d_gated = d_middle(1, gradient, EXT)
    d_att_t = d_gated * gating[1]
    d_att = by_head(flip(d_att_t[:, :ATOMS]))
    d_att_rim = by_head(flip(d_att_t[:, ATOMS:]))
    d_gate = (d_gated[:, :ATOMS] * gate_back[1]).astype(BF16)
    d_queries, d_keys, d_vals = d_own(1, kv_wide, d_att, None)
    rim_d = jnp.where(
        low_all,
        nt(right_rows(kv_wide[:, CA:]), d_att_rim),
        nt(left_rows(kv_wide[:, CA:]), d_att_rim),
    )
    rim_prod = soft_rim[...] * rim_d
    rim_inner = jnp.sum(rim_prod, axis=0, keepdims=True)
    rim_ds = (rim_prod[:HALF] - soft_rim[:HALF] * rim_inner) * SCALE
    rim_ds = jnp.concatenate(
        [jnp.where(low_all, 0.0, rim_ds), jnp.where(low_all, rim_ds, 0.0)], axis=0
    ).astype(BF16)
    d_keys = d_keys + nn(rim_ds, q_rim[...])
    d_vals = d_vals + nn(soft_rim_own[...], d_att_rim)
    d_normed = (
        nn(attn_in_ref[1, :, :CA], d_queries)
        + nn(attn_in_ref[1, :, 3 * CA :], d_gate)
        + weigh_kv(1, d_keys.astype(BF16), d_vals.astype(BF16))
    )
    gradient = d_mid[:, :ATOMS] + norm_back(
        normal_x[1, :, :ATOMS], scale_x[1, :, :ATOMS], d_normed
    )

    def per_token(picks, values):
        high, rest = split(values)
        return nt(picks, high) + nt(picks, rest)

    part, group = local_back(0, gradient)
    d_cond = per_token(pick, part)
    cond_send[0] = d_cond[:TOK].astype(BF16)
    cond_send[1] = d_cond[2 * TOK :].astype(BF16)
    last_copies = send_all(
        [(cond_send.at[(ds + 1) // 2], cond_recv.at[(ds + 1) // 2], ds, 0, 0) for ds in SIDES]
    )
    d_cond = d_cond[TOK : 2 * TOK] + per_token(pick_ext[TOK : 2 * TOK, ATOMS:], beside(0))
    arrive(sums_copies)
    token_sums = own_sums + (sums_recv[0].astype(F32) + sums_recv[1].astype(F32))
    diagonal = iota((TOK, TOK), 0) == iota((TOK, TOK), 1)
    counts = jnp.sum(
        jnp.where(diagonal, counts_ref[...].astype(F32), 0.0), axis=1, keepdims=True
    )
    act_out[...] = (token_sums / counts).astype(BF16)
    arrive(group)
    rest_gradient = from_beside(0)
    grad_out[...] = flip(part + rest_gradient).astype(BF16)
    d_cond = d_cond + per_token(pick[TOK : 2 * TOK], rest_gradient)
    arrive(last_copies)
    d_cond = d_cond + (cond_recv[0].astype(F32) + cond_recv[1].astype(F32))
    high, rest = split(d_cond)
    single_out[...] = (nt(high, proj_ref[...]) + nt(rest, proj_ref[...])).astype(BF16)
    for side in (0, -1, 1):
        toward(
            side, lambda side=side: [copy.wait_send() for copy, ds in copies if ds == side] and None
        )


N_COPIES = 5 + 2 + 2 + 11 + 5 + 1 + 6 + 2 + 4 + 2 + 4 + 2


def hand_on(act, grad, single, act_out, grad_out, single_out):
    act_out[...] = act[...]
    grad_out[...] = grad[...]
    single_out[...] = single[...]


def local(
    atom_single,
    token_single,
    pair_band,
    token_counts,
    atom_token,
    window_starts,
    single_proj,
    pair_proj,
    attn_in,
    attn_out,
    trans_in,
    trans_out,
    agg_proj,
    token_cot,
):
    vmem = pl.BlockSpec(memory_space=pltpu.VMEM)
    hbm = pl.BlockSpec(memory_space=pltpu.HBM)

    def scratch(dtype, *shape):
        return pltpu.VMEM(shape, dtype)

    results = (
        jax.ShapeDtypeStruct((TOK, ACT), BF16),
        jax.ShapeDtypeStruct((ATOMS, CA), BF16),
        jax.ShapeDtypeStruct((TOK, COND), BF16),
    )
    results_here = pl.pallas_call(
        kernel,
        out_shape=results,
        in_specs=[hbm] * 14,
        out_specs=(vmem, vmem, vmem),
        scratch_shapes=[
            scratch(BF16, ATOMS, CA),
            scratch(BF16, TOK, COND),
            scratch(BF16, PAIR_ROWS, PAIR_COLS, CA),
            scratch(jnp.int32, 1, TOK),
            scratch(jnp.int32, 1, ATOMS),
            pltpu.SMEM((ATOMS // QB,), jnp.int32),
            scratch(BF16, COND, CA),
            scratch(F32, LAYERS * HEADS, CA),
            scratch(BF16, LAYERS, CA, 4 * CA),
            scratch(BF16, LAYERS, CA, CA),
            scratch(BF16, LAYERS, CA, 2 * FFA),
            scratch(BF16, LAYERS, FFA, CA),
            scratch(BF16, CA, ACT),
            scratch(jnp.int32, 3, 2, ATOMS),
            scratch(BF16, ATOMS, CA),
            scratch(F32, 3, 2, TOK, CA),
            scratch(BF16, 3, 2 * PAIR_PAD, 2 * CA),
            scratch(BF16, 3, 2, TOK, ACT),
            scratch(BF16, CA, ACT),
            scratch(BF16, 3 * ATOMS, CA),
            scratch(F32, 2, ATOMS, CA),
            scratch(BF16, 2, EXT, 2 * CA),
            scratch(BF16, 3 * ATOMS, 2 * CA),
            scratch(F32, LAYERS, EXT, ALL),
            scratch(F32, 3 * HALF, ALL),
            scratch(BF16, 3 * ATOMS, 6 * CA),
            scratch(BF16, LAYERS, CA, CA),
            scratch(BF16, LAYERS, CA, CA),
            scratch(BF16, LAYERS, 2 * FFA, CA),
            scratch(BF16, LAYERS, CA, FFA),
            scratch(F32, LAYERS, EXT, ALL),
            scratch(BF16, LAYERS, EXT, ALL),
            scratch(F32, 3 * HALF, ALL),
            scratch(BF16, ATOMS, ALL),
            scratch(BF16, LAYERS, ALL, CA),
            scratch(BF16, ALL, CA),
            scratch(BF16, LAYERS, CA, EXT),
            scratch(F32, LAYERS, CA, EXT),
            scratch(F32, LAYERS, 1, EXT),
            scratch(F32, LAYERS, CA, EXT),
            scratch(F32, LAYERS, 1, EXT),
            scratch(F32, LAYERS, CA, EXT),
            scratch(F32, LAYERS, CA, ATOMS),
            scratch(F32, LAYERS, FFA, EXT),
            scratch(F32, LAYERS, FFA, EXT),
            scratch(BF16, 2, 2, ATOMS, CA),
            scratch(BF16, 2, 2, ATOMS, CA),
            scratch(BF16, CA, ATOMS),
            scratch(BF16, 2, CA, ATOMS),
            scratch(BF16, 2, TOK, ACT),
            scratch(BF16, 2, TOK, ACT),
            scratch(BF16, 2, TOK, CA),
            scratch(BF16, 2, TOK, CA),
            pltpu.SemaphoreType.DMA((14,)),
            pltpu.SemaphoreType.DMA((N_COPIES,)),
            pltpu.SemaphoreType.DMA((N_COPIES,)),
        ],
        compiler_params=pltpu.CompilerParams(
            collective_id=0, has_side_effects=True, vmem_limit_bytes=64 * 1024 * 1024
        ),
        cost_estimate=pl.CostEstimate(
            flops=2_000_000_000, bytes_accessed=2_000_000, transcendentals=1_000_000
        ),
        name="atoms",
    )(
        atom_single,
        token_single,
        pair_band,
        token_counts.reshape(1, TOK),
        atom_token.reshape(1, ATOMS),
        window_starts,
        single_proj,
        pair_proj.T,
        attn_in,
        attn_out,
        trans_in,
        trans_out,
        agg_proj,
        token_cot,
    )
    return pl.pallas_call(
        hand_on,
        out_shape=results,
        in_specs=[vmem] * 3,
        out_specs=(vmem,) * 3,
        name="results",
    )(*results_here)


def solution(mesh):
    return jax.shard_map(
        local,
        mesh=mesh,
        in_specs=(
            P("seq", None),
            P("seq", "row"),
            P(("seq", "row"), "col", None),
            P("seq"),
            P("seq"),
            P("seq"),
            P("row", None),
            P(),
            P(),
            P(),
            P(),
            P(),
            P(None, "row"),
            P("seq", "row"),
        ),
        out_specs=(P("seq", "row"), P("seq", None), P("seq", "row")),
        check_vma=False,
    )
```

```python
import functools

import jax
import jax.numpy as jnp
from jax import lax
from jax.experimental import pallas as pl
from jax.experimental.pallas import tpu as pltpu
from jax.sharding import PartitionSpec as P

HEADS = 4
QB = 32
KW = 128
LAYERS = 3
ATOMS = 128
CA = 128
TOK = 16
COND = 192
ACT = 384
FFA = 256
PAIR_ROWS = 8
PAIR_COLS = 40
PAIR_PAD = 48
SPAN = 3 * TOK
HALF = 64
EXT = 256
ALL = HEADS * ATOMS
F32 = jnp.float32
BF16 = jnp.bfloat16
EPS = 1e-05
SCALE = (CA // HEADS) ** (-0.5)
MESH = pl.DeviceIdType.MESH

PARTNERS = [
    (ds, dr, dc)
    for ds in (0, -1, 1)
    for dr in (0, 1)
    for dc in (0, 1)
    if (ds, dr, dc) != (0, 0, 0)
]
COND_PARTNERS = [p for p in PARTNERS if p[2] == 0]
SIDES = (-1, 1)


def nn(a, b):
    return lax.dot_general(a, b, (((1,), (0,)), ((), ())), preferred_element_type=F32)


def nt(a, b):
    return lax.dot_general(a, b, (((1,), (1,)), ((), ())), preferred_element_type=F32)


def tn(a, b):
    return lax.dot_general(a, b, (((0,), (0,)), ((), ())), preferred_element_type=F32)


def flip(values):
    return jnp.transpose(values, (1, 0))


def iota(shape, dim):
    return lax.broadcasted_iota(jnp.int32, shape, dim)


def norm_rows(values):
    centre = values - jnp.mean(values, axis=0, keepdims=True)
    scaling = lax.rsqrt(jnp.mean(centre * centre, axis=0, keepdims=True) + EPS)
    return centre * scaling, scaling


def norm_back(normal, scaling, upstream):
    return scaling * (
        upstream
        - jnp.mean(upstream, axis=0, keepdims=True)
        - normal * jnp.mean(upstream * normal, axis=0, keepdims=True)
    )


def by_head(columns):
    width = CA // HEADS
    none = jnp.zeros((width, columns.shape[1]), BF16)
    return jnp.concatenate(
        [
            jnp.concatenate(
                [columns[width * h : width * (h + 1)] if g == h else none for g in range(HEADS)],
                axis=0,
            )
            for h in range(HEADS)
        ],
        axis=1,
    )


def split(values):
    high = values.astype(BF16)
    return high, (values - high.astype(F32)).astype(BF16)


def kernel(
    atom_hbm,
    single_hbm,
    band_hbm,
    counts_hbm,
    ids_hbm,
    starts_hbm,
    proj_hbm,
    pair_proj_hbm,
    attn_in_hbm,
    attn_out_hbm,
    trans_in_hbm,
    trans_out_hbm,
    agg_hbm,
    cot_hbm,
    act_out,
    grad_out,
    single_out,
    atom_ref,
    single_ref,
    band_ref,
    counts_ref,
    ids_ref,
    starts_ref,
    proj_ref,
    pair_proj_ref,
    attn_in_ref,
    attn_out_ref,
    trans_in_ref,
    trans_out_ref,
    agg_ref,
    id_buf,
    halo_buf,
    cond_buf,
    pair_buf,
    cot_buf,
    agg_buf,
    rows_buf,
    stream_buf,
    kv,
    kv_wide,
    bias,
    bias_rim,
    takes,
    query_t,
    gate_t,
    out_t,
    in_t,
    down_t,
    soft,
    soft_b,
    soft_rim,
    soft_rim_own,
    q_heads,
    q_rim,
    key_t,
    normal_x,
    scale_x,
    normal_m,
    scale_m,
    gating,
    gate_back,
    silu_a,
    back_a,
    own_picks,
    edge_send,
    edge_recv,
    sums_send,
    sums_recv,
    local_sem,
    send_sem,
    recv_sem,
):
    seq = lax.axis_index("seq")
    row = lax.axis_index("row")
    col = lax.axis_index("col")
    seqs = lax.axis_size("seq")
    width = CA // HEADS

    def partner(ds, dr, dc):
        return (
            lax.rem(seq + ds + seqs, seqs),
            lax.rem(row + dr, 2),
            lax.rem(col + dc, 2),
        )

    has = {-1: seq > 0, 1: seq < seqs - 1}

    def toward(ds, act):
        if ds == 0:
            act()
        else:
            pl.when(has[ds])(act)

    copies = []

    def each(group, side, source, act):
        mine = [copy for copy, ds in group if ds == side]

        def run():
            for copy in mine:
                act(copy)

        if mine:
            toward(source, run)

    def send_all(wanted):
        group = []
        for src, dst, ds, dr, dc in wanted:
            place = len(copies)
            copy = pltpu.make_async_remote_copy(
                src_ref=src,
                dst_ref=dst,
                send_sem=send_sem.at[place],
                recv_sem=recv_sem.at[place],
                device_id=partner(ds, dr, dc),
                device_id_type=MESH,
            )
            copies.append((copy, ds))
            group.append((copy, ds))
        for side in (-1, 1, 0):
            each(group, side, side, lambda copy: copy.start())
        return group

    def arrive(group):
        for side in (0, -1, 1):
            each(group, side, -side, lambda copy: copy.wait_recv())

    fetches = []

    def fetch(src, dst):
        copy = pltpu.make_async_copy(src, dst, local_sem.at[len(fetches)])
        copy.start()
        fetches.append(copy)
        return copy

    first_fetch = [fetch(single_hbm, single_ref), fetch(proj_hbm, proj_ref)]

    barrier = pltpu.get_barrier_semaphore()

    def greet(side):
        for ds, dr, dc in PARTNERS:
            if ds == side:
                pl.semaphore_signal(
                    barrier, inc=1, device_id=partner(ds, dr, dc), device_id_type=MESH
                )

    for side in (-1, 1, 0):
        toward(side, functools.partial(greet, side))

    pair_fetch = [fetch(band_hbm, band_ref), fetch(pair_proj_hbm, pair_proj_ref)]
    id_fetch = [fetch(ids_hbm, ids_ref), fetch(starts_hbm, starts_ref)]
    atom_fetch = [fetch(atom_hbm, atom_ref)]
    weight_fetch = [
        fetch(attn_in_hbm, attn_in_ref),
        fetch(attn_out_hbm, attn_out_ref),
        fetch(trans_in_hbm, trans_in_ref),
        fetch(trans_out_hbm, trans_out_ref),
        fetch(agg_hbm, agg_ref),
        fetch(cot_hbm, cot_buf.at[1, 0]),
        fetch(counts_hbm, counts_ref),
    ]

    near, far = pl.ds(0, HALF), pl.ds(HALF, HALF)

    def close(slot, half):
        id_buf[slot, 0:1] = jnp.full((1, ATOMS), -(2**20), jnp.int32)
        id_buf[slot, 1:2] = jnp.full((1, ATOMS), 2**20, jnp.int32)
        cond_buf[slot] = jnp.zeros(cond_buf.shape[1:], F32)
        pair_buf[slot] = jnp.zeros(pair_buf.shape[1:], BF16)
        cot_buf[slot] = jnp.zeros(cot_buf.shape[1:], BF16)
        halo_buf[half] = jnp.zeros((HALF, CA), BF16)
        for at in (ATOMS, EXT):
            other = (half.start + at - ATOMS) % ATOMS
            rows_buf[at + other : at + other + HALF] = jnp.zeros((HALF, CA), BF16)
        stream_buf[1, half] = jnp.zeros((HALF, CA), F32)
        side = 1 if slot == 0 else 0
        for back in range(2):
            edge_recv[back, side] = jnp.zeros((CA, ATOMS), BF16)
        sums_recv[side] = jnp.zeros((TOK, ACT), BF16)

    pl.when(seq == 0)(lambda: close(0, far))
    pl.when(seq == seqs - 1)(lambda: close(2, near))

    for copy in first_fetch:
        copy.wait()
    cond_buf[1, 0] = nn(single_ref[...], proj_ref[...])
    for copy in id_fetch:
        copy.wait()
    lane = iota((1, ATOMS), 1)
    own_first = jnp.zeros((1, ATOMS), jnp.int32)
    for b in range(ATOMS // QB):
        own_first = jnp.where(lane // QB == b, starts_ref[b], own_first)
    id_buf[1, 0:1] = ids_ref[...]
    id_buf[1, 1:2] = own_first
    for copy in pair_fetch:
        copy.wait()
    place_h = (iota((LAYERS * HEADS, CA), 1) == 8 * iota((LAYERS * HEADS, CA), 0)).astype(BF16)
    pp_high, pp_rest = split(pair_proj_ref[...])
    spread_high = tn(pp_high, place_h).astype(BF16)
    spread_rest = tn(pp_rest, place_h).astype(BF16)
    band = band_ref[...].astype(F32).reshape(PAIR_ROWS * PAIR_COLS, CA)
    centre = band - jnp.mean(band, axis=1, keepdims=True)
    normal = centre * lax.rsqrt(jnp.mean(centre * centre, axis=1, keepdims=True) + EPS)
    n_high, n_rest = split(normal)
    pairs = nn(n_high, spread_high) + nn(n_high, spread_rest) + nn(n_rest, spread_high)
    tile = pairs[:PAIR_COLS]
    for i in range(1, PAIR_ROWS):
        tile = tile + pltpu.roll(pairs[PAIR_COLS * i : PAIR_COLS * (i + 1)], i, 1)
    tile = jnp.concatenate([tile, jnp.zeros((PAIR_PAD - PAIR_COLS, CA), F32)], axis=0)
    pair_rows = pl.ds(pl.multiple_of(col * PAIR_PAD, 16), PAIR_PAD)
    pair_lanes = pl.ds(pl.multiple_of(row * CA, CA), CA)
    pair_buf[1, pair_rows, pair_lanes] = tile.astype(BF16)

    beyond = len(PARTNERS) // 3 + 1
    pl.semaphore_wait(
        barrier, beyond - 1 + beyond * (has[-1].astype(jnp.int32) + has[1].astype(jnp.int32))
    )

    cond_copies = send_all(
        [
            (cond_buf.at[1, 0], cond_buf.at[1 - ds, dr], ds, dr, dc)
            for ds, dr, dc in COND_PARTNERS
        ]
        + [(id_buf.at[1], id_buf.at[1 - ds], ds, 0, 0) for ds in SIDES]
        + [
            (atom_hbm.at[near], halo_buf.at[near], -1, 0, 0),
            (atom_hbm.at[far], halo_buf.at[far], 1, 0, 0),
        ]
    )
    pair_copies = send_all(
        [
            (
                pair_buf.at[1, pair_rows, pair_lanes],
                pair_buf.at[1 - ds, pair_rows, pair_lanes],
                ds,
                dr,
                dc,
            )
            for ds, dr, dc in PARTNERS
        ]
    )
    for copy in atom_fetch + weight_fetch:
        copy.wait()
    for n in range(LAYERS):
        query_t[n] = flip(attn_in_ref[n, :, :CA])
        gate_t[n] = flip(attn_in_ref[n, :, 3 * CA :])
        out_t[n] = flip(attn_out_ref[n])
        in_t[n] = flip(trans_in_ref[n])
        down_t[n] = flip(trans_out_ref[n])

    token_base = TOK * (seq - 1)
    atom_base = seq * ATOMS
    low = lane < HALF

    def as_cols(ids):
        return flip(jnp.broadcast_to(ids.astype(F32), (CA, ATOMS))).astype(jnp.int32)

    own_ids = ids_ref[...] - token_base
    own_id_cols = as_cols(own_ids)
    atom_t = flip(atom_ref[...]).astype(F32)

    arrive(cond_copies)
    left_ids = id_buf[0, 0:1] - token_base
    right_ids = id_buf[2, 0:1] - token_base
    halo_ids = jnp.where(low, right_ids, left_ids)
    halo_id_cols = as_cols(halo_ids)
    pick_ext = (iota((SPAN, EXT), 0) == jnp.concatenate([own_ids, halo_ids], axis=1)).astype(
        F32
    ).astype(BF16)
    pick = pick_ext[:, :ATOMS]
    cond = (cond_buf[:, 0] + cond_buf[:, 1]).astype(BF16).reshape(SPAN, CA)
    cond_t = flip(cond)
    stream_ext = jnp.concatenate([atom_t, flip(halo_buf[...]).astype(F32)], axis=1) + nn(
        cond_t, pick_ext
    )

    position = iota((EXT, ATOMS), 0)
    position = jnp.where(position < ATOMS + HALF, position, position - EXT)
    first = own_first - atom_base
    outside = jnp.where((position >= first) & (position < first + KW), 0.0, -1e30)
    outside = jnp.concatenate([outside] * HEADS, axis=1)

    place = iota((2 * CA, ATOMS), 0)
    head_of = (place // PAIR_ROWS) % HEADS
    token_of = PAIR_ROWS * (place // (PAIR_ROWS * HEADS)) + place % PAIR_ROWS

    def take_of(id_cols):
        lanes = iota((id_cols.shape[0], CA), 1)
        column = jnp.where(
            lanes < PAIR_PAD,
            jnp.where(lanes < PAIR_COLS, lanes, -4096),
            jnp.where(lanes < PAIR_PAD + PAIR_COLS, lanes - (PAIR_PAD - PAIR_COLS), -4096),
        )
        return jnp.concatenate(
            [
                (id_cols + (2 - s) * TOK == column).astype(F32).astype(BF16)
                for s in range(3)
            ],
            axis=1,
        )

    def table_of(n):
        part = PAIR_ROWS * HEADS
        none = jnp.zeros((CA, CA), BF16)
        blocks = []
        for s in range(3):
            at = 2 * part * (s % 2)
            here = pair_buf[s].astype(F32)
            halves = []
            for r in range(2):
                shift = (at + part * r - part * n) % CA
                half = here[:, CA * r : CA * (r + 1)]
                halves.append(pltpu.roll(half, shift, 1) if shift else half)
            inside = lane - at
            piece = jnp.where(
                (inside >= 0) & (inside < part),
                halves[0],
                jnp.where((inside >= part) & (inside < 2 * part), halves[1], 0.0),
            ).astype(BF16)
            piece = jnp.concatenate([piece, none[: CA - 2 * PAIR_PAD]], axis=0)
            blocks.append(jnp.concatenate([piece, none] if s < 2 else [none, piece], axis=1))
        return jnp.concatenate(blocks, axis=0)

    def bias_picks(ids):
        hit = token_of == ids
        return jnp.concatenate(
            [(hit & (head_of == h)).astype(F32).astype(BF16) for h in range(HEADS)], axis=1
        )

    def bias_of(taken, n, picks):
        return nn(nn(taken, table_of(n)).astype(BF16), picks)

    def right_rows(values):
        return jnp.concatenate(
            [values[HALF:ATOMS], values[ATOMS : ATOMS + HALF], values[EXT : EXT + HALF]], axis=0
        )

    def left_rows(values):
        return jnp.concatenate(
            [values[:HALF], values[ATOMS + HALF : EXT], values[EXT + HALF :]], axis=0
        )

    low_all = jnp.concatenate([low] * HEADS, axis=1)

    def attend_own(n, kv_n, heads):
        scores = nn(kv_n[:EXT, :CA], heads) * SCALE + bias[n]
        values_t = flip(kv_n[:EXT, CA:])
        exps = jnp.exp(scores - jnp.max(scores, axis=0, keepdims=True))
        weights = exps * (1.0 / jnp.sum(exps, axis=0, keepdims=True))
        rounded = weights.astype(BF16)
        soft[n] = weights
        soft_b[n] = rounded
        key_t[n] = flip(kv_n[:EXT, :CA])
        return jnp.concatenate(
            [
                nn(
                    values_t[width * h : width * (h + 1)],
                    rounded[:, ATOMS * h : ATOMS * (h + 1)],
                )
                for h in range(HEADS)
            ],
            axis=0,
        )

    def attend_rim(n, kv_n, heads):
        right_kv = right_rows(kv_n)
        left_kv = left_rows(kv_n)
        scores = jnp.where(
            low_all, nn(right_kv[:, :CA], heads), nn(left_kv[:, :CA], heads)
        )
        scores = scores * SCALE + bias_rim[...]
        most = jnp.maximum(jnp.max(scores, axis=0, keepdims=True), -1e29)
        exps = jnp.exp(scores - most)
        weights = exps * (1.0 / jnp.maximum(jnp.sum(exps, axis=0, keepdims=True), 1e-30))
        soft_rim[...] = weights
        rounded = weights.astype(BF16)
        near = weights[:HALF]
        soft_rim_own[:HALF] = jnp.where(low_all, 0.0, near).astype(BF16)
        soft_rim_own[HALF:] = jnp.where(low_all, near, 0.0).astype(BF16)
        right_t = flip(right_kv[:, CA:])
        left_t = flip(left_kv[:, CA:])
        parts = []
        for h in range(HEADS):
            here = rounded[:, ATOMS * h : ATOMS * (h + 1)]
            parts.append(
                jnp.where(
                    low,
                    nn(right_t[width * h : width * (h + 1)], here),
                    nn(left_t[width * h : width * (h + 1)], here),
                )
            )
        return jnp.concatenate(parts, axis=0)

    def transition(n, stream, gates, attended, lanes):
        gated = gates * attended
        gating[n, :, :lanes] = gates
        gate_back[n] = gated[:, :ATOMS] * (1.0 - gates[:, :ATOMS])
        x_mid = stream + nn(out_t[n], gated.astype(BF16))
        normal, scaling = norm_rows(x_mid)
        normal_m[n, :, :lanes] = normal
        scale_m[n, :, :lanes] = scaling
        widened = nn(in_t[n], normal.astype(BF16))
        part_a = widened[:FFA]
        part_b = widened[FFA:]
        sig = jax.nn.sigmoid(part_a)
        act = part_a * sig
        silu_a[n, :, :lanes] = act
        back_a[n, :, :lanes] = part_b * (sig * (1.0 + part_a * (1.0 - sig)))
        return x_mid + nn(down_t[n], (act * part_b).astype(BF16))

    def local_layer(n, stream_ext):
        normal_ext, scale_ext = norm_rows(stream_ext)
        normal_x[n] = normal_ext
        scale_x[n] = scale_ext
        rows_ext = flip(normal_ext.astype(BF16))
        kv[n // 2] = nn(rows_ext, attn_in_ref[n, :, CA : 3 * CA]).astype(BF16)
        normed = normal_ext[:, :ATOMS].astype(BF16)
        heads = by_head(nn(query_t[n], normed).astype(BF16))
        q_heads[n] = flip(heads)
        gates = jax.nn.sigmoid(nn(gate_t[n], normed))
        if n == 0:
            own_picks[...] = bias_picks(own_ids)
            takes[:EXT] = take_of(jnp.concatenate([own_id_cols, halo_id_cols], axis=0))
            arrive(pair_copies)
            bias[0] = bias_of(takes[:EXT], 0, own_picks[...]) + outside
        attended = attend_own(n, kv[n // 2], heads)
        return transition(n, stream_ext[:, :ATOMS], gates, attended, ATOMS)

    stream = local_layer(0, stream_ext)

    normal, scaling = norm_rows(stream)
    normal_x[1, :, :ATOMS] = normal
    scale_x[1, :, :ATOMS] = scaling
    rows_buf[:ATOMS] = flip(normal.astype(BF16))
    lower, upper = near, far
    inner_copies = send_all(
        [
            (rows_buf.at[lower], rows_buf.at[pl.ds(ATOMS, HALF)], -1, 0, 0),
            (rows_buf.at[upper], rows_buf.at[pl.ds(ATOMS + HALF, HALF)], 1, 0, 0),
        ]
    )
    outer_copies = send_all(
        [
            (rows_buf.at[upper], rows_buf.at[pl.ds(EXT, HALF)], -1, 0, 0),
            (rows_buf.at[lower], rows_buf.at[pl.ds(EXT + HALF, HALF)], 1, 0, 0),
        ]
    )
    stream_buf[0] = flip(stream)
    stream_copies = send_all(
        [
            (stream_buf.at[0, lower], stream_buf.at[1, lower], -1, 0, 0),
            (stream_buf.at[0, upper], stream_buf.at[1, upper], 1, 0, 0),
        ]
    )
    late_copies = send_all(
        [(cot_hbm, cot_buf.at[1 - ds, dr], ds, dr, dc) for ds, dr, dc in COND_PARTNERS]
        + [(agg_hbm, agg_buf, 0, 1, 0)]
    )

    kv_wide[:ATOMS] = nn(rows_buf[:ATOMS], attn_in_ref[1, :, CA : 3 * CA]).astype(BF16)
    heads = by_head(nn(query_t[1], normal.astype(BF16)).astype(BF16))
    q_heads[1] = flip(heads)
    outer_ids = pltpu.roll(jnp.where(low, left_ids, right_ids), HALF, 1)
    takes[EXT:] = take_of(as_cols(outer_ids))
    mixed = nn(takes[...], table_of(1)).astype(BF16)
    bias[1] = nn(mixed[:EXT], own_picks[...]) + outside
    rim_full = nn(mixed, bias_picks(halo_ids))
    rim_rows = iota((3 * HALF, ATOMS), 0)
    left_position = jnp.where(
        rim_rows < HALF,
        rim_rows,
        jnp.where(rim_rows < ATOMS, rim_rows - ATOMS, rim_rows - EXT),
    )
    rim_position = jnp.where(low, HALF + rim_rows, left_position)
    rim_first = jnp.where(low, id_buf[2, 1:2], id_buf[0, 1:2]) - atom_base
    rim_outside = jnp.where(
        (rim_position >= rim_first) & (rim_position < rim_first + KW), 0.0, -1e30
    )
    bias_rim[...] = jnp.where(low_all, right_rows(rim_full), left_rows(rim_full)) + jnp.concatenate(
        [rim_outside] * HEADS, axis=1
    )
    bias[2] = bias_of(takes[:EXT], 2, own_picks[...]) + outside
    at_token = jnp.concatenate([own_id_cols, halo_id_cols], axis=0) == iota((EXT, CA), 1)
    pick_t = at_token[:ATOMS].astype(F32).astype(BF16)[:, :SPAN]
    token_atoms = jnp.sum(at_token.astype(F32), axis=0, keepdims=True)
    atom_counts = jnp.sum(jnp.where(at_token[:ATOMS], token_atoms, 0.0), axis=1, keepdims=True)
    inverse = 1.0 / jnp.maximum(atom_counts, 1.0)
    arrive(inner_copies)
    kv_wide[ATOMS:EXT] = nn(rows_buf[ATOMS:EXT], attn_in_ref[1, :, CA : 3 * CA]).astype(BF16)
    attended = attend_own(1, kv_wide, heads)
    gates = jax.nn.sigmoid(nt(gate_t[1], rows_buf[:EXT]))
    heads = by_head(nt(query_t[1], rows_buf[ATOMS:EXT]).astype(BF16))
    q_rim[...] = flip(heads)
    arrive(outer_copies)
    kv_wide[EXT:] = nn(rows_buf[EXT:], attn_in_ref[1, :, CA : 3 * CA]).astype(BF16)
    attended = jnp.concatenate([attended, attend_rim(1, kv_wide, heads)], axis=1)
    arrive(stream_copies)
    stream_ext = jnp.concatenate([stream, flip(stream_buf[1])], axis=1)
    stream_ext = transition(1, stream_ext, gates, attended, EXT)

    stream = local_layer(2, stream_ext)

    final = flip(stream.astype(BF16))
    arrive(late_copies)
    gradient = None
    for part in range(2):
        weights = agg_ref[...] if part == 0 else agg_buf[...]
        pre = nn(final, weights)
        sig = jax.nn.sigmoid(pre)
        d_act = nn(pick_t, cot_buf[:, part].reshape(SPAN, ACT)) * inverse
        d_pre = (d_act * (sig * (1.0 + pre * (1.0 - sig)))).astype(BF16)
        term = nt(weights, d_pre)
        gradient = term if part == 0 else gradient + term
        if part == 0:
            high, rest = split(pre * sig)
            sums = nn(pick, high) + nn(pick, rest)
            sums_send[0] = sums[:TOK].astype(BF16)
            sums_send[1] = sums[2 * TOK :].astype(BF16)
            own_sums = sums[TOK : 2 * TOK]
            sums_copies = send_all(
                [
                    (sums_send.at[(ds + 1) // 2], sums_recv.at[(ds + 1) // 2], ds, 0, 0)
                    for ds in SIDES
                ]
            )

    def d_middle(n, upstream, lanes):
        d_transit = nn(trans_out_ref[n], upstream.astype(BF16))
        d_wide = jnp.concatenate(
            [
                (d_transit * back_a[n, :, :lanes]).astype(BF16),
                (d_transit * silu_a[n, :, :lanes]).astype(BF16),
            ],
            axis=0,
        )
        d_mid = upstream + norm_back(
            normal_m[n, :, :lanes], scale_m[n, :, :lanes], nn(trans_in_ref[n], d_wide)
        )
        return d_mid, nn(attn_out_ref[n], d_mid.astype(BF16))

    def d_own(n, kv_n, d_heads, d_att):
        own_d = nn(kv_n[:ATOMS, CA:], d_heads)
        halo_d = nn(kv_n[ATOMS:EXT, CA:], d_heads)
        own_prod = soft[n, :ATOMS] * own_d
        halo_prod = soft[n, ATOMS:] * halo_d
        inner = jnp.sum(own_prod, axis=0, keepdims=True) + jnp.sum(
            halo_prod, axis=0, keepdims=True
        )
        halo_ds = ((halo_prod - soft[n, ATOMS:] * inner) * SCALE).astype(BF16)
        own_ds = ((own_prod - soft[n, :ATOMS] * inner) * SCALE).astype(BF16)
        d_queries = jnp.concatenate(
            [
                nn(
                    key_t[n, width * h : width * (h + 1), :ATOMS],
                    own_ds[:, ATOMS * h : ATOMS * (h + 1)],
                )
                + nn(
                    key_t[n, width * h : width * (h + 1), ATOMS:],
                    halo_ds[:, ATOMS * h : ATOMS * (h + 1)],
                )
                for h in range(HEADS)
            ],
            axis=0,
        ).astype(BF16)
        return d_queries, nn(own_ds, q_heads[n]), nn(soft_b[n, :ATOMS], d_att), halo_ds

    def weigh_kv(n, d_keys, d_vals):
        return nt(attn_in_ref[n, :, CA : 2 * CA], d_keys) + nt(
            attn_in_ref[n, :, 2 * CA : 3 * CA], d_vals
        )

    def local_back(n, upstream):
        slot = n // 2
        d_mid, d_gated = d_middle(n, upstream, ATOMS)
        d_heads = by_head((d_gated * gating[n, :, :ATOMS]).astype(BF16))
        d_att = flip(d_heads)
        d_gate = (d_gated * gate_back[n]).astype(BF16)
        d_queries, d_keys, d_vals, halo_ds = d_own(n, kv[slot], d_heads, d_att)
        beside = norm_back(
            normal_x[n, :, ATOMS:],
            scale_x[n, :, ATOMS:],
            weigh_kv(
                n,
                nn(halo_ds, q_heads[n]).astype(BF16),
                nn(soft_b[n, ATOMS:], d_att).astype(BF16),
            ),
        )
        d_normed = (
            nn(attn_in_ref[n, :, :CA], d_queries)
            + nn(attn_in_ref[n, :, 3 * CA :], d_gate)
            + weigh_kv(n, d_keys.astype(BF16), d_vals.astype(BF16))
        )
        part = d_mid + norm_back(normal_x[n, :, :ATOMS], scale_x[n, :, :ATOMS], d_normed)
        edge_send[slot, 0] = jnp.where(low, part, beside).astype(BF16)
        edge_send[slot, 1] = jnp.where(low, beside, part).astype(BF16)
        arrive(
            send_all(
                [
                    (edge_send.at[slot, side], edge_recv.at[slot, side], ds, 0, 0)
                    for side, ds in enumerate(SIDES)
                ]
            )
        )
        from_right, from_left = edge_recv[slot, 0].astype(F32), edge_recv[slot, 1].astype(F32)
        return jnp.concatenate(
            [
                part + jnp.where(low, from_left, from_right),
                beside + jnp.where(low, from_right, from_left),
            ],
            axis=1,
        )

    gradient = local_back(2, gradient)

    d_mid, d_gated = d_middle(1, gradient, EXT)
    d_att_t = (d_gated * gating[1]).astype(BF16)
    d_heads = by_head(d_att_t[:, :ATOMS])
    d_att = flip(d_heads)
    d_heads_rim = by_head(d_att_t[:, ATOMS:])
    d_att_rim = flip(d_heads_rim)
    d_gate = (d_gated[:, :ATOMS] * gate_back[1]).astype(BF16)
    d_queries, d_keys, d_vals, _ = d_own(1, kv_wide, d_heads, d_att)
    rim_d = jnp.where(
        low_all,
        nn(right_rows(kv_wide[:, CA:]), d_heads_rim),
        nn(left_rows(kv_wide[:, CA:]), d_heads_rim),
    )
    rim_prod = soft_rim[...] * rim_d
    rim_inner = jnp.sum(rim_prod, axis=0, keepdims=True)
    rim_ds = (rim_prod[:HALF] - soft_rim[:HALF] * rim_inner) * SCALE
    rim_ds = jnp.concatenate(
        [jnp.where(low_all, 0.0, rim_ds), jnp.where(low_all, rim_ds, 0.0)], axis=0
    ).astype(BF16)
    d_keys = d_keys + nn(rim_ds, q_rim[...])
    d_vals = d_vals + nn(soft_rim_own[...], d_att_rim)
    d_normed = (
        nn(attn_in_ref[1, :, :CA], d_queries)
        + nn(attn_in_ref[1, :, 3 * CA :], d_gate)
        + weigh_kv(1, d_keys.astype(BF16), d_vals.astype(BF16))
    )
    gradient = d_mid[:, :ATOMS] + norm_back(
        normal_x[1, :, :ATOMS], scale_x[1, :, :ATOMS], d_normed
    )

    def per_token(picks, values):
        high, rest = split(values)
        return nt(picks, high) + nt(picks, rest)

    arrive(sums_copies)
    token_sums = own_sums + (sums_recv[0].astype(F32) + sums_recv[1].astype(F32))
    diagonal = iota((TOK, TOK), 0) == iota((TOK, TOK), 1)
    counts = jnp.sum(
        jnp.where(diagonal, counts_ref[...].astype(F32), 0.0), axis=1, keepdims=True
    )
    act_out[...] = (token_sums / counts).astype(BF16)
    gradient = local_back(0, gradient)
    grad_out[...] = flip(gradient[:, :ATOMS].astype(BF16))
    d_cond = per_token(pick_ext[TOK : 2 * TOK], gradient)
    high, rest = split(d_cond)
    single_out[...] = (nt(high, proj_ref[...]) + nt(rest, proj_ref[...])).astype(BF16)
    for side in (0, -1, 1):
        each(copies, side, side, lambda copy: copy.wait_send())


N_COPIES = 5 + 2 + 2 + 11 + 5 + 1 + 6 + 2 + 2 + 2


def hand_on(act, grad, single, act_out, grad_out, single_out):
    act_out[...] = act[...]
    grad_out[...] = grad[...]
    single_out[...] = single[...]


def local(
    atom_single,
    token_single,
    pair_band,
    token_counts,
    atom_token,
    window_starts,
    single_proj,
    pair_proj,
    attn_in,
    attn_out,
    trans_in,
    trans_out,
    agg_proj,
    token_cot,
):
    vmem = pl.BlockSpec(memory_space=pltpu.VMEM)
    hbm = pl.BlockSpec(memory_space=pltpu.HBM)

    def scratch(dtype, *shape):
        return pltpu.VMEM(shape, dtype)

    results = (
        jax.ShapeDtypeStruct((TOK, ACT), BF16),
        jax.ShapeDtypeStruct((ATOMS, CA), BF16),
        jax.ShapeDtypeStruct((TOK, COND), BF16),
    )
    results_here = pl.pallas_call(
        kernel,
        out_shape=results,
        in_specs=[hbm] * 14,
        out_specs=(vmem, vmem, vmem),
        scratch_shapes=[
            scratch(BF16, ATOMS, CA),
            scratch(BF16, TOK, COND),
            scratch(BF16, PAIR_ROWS, PAIR_COLS, CA),
            scratch(jnp.int32, 1, TOK),
            scratch(jnp.int32, 1, ATOMS),
            pltpu.SMEM((ATOMS // QB,), jnp.int32),
            scratch(BF16, COND, CA),
            scratch(F32, LAYERS * HEADS, CA),
            scratch(BF16, LAYERS, CA, 4 * CA),
            scratch(BF16, LAYERS, CA, CA),
            scratch(BF16, LAYERS, CA, 2 * FFA),
            scratch(BF16, LAYERS, FFA, CA),
            scratch(BF16, CA, ACT),
            scratch(jnp.int32, 3, 2, ATOMS),
            scratch(BF16, ATOMS, CA),
            scratch(F32, 3, 2, TOK, CA),
            scratch(BF16, 3, 2 * PAIR_PAD, 2 * CA),
            scratch(BF16, 3, 2, TOK, ACT),
            scratch(BF16, CA, ACT),
            scratch(BF16, 3 * ATOMS, CA),
            scratch(F32, 2, ATOMS, CA),
            scratch(BF16, 2, EXT, 2 * CA),
            scratch(BF16, 3 * ATOMS, 2 * CA),
            scratch(F32, LAYERS, EXT, ALL),
            scratch(F32, 3 * HALF, ALL),
            scratch(BF16, 3 * ATOMS, 3 * CA),
            scratch(BF16, LAYERS, CA, CA),
            scratch(BF16, LAYERS, CA, CA),
            scratch(BF16, LAYERS, CA, CA),
            scratch(BF16, LAYERS, 2 * FFA, CA),
            scratch(BF16, LAYERS, CA, FFA),
            scratch(F32, LAYERS, EXT, ALL),
            scratch(BF16, LAYERS, EXT, ALL),
            scratch(F32, 3 * HALF, ALL),
            scratch(BF16, ATOMS, ALL),
            scratch(BF16, LAYERS, ALL, CA),
            scratch(BF16, ALL, CA),
            scratch(BF16, LAYERS, CA, EXT),
            scratch(F32, LAYERS, CA, EXT),
            scratch(F32, LAYERS, 1, EXT),
            scratch(F32, LAYERS, CA, EXT),
            scratch(F32, LAYERS, 1, EXT),
            scratch(F32, LAYERS, CA, EXT),
            scratch(F32, LAYERS, CA, ATOMS),
            scratch(F32, LAYERS, FFA, EXT),
            scratch(F32, LAYERS, FFA, EXT),
            scratch(BF16, 2 * CA, ALL),
            scratch(BF16, 2, 2, CA, ATOMS),
            scratch(BF16, 2, 2, CA, ATOMS),
            scratch(BF16, 2, TOK, ACT),
            scratch(BF16, 2, TOK, ACT),
            pltpu.SemaphoreType.DMA((14,)),
            pltpu.SemaphoreType.DMA((N_COPIES,)),
            pltpu.SemaphoreType.DMA((N_COPIES,)),
        ],
        compiler_params=pltpu.CompilerParams(
            collective_id=0, has_side_effects=True, vmem_limit_bytes=64 * 1024 * 1024
        ),
        cost_estimate=pl.CostEstimate(
            flops=2_000_000_000, bytes_accessed=2_000_000, transcendentals=1_000_000
        ),
        name="atoms",
    )(
        atom_single,
        token_single,
        pair_band,
        token_counts.reshape(1, TOK),
        atom_token.reshape(1, ATOMS),
        window_starts,
        single_proj,
        pair_proj.T,
        attn_in,
        attn_out,
        trans_in,
        trans_out,
        agg_proj,
        token_cot,
    )
    return pl.pallas_call(
        hand_on,
        out_shape=results,
        in_specs=[vmem] * 3,
        out_specs=(vmem,) * 3,
        name="results",
    )(*results_here)


def solution(mesh):
    return jax.shard_map(
        local,
        mesh=mesh,
        in_specs=(
            P("seq", None),
            P("seq", "row"),
            P(("seq", "row"), "col", None),
            P("seq"),
            P("seq"),
            P("seq"),
            P("row", None),
            P(),
            P(),
            P(),
            P(),
            P(),
            P(None, "row"),
            P("seq", "row"),
        ),
        out_specs=(P("seq", "row"), P("seq", None), P("seq", "row")),
        check_vma=False,
    )
```

```python
import functools

import jax
import jax.numpy as jnp
from jax import lax
from jax.experimental import pallas as pl
from jax.experimental.pallas import tpu as pltpu
from jax.sharding import PartitionSpec as P

HEADS = 4
QB = 32
KW = 128
LAYERS = 3
ATOMS = 128
CA = 128
TOK = 16
COND = 192
ACT = 384
FFA = 256
PAIR_ROWS = 8
PAIR_COLS = 40
PAIR_PAD = 48
SPAN = 3 * TOK
HALF = 64
EXT = 256
ALL = HEADS * ATOMS
F32 = jnp.float32
BF16 = jnp.bfloat16
EPS = 1e-05
SCALE = (CA // HEADS) ** (-0.5)
MESH = pl.DeviceIdType.MESH

PARTNERS = [
    (ds, dr, dc)
    for ds in (0, -1, 1, -2, 2)
    for dr in (0, 1)
    for dc in (0, 1)
    if (ds, dr, dc) != (0, 0, 0)
]
COND_PARTNERS = [p for p in PARTNERS if p[2] == 0]
SIDES = (-1, 1)
REACH = 2
SLOTS = 2 * REACH + 1


def nn(a, b):
    return lax.dot_general(a, b, (((1,), (0,)), ((), ())), preferred_element_type=F32)


def nt(a, b):
    return lax.dot_general(a, b, (((1,), (1,)), ((), ())), preferred_element_type=F32)


def tn(a, b):
    return lax.dot_general(a, b, (((0,), (0,)), ((), ())), preferred_element_type=F32)


def flip(values):
    return jnp.transpose(values, (1, 0))


def iota(shape, dim):
    return lax.broadcasted_iota(jnp.int32, shape, dim)


def norm_rows(values):
    centre = values - jnp.mean(values, axis=0, keepdims=True)
    scaling = lax.rsqrt(jnp.mean(centre * centre, axis=0, keepdims=True) + EPS)
    return centre * scaling, scaling


def norm_back(normal, scaling, upstream):
    return scaling * (
        upstream
        - jnp.mean(upstream, axis=0, keepdims=True)
        - normal * jnp.mean(upstream * normal, axis=0, keepdims=True)
    )


def by_head(columns):
    width = CA // HEADS
    none = jnp.zeros((width, columns.shape[1]), BF16)
    return jnp.concatenate(
        [
            jnp.concatenate(
                [columns[width * h : width * (h + 1)] if g == h else none for g in range(HEADS)],
                axis=0,
            )
            for h in range(HEADS)
        ],
        axis=1,
    )


def split(values):
    high = values.astype(BF16)
    return high, (values - high.astype(F32)).astype(BF16)


def kernel(
    atom_hbm,
    single_hbm,
    band_hbm,
    counts_hbm,
    ids_hbm,
    starts_hbm,
    proj_hbm,
    pair_proj_hbm,
    attn_in_hbm,
    attn_out_hbm,
    trans_in_hbm,
    trans_out_hbm,
    agg_hbm,
    cot_hbm,
    act_out,
    grad_out,
    single_out,
    atom_ref,
    single_ref,
    band_ref,
    counts_ref,
    ids_ref,
    starts_ref,
    proj_ref,
    pair_proj_ref,
    attn_in_ref,
    attn_out_ref,
    trans_in_ref,
    trans_out_ref,
    agg_ref,
    id_buf,
    halo_buf,
    cond_buf,
    pair_buf,
    cot_buf,
    agg_buf,
    atom_buf,
    kv_side,
    kv,
    kv_wide,
    bias,
    bias_rim,
    takes,
    query_t,
    gate_t,
    out_t,
    in_t,
    down_t,
    soft,
    soft_b,
    soft_rim,
    soft_rim_own,
    q_heads,
    q_rim,
    key_t,
    normal_x,
    scale_x,
    normal_m,
    scale_m,
    gating,
    gate_back,
    silu_a,
    back_a,
    own_picks,
    edge_send,
    edge_recv,
    sums_send,
    sums_recv,
    local_sem,
    send_sem,
    recv_sem,
):
    seq = lax.axis_index("seq")
    row = lax.axis_index("row")
    col = lax.axis_index("col")
    seqs = lax.axis_size("seq")
    width = CA // HEADS

    def partner(ds, dr, dc):
        return (
            lax.rem(seq + ds + seqs, seqs),
            lax.rem(row + dr, 2),
            lax.rem(col + dc, 2),
        )

    has = {-1: seq > 0, 1: seq < seqs - 1, -2: seq > 1, 2: seq < seqs - 2}

    def toward(ds, act):
        if ds == 0:
            act()
        else:
            pl.when(has[ds])(act)

    copies = []

    def each(group, side, source, act):
        mine = [copy for copy, ds in group if ds == side]

        def run():
            for copy in mine:
                act(copy)

        if mine:
            toward(source, run)

    def send_all(wanted):
        group = []
        for src, dst, ds, dr, dc in wanted:
            place = len(copies)
            copy = pltpu.make_async_remote_copy(
                src_ref=src,
                dst_ref=dst,
                send_sem=send_sem.at[place],
                recv_sem=recv_sem.at[place],
                device_id=partner(ds, dr, dc),
                device_id_type=MESH,
            )
            copies.append((copy, ds))
            group.append((copy, ds))
        for side in (-1, 1, -2, 2, 0):
            each(group, side, side, lambda copy: copy.start())
        return group

    def arrive(group):
        for side in (0, -1, 1, -2, 2):
            each(group, side, -side, lambda copy: copy.wait_recv())

    barrier = pltpu.get_barrier_semaphore()

    def greet(side):
        for ds, dr, dc in PARTNERS:
            if ds == side:
                pl.semaphore_signal(
                    barrier, inc=1, device_id=partner(ds, dr, dc), device_id_type=MESH
                )

    for side in (-1, 1, -2, 2, 0):
        toward(side, functools.partial(greet, side))

    fetches = []

    def fetch(src, dst):
        copy = pltpu.make_async_copy(src, dst, local_sem.at[len(fetches)])
        copy.start()
        fetches.append(copy)
        return copy

    first_fetch = [fetch(single_hbm, single_ref), fetch(proj_hbm, proj_ref)]
    pair_fetch = [fetch(band_hbm, band_ref), fetch(pair_proj_hbm, pair_proj_ref)]
    id_fetch = [fetch(ids_hbm, ids_ref), fetch(starts_hbm, starts_ref)]
    atom_fetch = [fetch(atom_hbm, atom_ref)]
    weight_fetch = [
        fetch(attn_in_hbm, attn_in_ref),
        fetch(attn_out_hbm, attn_out_ref),
        fetch(trans_in_hbm, trans_in_ref),
        fetch(trans_out_hbm, trans_out_ref),
        fetch(agg_hbm, agg_ref),
        fetch(cot_hbm, cot_buf.at[1, 0]),
        fetch(counts_hbm, counts_ref),
    ]

    near, far = pl.ds(0, HALF), pl.ds(HALF, HALF)

    def close(ds):
        slot = ds + REACH
        id_buf[slot, 0:1] = jnp.full((1, ATOMS), -(2**20), jnp.int32)
        id_buf[slot, 1:2] = jnp.full((1, ATOMS), 2**20, jnp.int32)
        cond_buf[slot] = jnp.zeros(cond_buf.shape[1:], F32)
        pair_buf[slot] = jnp.zeros(pair_buf.shape[1:], BF16)
        if abs(ds) == REACH:
            halo_buf[near if ds > 0 else far] = jnp.zeros((HALF, CA), BF16)
        else:
            side = (1 - ds) // 2
            atom_buf[side] = jnp.zeros((ATOMS, CA), BF16)
            cot_buf[1 + ds] = jnp.zeros(cot_buf.shape[1:], BF16)
            for back in range(2):
                edge_recv[back, side] = jnp.zeros((CA, ATOMS), BF16)
            sums_recv[side] = jnp.zeros((TOK, ACT), BF16)

    for ds in (-2, -1, 1, 2):
        pl.when(jnp.logical_not(has[ds]))(functools.partial(close, ds))

    for copy in first_fetch:
        copy.wait()
    cond_buf[REACH, 0] = nn(single_ref[...], proj_ref[...])
    for copy in id_fetch:
        copy.wait()
    lane = iota((1, ATOMS), 1)
    own_first = jnp.zeros((1, ATOMS), jnp.int32)
    for b in range(ATOMS // QB):
        own_first = jnp.where(lane // QB == b, starts_ref[b], own_first)
    id_buf[REACH, 0:1] = ids_ref[...]
    id_buf[REACH, 1:2] = own_first
    places = sum(here.astype(jnp.int32) for here in has.values())
    pl.semaphore_wait(barrier, 3 + 4 * places)

    def outward(reach):
        group = [
            (cond_buf.at[REACH, 0], cond_buf.at[REACH - ds, dr], ds, dr, dc)
            for ds, dr, dc in COND_PARTNERS
            if abs(ds) in reach
        ]
        group += [
            (id_buf.at[REACH], id_buf.at[REACH - ds], ds, 0, 0)
            for ds in (-1, 1, -2, 2)
            if abs(ds) in reach
        ]
        if REACH in reach:
            group += [
                (atom_hbm.at[near], halo_buf.at[near], -2, 0, 0),
                (atom_hbm.at[far], halo_buf.at[far], 2, 0, 0),
            ]
        else:
            group += [(atom_hbm, atom_buf.at[(ds + 1) // 2], ds, 0, 0) for ds in SIDES]
        return send_all(group)

    def outward_pairs(reach):
        return send_all(
            [
                (
                    pair_buf.at[REACH, pair_rows, pair_lanes],
                    pair_buf.at[REACH - ds, pair_rows, pair_lanes],
                    ds,
                    dr,
                    dc,
                )
                for ds, dr, dc in PARTNERS
                if abs(ds) in reach
            ]
        )

    cond_copies = outward((0, 1))
    for copy in pair_fetch:
        copy.wait()
    place_h = (iota((LAYERS * HEADS, CA), 1) == 8 * iota((LAYERS * HEADS, CA), 0)).astype(BF16)
    pp_high, pp_rest = split(pair_proj_ref[...])
    spread_high = tn(pp_high, place_h).astype(BF16)
    spread_rest = tn(pp_rest, place_h).astype(BF16)
    band = band_ref[...].astype(F32).reshape(PAIR_ROWS * PAIR_COLS, CA)
    centre = band - jnp.mean(band, axis=1, keepdims=True)
    normal = centre * lax.rsqrt(jnp.mean(centre * centre, axis=1, keepdims=True) + EPS)
    n_high, n_rest = split(normal)
    pairs = nn(n_high, spread_high) + nn(n_high, spread_rest) + nn(n_rest, spread_high)
    tile = pairs[:PAIR_COLS]
    for i in range(1, PAIR_ROWS):
        tile = tile + pltpu.roll(pairs[PAIR_COLS * i : PAIR_COLS * (i + 1)], i, 1)
    tile = jnp.concatenate([tile, jnp.zeros((PAIR_PAD - PAIR_COLS, CA), F32)], axis=0)
    pair_rows = pl.ds(pl.multiple_of(col * PAIR_PAD, 16), PAIR_PAD)
    pair_lanes = pl.ds(pl.multiple_of(row * CA, CA), CA)
    pair_buf[REACH, pair_rows, pair_lanes] = tile.astype(BF16)

    pair_copies = outward_pairs((0, 1))
    far_copies = outward((2,)) + outward_pairs((2,))

    for copy in atom_fetch + weight_fetch:
        copy.wait()
    for n in range(LAYERS):
        query_t[n] = flip(attn_in_ref[n, :, :CA])
        gate_t[n] = flip(attn_in_ref[n, :, 3 * CA :])
        out_t[n] = flip(attn_out_ref[n])
        in_t[n] = flip(trans_in_ref[n])
        down_t[n] = flip(trans_out_ref[n])

    token_base = TOK * (seq - 1)
    atom_base = seq * ATOMS
    low = lane < HALF

    def as_cols(ids):
        return flip(jnp.broadcast_to(ids.astype(F32), (CA, ATOMS))).astype(jnp.int32)

    own_ids = ids_ref[...] - token_base
    own_id_cols = as_cols(own_ids)
    atom_t = flip(atom_ref[...]).astype(F32)

    arrive(cond_copies)
    ids_at = {ds: id_buf[REACH + ds, 0:1] - token_base for ds in (-1, 0, 1)}
    halo_ids = jnp.where(low, ids_at[1], ids_at[-1])
    halo_id_cols = as_cols(halo_ids)

    def conditioning(slots):
        cond = (cond_buf[slots, 0] + cond_buf[slots, 1]).astype(BF16).reshape(-1, CA)
        return flip(cond)

    pick_ext = (iota((SPAN, EXT), 0) == jnp.concatenate([own_ids, halo_ids], axis=1)).astype(
        F32
    ).astype(BF16)
    beside_atoms = [flip(atom_buf[side]).astype(F32) for side in range(2)]
    stream_ext = jnp.concatenate([atom_t, jnp.where(low, *beside_atoms)], axis=1) + nn(
        conditioning(slice(1, 4)), pick_ext
    )
    pick = pick_ext[:, :ATOMS]

    position = iota((EXT, ATOMS), 0)
    position = jnp.where(position < ATOMS + HALF, position, position - EXT)

    def mask_of(tile):
        first = id_buf[REACH + tile, 1:2] - atom_base - tile * ATOMS
        out = jnp.where((position >= first) & (position < first + KW), 0.0, -1e30)
        return jnp.concatenate([out] * HEADS, axis=1)

    outside = mask_of(0)

    place = iota((2 * CA, ATOMS), 0)
    head_of = (place // PAIR_ROWS) % HEADS
    token_of = PAIR_ROWS * (place // (PAIR_ROWS * HEADS)) + place % PAIR_ROWS

    def take_of(id_cols):
        lanes = iota((id_cols.shape[0], CA), 1)
        column = jnp.where(
            lanes < PAIR_PAD,
            jnp.where(lanes < PAIR_COLS, lanes, -4096),
            jnp.where(lanes < PAIR_PAD + PAIR_COLS, lanes - (PAIR_PAD - PAIR_COLS), -4096),
        )
        return jnp.concatenate(
            [
                (id_cols + (2 - s) * TOK == column).astype(F32).astype(BF16)
                for s in range(3)
            ],
            axis=1,
        )

    def table_of(n, tile):
        part = PAIR_ROWS * HEADS
        none = jnp.zeros((CA, CA), BF16)
        blocks = []
        for s in range(3):
            at = 2 * part * (s % 2)
            here = pair_buf[REACH - 1 + tile + s].astype(F32)
            halves = []
            for r in range(2):
                shift = (at + part * r - part * n) % CA
                half = here[:, CA * r : CA * (r + 1)]
                halves.append(pltpu.roll(half, shift, 1) if shift else half)
            inside = lane - at
            piece = jnp.where(
                (inside >= 0) & (inside < part),
                halves[0],
                jnp.where((inside >= part) & (inside < 2 * part), halves[1], 0.0),
            ).astype(BF16)
            piece = jnp.concatenate([piece, none[: CA - 2 * PAIR_PAD]], axis=0)
            blocks.append(jnp.concatenate([piece, none] if s < 2 else [none, piece], axis=1))
        return jnp.concatenate(blocks, axis=0)

    def bias_picks(ids):
        hit = token_of == ids
        return jnp.concatenate(
            [(hit & (head_of == h)).astype(F32).astype(BF16) for h in range(HEADS)], axis=1
        )

    def bias_of(taken, n, tile, picks):
        return nn(nn(taken, table_of(n, tile)).astype(BF16), picks)

    def right_rows(values):
        return jnp.concatenate(
            [values[HALF:ATOMS], values[ATOMS : ATOMS + HALF], values[EXT : EXT + HALF]], axis=0
        )

    def left_rows(values):
        return jnp.concatenate(
            [values[:HALF], values[ATOMS + HALF : EXT], values[EXT + HALF :]], axis=0
        )

    low_all = jnp.concatenate([low] * HEADS, axis=1)

    def attend(kv_n, heads, bias_n):
        scores = nn(kv_n[:EXT, :CA], heads) * SCALE + bias_n
        values_t = flip(kv_n[:EXT, CA:])
        exps = jnp.exp(scores - jnp.max(scores, axis=0, keepdims=True))
        weights = exps * (1.0 / jnp.sum(exps, axis=0, keepdims=True))
        rounded = weights.astype(BF16)
        attended = jnp.concatenate(
            [
                nn(
                    values_t[width * h : width * (h + 1)],
                    rounded[:, ATOMS * h : ATOMS * (h + 1)],
                )
                for h in range(HEADS)
            ],
            axis=0,
        )
        return attended, weights, rounded

    def attend_own(n, kv_n, heads):
        attended, weights, rounded = attend(kv_n, heads, bias[n])
        soft[n] = weights
        soft_b[n] = rounded
        key_t[n] = flip(kv_n[:EXT, :CA])
        return attended

    def attend_rim(n, kv_n, heads):
        right_kv = right_rows(kv_n)
        left_kv = left_rows(kv_n)
        scores = jnp.where(
            low_all, nn(right_kv[:, :CA], heads), nn(left_kv[:, :CA], heads)
        )
        scores = scores * SCALE + bias_rim[...]
        most = jnp.maximum(jnp.max(scores, axis=0, keepdims=True), -1e29)
        exps = jnp.exp(scores - most)
        weights = exps * (1.0 / jnp.maximum(jnp.sum(exps, axis=0, keepdims=True), 1e-30))
        soft_rim[...] = weights
        rounded = weights.astype(BF16)
        near = weights[:HALF]
        soft_rim_own[:HALF] = jnp.where(low_all, 0.0, near).astype(BF16)
        soft_rim_own[HALF:] = jnp.where(low_all, near, 0.0).astype(BF16)
        right_t = flip(right_kv[:, CA:])
        left_t = flip(left_kv[:, CA:])
        parts = []
        for h in range(HEADS):
            here = rounded[:, ATOMS * h : ATOMS * (h + 1)]
            parts.append(
                jnp.where(
                    low,
                    nn(right_t[width * h : width * (h + 1)], here),
                    nn(left_t[width * h : width * (h + 1)], here),
                )
            )
        return jnp.concatenate(parts, axis=0)

    def transition(n, stream, gates, attended, lanes):
        gated = gates * attended
        x_mid = stream + nn(out_t[n], gated.astype(BF16))
        normal, scaling = norm_rows(x_mid)
        widened = nn(in_t[n], normal.astype(BF16))
        part_a = widened[:FFA]
        part_b = widened[FFA:]
        sig = jax.nn.sigmoid(part_a)
        act = part_a * sig
        if lanes:
            gating[n, :, :lanes] = gates
            gate_back[n] = gated[:, :ATOMS] * (1.0 - gates[:, :ATOMS])
            normal_m[n, :, :lanes] = normal
            scale_m[n, :, :lanes] = scaling
            silu_a[n, :, :lanes] = act
            back_a[n, :, :lanes] = part_b * (sig * (1.0 + part_a * (1.0 - sig)))
        return x_mid + nn(down_t[n], (act * part_b).astype(BF16))

    def local_layer(n, stream_ext):
        normal_ext, scale_ext = norm_rows(stream_ext)
        normal_x[n] = normal_ext
        scale_x[n] = scale_ext
        rows_ext = flip(normal_ext.astype(BF16))
        kv[n // 2] = nn(rows_ext, attn_in_ref[n, :, CA : 3 * CA]).astype(BF16)
        normed = normal_ext[:, :ATOMS].astype(BF16)
        heads = by_head(nn(query_t[n], normed).astype(BF16))
        q_heads[n] = flip(heads)
        gates = jax.nn.sigmoid(nn(gate_t[n], normed))
        if n == 0:
            own_picks[...] = bias_picks(own_ids)
            takes[:EXT] = take_of(jnp.concatenate([own_id_cols, halo_id_cols], axis=0))
            arrive(pair_copies)
            bias[0] = bias_of(takes[:EXT], 0, 0, own_picks[...]) + outside
        attended = attend_own(n, kv[n // 2], heads)
        return transition(n, stream_ext[:, :ATOMS], gates, attended, ATOMS)

    stream = local_layer(0, stream_ext)
    late_copies = send_all(
        [(cot_hbm, cot_buf.at[1 - ds, dr], ds, dr, dc) for ds, dr, dc in COND_PARTNERS if abs(ds) < REACH]
        + [(agg_hbm, agg_buf, 0, 1, 0)]
    )


    normal, scaling = norm_rows(stream)
    normal_x[1, :, :ATOMS] = normal
    scale_x[1, :, :ATOMS] = scaling
    normed = normal.astype(BF16)
    rows_own = flip(normed)
    kv_wide[:ATOMS] = nn(rows_own, attn_in_ref[1, :, CA : 3 * CA]).astype(BF16)
    own_heads = by_head(nn(query_t[1], normed).astype(BF16))
    q_heads[1] = flip(own_heads)
    own_gates = jax.nn.sigmoid(nn(gate_t[1], normed))
    outer_ids = pltpu.roll(jnp.where(low, ids_at[-1], ids_at[1]), HALF, 1)
    takes[EXT:] = take_of(as_cols(outer_ids))
    mixed = nn(takes[...], table_of(1, 0)).astype(BF16)
    bias[1] = nn(mixed[:EXT], own_picks[...]) + outside
    rim_full = nn(mixed, bias_picks(halo_ids))
    rim_rows = iota((3 * HALF, ATOMS), 0)
    left_position = jnp.where(
        rim_rows < HALF,
        rim_rows,
        jnp.where(rim_rows < ATOMS, rim_rows - ATOMS, rim_rows - EXT),
    )
    rim_position = jnp.where(low, HALF + rim_rows, left_position)
    rim_first = jnp.where(low, id_buf[REACH + 1, 1:2], id_buf[REACH - 1, 1:2]) - atom_base
    rim_outside = jnp.where(
        (rim_position >= rim_first) & (rim_position < rim_first + KW), 0.0, -1e30
    )
    bias_rim[...] = jnp.where(low_all, right_rows(rim_full), left_rows(rim_full)) + jnp.concatenate(
        [rim_outside] * HEADS, axis=1
    )
    bias[2] = bias_of(takes[:EXT], 2, 0, own_picks[...]) + outside
    at_token = jnp.concatenate([own_id_cols, halo_id_cols], axis=0) == iota((EXT, CA), 1)
    pick_t = at_token[:ATOMS].astype(F32).astype(BF16)[:, :SPAN]
    token_atoms = jnp.sum(at_token.astype(F32), axis=0, keepdims=True)
    atom_counts = jnp.sum(jnp.where(at_token[:ATOMS], token_atoms, 0.0), axis=1, keepdims=True)
    inverse = 1.0 / jnp.maximum(atom_counts, 1.0)

    arrive(far_copies)
    ids_at.update({ds: id_buf[REACH + ds, 0:1] - token_base for ds in (-2, 2)})
    side_ids = jnp.concatenate(
        [ids_at[1], ids_at[-1], jnp.where(low, ids_at[2], ids_at[-2])], axis=1
    )
    pick_side = (iota((SLOTS * TOK, 3 * ATOMS), 0) - TOK == side_ids).astype(F32).astype(BF16)
    stream_side = jnp.concatenate(beside_atoms + [flip(halo_buf[...]).astype(F32)], axis=1) + nn(
        conditioning(slice(0, SLOTS)), pick_side
    )
    normal_side, _ = norm_rows(stream_side)
    normed_side = normal_side.astype(BF16)
    rows_side = flip(normed_side)
    kv_side[...] = nn(rows_side, attn_in_ref[0, :, CA : 3 * CA]).astype(BF16)
    queries = nn(query_t[0], normed_side[:, :EXT]).astype(BF16)
    gates = jax.nn.sigmoid(nn(gate_t[0], normed_side[:, :EXT]))
    kv_of = {
        1: [kv_side[:ATOMS], kv_side[EXT : EXT + HALF], kv[0, HALF:ATOMS]],
        -1: [kv_side[ATOMS:EXT], kv[0, :HALF], kv_side[EXT + HALF :]],
    }
    attended = []
    for place, tile in enumerate((1, -1)):
        here = ids_at[tile] - TOK * tile
        there = jnp.where(low, ids_at[tile + 1], ids_at[tile - 1]) - TOK * tile
        taken = take_of(jnp.concatenate([as_cols(here), as_cols(there)], axis=0))
        bias_here = bias_of(taken, 0, tile, bias_picks(here)) + mask_of(tile)
        attended.append(
            attend(
                jnp.concatenate(kv_of[tile], axis=0),
                by_head(queries[:, ATOMS * place : ATOMS * (place + 1)]),
                bias_here,
            )[0]
        )
    stream_side = transition(
        0, stream_side[:, :EXT], gates, jnp.concatenate(attended, axis=1), 0
    )

    rows_side = flip(norm_rows(stream_side)[0].astype(BF16))
    rows_right, rows_left = rows_side[:ATOMS], rows_side[ATOMS:]
    rows_side = jnp.concatenate(
        [rows_right[:HALF], rows_left[HALF:], rows_right[HALF:], rows_left[:HALF]], axis=0
    )
    kv_wide[ATOMS:] = nn(rows_side, attn_in_ref[1, :, CA : 3 * CA]).astype(BF16)
    rim_heads = by_head(nt(query_t[1], rows_side[:ATOMS]).astype(BF16))
    q_rim[...] = flip(rim_heads)
    gates = jnp.concatenate(
        [own_gates, jax.nn.sigmoid(nt(gate_t[1], rows_side[:ATOMS]))], axis=1
    )
    attended = jnp.concatenate([attend_own(1, kv_wide, own_heads), attend_rim(1, kv_wide, rim_heads)], axis=1)
    stream_ext = jnp.concatenate(
        [stream, jnp.where(low, stream_side[:, :ATOMS], stream_side[:, ATOMS:])], axis=1
    )
    stream_ext = transition(1, stream_ext, gates, attended, EXT)

    stream = local_layer(2, stream_ext)

    final = flip(stream.astype(BF16))
    arrive(late_copies)
    gradient = None
    for part in range(2):
        weights = agg_ref[...] if part == 0 else agg_buf[...]
        pre = nn(final, weights)
        sig = jax.nn.sigmoid(pre)
        d_act = nn(pick_t, cot_buf[:, part].reshape(SPAN, ACT)) * inverse
        d_pre = (d_act * (sig * (1.0 + pre * (1.0 - sig)))).astype(BF16)
        term = nt(weights, d_pre)
        gradient = term if part == 0 else gradient + term
        if part == 0:
            high, rest = split(pre * sig)
            sums = nn(pick, high) + nn(pick, rest)
            sums_send[0] = sums[:TOK].astype(BF16)
            sums_send[1] = sums[2 * TOK :].astype(BF16)
            own_sums = sums[TOK : 2 * TOK]
            sums_copies = send_all(
                [
                    (sums_send.at[(ds + 1) // 2], sums_recv.at[(ds + 1) // 2], ds, 0, 0)
                    for ds in SIDES
                ]
            )

    def d_middle(n, upstream, lanes):
        d_transit = nn(trans_out_ref[n], upstream.astype(BF16))
        d_wide = jnp.concatenate(
            [
                (d_transit * back_a[n, :, :lanes]).astype(BF16),
                (d_transit * silu_a[n, :, :lanes]).astype(BF16),
            ],
            axis=0,
        )
        d_mid = upstream + norm_back(
            normal_m[n, :, :lanes], scale_m[n, :, :lanes], nn(trans_in_ref[n], d_wide)
        )
        return d_mid, nn(attn_out_ref[n], d_mid.astype(BF16))

    def d_own(n, kv_n, d_heads, d_att):
        own_d = nn(kv_n[:ATOMS, CA:], d_heads)
        halo_d = nn(kv_n[ATOMS:EXT, CA:], d_heads)
        own_prod = soft[n, :ATOMS] * own_d
        halo_prod = soft[n, ATOMS:] * halo_d
        inner = jnp.sum(own_prod, axis=0, keepdims=True) + jnp.sum(
            halo_prod, axis=0, keepdims=True
        )
        halo_ds = ((halo_prod - soft[n, ATOMS:] * inner) * SCALE).astype(BF16)
        own_ds = ((own_prod - soft[n, :ATOMS] * inner) * SCALE).astype(BF16)
        d_queries = jnp.concatenate(
            [
                nn(
                    key_t[n, width * h : width * (h + 1), :ATOMS],
                    own_ds[:, ATOMS * h : ATOMS * (h + 1)],
                )
                + nn(
                    key_t[n, width * h : width * (h + 1), ATOMS:],
                    halo_ds[:, ATOMS * h : ATOMS * (h + 1)],
                )
                for h in range(HEADS)
            ],
            axis=0,
        ).astype(BF16)
        return d_queries, nn(own_ds, q_heads[n]), nn(soft_b[n, :ATOMS], d_att), halo_ds

    def weigh_kv(n, d_keys, d_vals):
        return nt(attn_in_ref[n, :, CA : 2 * CA], d_keys) + nt(
            attn_in_ref[n, :, 2 * CA : 3 * CA], d_vals
        )

    def local_back(n, upstream):
        slot = n // 2
        d_mid, d_gated = d_middle(n, upstream, ATOMS)
        d_heads = by_head((d_gated * gating[n, :, :ATOMS]).astype(BF16))
        d_att = flip(d_heads)
        d_gate = (d_gated * gate_back[n]).astype(BF16)
        d_queries, d_keys, d_vals, halo_ds = d_own(n, kv[slot], d_heads, d_att)
        beside = norm_back(
            normal_x[n, :, ATOMS:],
            scale_x[n, :, ATOMS:],
            weigh_kv(
                n,
                nn(halo_ds, q_heads[n]).astype(BF16),
                nn(soft_b[n, ATOMS:], d_att).astype(BF16),
            ),
        )
        d_normed = (
            nn(attn_in_ref[n, :, :CA], d_queries)
            + nn(attn_in_ref[n, :, 3 * CA :], d_gate)
            + weigh_kv(n, d_keys.astype(BF16), d_vals.astype(BF16))
        )
        part = d_mid + norm_back(normal_x[n, :, :ATOMS], scale_x[n, :, :ATOMS], d_normed)
        edge_send[slot, 0] = jnp.where(low, part, beside).astype(BF16)
        edge_send[slot, 1] = jnp.where(low, beside, part).astype(BF16)
        arrive(
            send_all(
                [
                    (edge_send.at[slot, side], edge_recv.at[slot, side], ds, 0, 0)
                    for side, ds in enumerate(SIDES)
                ]
            )
        )
        from_right, from_left = edge_recv[slot, 0].astype(F32), edge_recv[slot, 1].astype(F32)
        return jnp.concatenate(
            [
                part + jnp.where(low, from_left, from_right),
                beside + jnp.where(low, from_right, from_left),
            ],
            axis=1,
        )

    gradient = local_back(2, gradient)

    d_mid, d_gated = d_middle(1, gradient, EXT)
    d_att_t = (d_gated * gating[1]).astype(BF16)
    d_heads = by_head(d_att_t[:, :ATOMS])
    d_att = flip(d_heads)
    d_heads_rim = by_head(d_att_t[:, ATOMS:])
    d_att_rim = flip(d_heads_rim)
    d_gate = (d_gated[:, :ATOMS] * gate_back[1]).astype(BF16)
    d_queries, d_keys, d_vals, _ = d_own(1, kv_wide, d_heads, d_att)
    rim_d = jnp.where(
        low_all,
        nn(right_rows(kv_wide[:, CA:]), d_heads_rim),
        nn(left_rows(kv_wide[:, CA:]), d_heads_rim),
    )
    rim_prod = soft_rim[...] * rim_d
    rim_inner = jnp.sum(rim_prod, axis=0, keepdims=True)
    rim_ds = (rim_prod[:HALF] - soft_rim[:HALF] * rim_inner) * SCALE
    rim_ds = jnp.concatenate(
        [jnp.where(low_all, 0.0, rim_ds), jnp.where(low_all, rim_ds, 0.0)], axis=0
    ).astype(BF16)
    d_keys = d_keys + nn(rim_ds, q_rim[...])
    d_vals = d_vals + nn(soft_rim_own[...], d_att_rim)
    d_normed = (
        nn(attn_in_ref[1, :, :CA], d_queries)
        + nn(attn_in_ref[1, :, 3 * CA :], d_gate)
        + weigh_kv(1, d_keys.astype(BF16), d_vals.astype(BF16))
    )
    gradient = d_mid[:, :ATOMS] + norm_back(
        normal_x[1, :, :ATOMS], scale_x[1, :, :ATOMS], d_normed
    )

    def per_token(picks, values):
        high, rest = split(values)
        return nt(picks, high) + nt(picks, rest)

    arrive(sums_copies)
    token_sums = own_sums + (sums_recv[0].astype(F32) + sums_recv[1].astype(F32))
    diagonal = iota((TOK, TOK), 0) == iota((TOK, TOK), 1)
    counts = jnp.sum(
        jnp.where(diagonal, counts_ref[...].astype(F32), 0.0), axis=1, keepdims=True
    )
    act_out[...] = (token_sums / counts).astype(BF16)
    gradient = local_back(0, gradient)
    grad_out[...] = flip(gradient[:, :ATOMS].astype(BF16))
    d_cond = per_token(pick_ext[TOK : 2 * TOK], gradient)
    high, rest = split(d_cond)
    single_out[...] = (nt(high, proj_ref[...]) + nt(rest, proj_ref[...])).astype(BF16)
    for side in (0, -1, 1, -2, 2):
        each(copies, side, side, lambda copy: copy.wait_send())


N_COPIES = 9 + 4 + 4 + 19 + 5 + 1 + 2 + 2 + 2


def hand_on(act, grad, single, act_out, grad_out, single_out):
    act_out[...] = act[...]
    grad_out[...] = grad[...]
    single_out[...] = single[...]


def local(
    atom_single,
    token_single,
    pair_band,
    token_counts,
    atom_token,
    window_starts,
    single_proj,
    pair_proj,
    attn_in,
    attn_out,
    trans_in,
    trans_out,
    agg_proj,
    token_cot,
):
    vmem = pl.BlockSpec(memory_space=pltpu.VMEM)
    hbm = pl.BlockSpec(memory_space=pltpu.HBM)

    def scratch(dtype, *shape):
        return pltpu.VMEM(shape, dtype)

    results = (
        jax.ShapeDtypeStruct((TOK, ACT), BF16),
        jax.ShapeDtypeStruct((ATOMS, CA), BF16),
        jax.ShapeDtypeStruct((TOK, COND), BF16),
    )
    results_here = pl.pallas_call(
        kernel,
        out_shape=results,
        in_specs=[hbm] * 14,
        out_specs=(vmem, vmem, vmem),
        scratch_shapes=[
            scratch(BF16, ATOMS, CA),
            scratch(BF16, TOK, COND),
            scratch(BF16, PAIR_ROWS, PAIR_COLS, CA),
            scratch(jnp.int32, 1, TOK),
            scratch(jnp.int32, 1, ATOMS),
            pltpu.SMEM((ATOMS // QB,), jnp.int32),
            scratch(BF16, COND, CA),
            scratch(F32, LAYERS * HEADS, CA),
            scratch(BF16, LAYERS, CA, 4 * CA),
            scratch(BF16, LAYERS, CA, CA),
            scratch(BF16, LAYERS, CA, 2 * FFA),
            scratch(BF16, LAYERS, FFA, CA),
            scratch(BF16, CA, ACT),
            scratch(jnp.int32, SLOTS, 2, ATOMS),
            scratch(BF16, ATOMS, CA),
            scratch(F32, SLOTS, 2, TOK, CA),
            scratch(BF16, SLOTS, 2 * PAIR_PAD, 2 * CA),
            scratch(BF16, 3, 2, TOK, ACT),
            scratch(BF16, CA, ACT),
            scratch(BF16, 2, ATOMS, CA),
            scratch(BF16, 3 * ATOMS, 2 * CA),
            scratch(BF16, 2, EXT, 2 * CA),
            scratch(BF16, 3 * ATOMS, 2 * CA),
            scratch(F32, LAYERS, EXT, ALL),
            scratch(F32, 3 * HALF, ALL),
            scratch(BF16, 3 * ATOMS, 3 * CA),
            scratch(BF16, LAYERS, CA, CA),
            scratch(BF16, LAYERS, CA, CA),
            scratch(BF16, LAYERS, CA, CA),
            scratch(BF16, LAYERS, 2 * FFA, CA),
            scratch(BF16, LAYERS, CA, FFA),
            scratch(F32, LAYERS, EXT, ALL),
            scratch(BF16, LAYERS, EXT, ALL),
            scratch(F32, 3 * HALF, ALL),
            scratch(BF16, ATOMS, ALL),
            scratch(BF16, LAYERS, ALL, CA),
            scratch(BF16, ALL, CA),
            scratch(BF16, LAYERS, CA, EXT),
            scratch(F32, LAYERS, CA, EXT),
            scratch(F32, LAYERS, 1, EXT),
            scratch(F32, LAYERS, CA, EXT),
            scratch(F32, LAYERS, 1, EXT),
            scratch(F32, LAYERS, CA, EXT),
            scratch(F32, LAYERS, CA, ATOMS),
            scratch(F32, LAYERS, FFA, EXT),
            scratch(F32, LAYERS, FFA, EXT),
            scratch(BF16, 2 * CA, ALL),
            scratch(BF16, 2, 2, CA, ATOMS),
            scratch(BF16, 2, 2, CA, ATOMS),
            scratch(BF16, 2, TOK, ACT),
            scratch(BF16, 2, TOK, ACT),
            pltpu.SemaphoreType.DMA((14,)),
            pltpu.SemaphoreType.DMA((N_COPIES,)),
            pltpu.SemaphoreType.DMA((N_COPIES,)),
        ],
        compiler_params=pltpu.CompilerParams(
            collective_id=0, has_side_effects=True, vmem_limit_bytes=64 * 1024 * 1024
        ),
        cost_estimate=pl.CostEstimate(
            flops=2_000_000_000, bytes_accessed=2_000_000, transcendentals=1_000_000
        ),
        name="atoms",
    )(
        atom_single,
        token_single,
        pair_band,
        token_counts.reshape(1, TOK),
        atom_token.reshape(1, ATOMS),
        window_starts,
        single_proj,
        pair_proj.T,
        attn_in,
        attn_out,
        trans_in,
        trans_out,
        agg_proj,
        token_cot,
    )
    return pl.pallas_call(
        hand_on,
        out_shape=results,
        in_specs=[vmem] * 3,
        out_specs=(vmem,) * 3,
        name="results",
    )(*results_here)


def solution(mesh):
    return jax.shard_map(
        local,
        mesh=mesh,
        in_specs=(
            P("seq", None),
            P("seq", "row"),
            P(("seq", "row"), "col", None),
            P("seq"),
            P("seq"),
            P("seq"),
            P("row", None),
            P(),
            P(),
            P(),
            P(),
            P(),
            P(None, "row"),
            P("seq", "row"),
        ),
        out_specs=(P("seq", "row"), P("seq", None), P("seq", "row")),
        check_vma=False,
    )
```

```python
import functools

import jax
import jax.numpy as jnp
from jax import lax
from jax.experimental import pallas as pl
from jax.experimental.pallas import tpu as pltpu
from jax.sharding import PartitionSpec as P

HEADS = 4
QB = 32
KW = 128
LAYERS = 3
ATOMS = 128
CA = 128
TOK = 16
COND = 192
ACT = 384
FFA = 256
PAIR_ROWS = 8
PAIR_COLS = 40
PAIR_PAD = 48
SPAN = 3 * TOK
HALF = 64
EXT = 256
ALL = HEADS * ATOMS
F32 = jnp.float32
BF16 = jnp.bfloat16
EPS = 1e-05
SCALE = (CA // HEADS) ** (-0.5)
MESH = pl.DeviceIdType.MESH

PARTNERS = [
    (ds, dr, dc)
    for ds in (0, -1, 1, -2, 2)
    for dr in (0, 1)
    for dc in (0, 1)
    if (ds, dr, dc) != (0, 0, 0)
]
COND_PARTNERS = [p for p in PARTNERS if p[2] == 0]
SIDES = (-1, 1)
REACH = 2
SLOTS = 2 * REACH + 1


def nn(a, b):
    return lax.dot_general(a, b, (((1,), (0,)), ((), ())), preferred_element_type=F32)


def nt(a, b):
    return lax.dot_general(a, b, (((1,), (1,)), ((), ())), preferred_element_type=F32)


def tn(a, b):
    return lax.dot_general(a, b, (((0,), (0,)), ((), ())), preferred_element_type=F32)


def flip(values):
    return jnp.transpose(values, (1, 0))


def iota(shape, dim):
    return lax.broadcasted_iota(jnp.int32, shape, dim)


def norm_rows(values):
    centre = values - jnp.mean(values, axis=0, keepdims=True)
    scaling = lax.rsqrt(jnp.mean(centre * centre, axis=0, keepdims=True) + EPS)
    return centre * scaling, scaling


def norm_back(normal, scaling, upstream):
    return scaling * (
        upstream
        - jnp.mean(upstream, axis=0, keepdims=True)
        - normal * jnp.mean(upstream * normal, axis=0, keepdims=True)
    )


def by_head(columns):
    width = CA // HEADS
    none = jnp.zeros((width, columns.shape[1]), BF16)
    return jnp.concatenate(
        [
            jnp.concatenate(
                [columns[width * h : width * (h + 1)] if g == h else none for g in range(HEADS)],
                axis=0,
            )
            for h in range(HEADS)
        ],
        axis=1,
    )


def split(values):
    high = values.astype(BF16)
    return high, (values - high.astype(F32)).astype(BF16)


def kernel(
    atom_hbm,
    single_hbm,
    band_hbm,
    counts_hbm,
    ids_hbm,
    starts_hbm,
    proj_hbm,
    pair_proj_hbm,
    attn_in_hbm,
    attn_out_hbm,
    trans_in_hbm,
    trans_out_hbm,
    agg_hbm,
    cot_hbm,
    act_out,
    grad_out,
    single_out,
    atom_ref,
    single_ref,
    band_ref,
    counts_ref,
    ids_ref,
    starts_ref,
    proj_ref,
    pair_proj_ref,
    attn_in_ref,
    attn_out_ref,
    trans_in_ref,
    trans_out_ref,
    agg_ref,
    id_buf,
    halo_buf,
    cond_buf,
    pair_buf,
    cot_buf,
    agg_buf,
    atom_buf,
    kv_side,
    kv,
    kv_wide,
    bias,
    bias_rim,
    takes,
    query_t,
    gate_t,
    out_t,
    in_t,
    down_t,
    soft,
    soft_b,
    soft_rim,
    soft_rim_own,
    q_heads,
    q_rim,
    key_t,
    normal_x,
    scale_x,
    normal_m,
    scale_m,
    gating,
    gate_back,
    silu_a,
    back_a,
    own_picks,
    edge_send,
    edge_recv,
    sums_send,
    sums_recv,
    local_sem,
    relay_sem,
    send_sem,
    recv_sem,
):
    seq = lax.axis_index("seq")
    row = lax.axis_index("row")
    col = lax.axis_index("col")
    seqs = lax.axis_size("seq")
    width = CA // HEADS

    def partner(ds, dr, dc):
        return (
            lax.rem(seq + ds + seqs, seqs),
            lax.rem(row + dr, 2),
            lax.rem(col + dc, 2),
        )

    has = {-1: seq > 0, 1: seq < seqs - 1, -2: seq > 1, 2: seq < seqs - 2}

    def toward(ds, act):
        if ds == 0:
            act()
        else:
            pl.when(has[ds])(act)

    copies = []

    def each(group, side, source, act):
        mine = [copy for copy, ds in group if ds == side]

        def run():
            for copy in mine:
                act(copy)

        if mine:
            toward(source, run)

    def send_all(wanted):
        group = []
        for src, dst, ds, dr, dc in wanted:
            place = len(copies)
            copy = pltpu.make_async_remote_copy(
                src_ref=src,
                dst_ref=dst,
                send_sem=send_sem.at[place],
                recv_sem=recv_sem.at[place],
                device_id=partner(ds, dr, dc),
                device_id_type=MESH,
            )
            copies.append((copy, ds))
            group.append((copy, ds))
        for side in (-1, 1, -2, 2, 0):
            each(group, side, side, lambda copy: copy.start())
        return group

    def arrive(group):
        for side in (0, -1, 1, -2, 2):
            each(group, side, -side, lambda copy: copy.wait_recv())

    barrier = pltpu.get_barrier_semaphore()

    def greet(side):
        for ds, dr, dc in PARTNERS:
            if ds == side:
                pl.semaphore_signal(
                    barrier, inc=1, device_id=partner(ds, dr, dc), device_id_type=MESH
                )

    for side in (-1, 1, 0):
        toward(side, functools.partial(greet, side))

    fetches = []

    def fetch(src, dst):
        copy = pltpu.make_async_copy(src, dst, local_sem.at[len(fetches)])
        copy.start()
        fetches.append(copy)
        return copy

    first_fetch = [fetch(single_hbm, single_ref), fetch(proj_hbm, proj_ref)]
    pair_fetch = [fetch(band_hbm, band_ref), fetch(pair_proj_hbm, pair_proj_ref)]
    id_fetch = [fetch(ids_hbm, ids_ref), fetch(starts_hbm, starts_ref)]
    atom_fetch = [fetch(atom_hbm, atom_ref)]
    weight_fetch = [
        fetch(attn_in_hbm, attn_in_ref),
        fetch(attn_out_hbm, attn_out_ref),
        fetch(trans_in_hbm, trans_in_ref),
        fetch(trans_out_hbm, trans_out_ref),
        fetch(agg_hbm, agg_ref),
        fetch(cot_hbm, cot_buf.at[1, 0]),
        fetch(counts_hbm, counts_ref),
    ]

    near, far = pl.ds(0, HALF), pl.ds(HALF, HALF)

    def close(ds):
        slot = ds + REACH
        id_buf[slot, 0:1] = jnp.full((1, ATOMS), -(2**20), jnp.int32)
        id_buf[slot, 1:2] = jnp.full((1, ATOMS), 2**20, jnp.int32)
        cond_buf[slot] = jnp.zeros(cond_buf.shape[1:], F32)
        pair_buf[slot] = jnp.zeros(pair_buf.shape[1:], BF16)
        if abs(ds) == REACH:
            halo_buf[near if ds > 0 else far] = jnp.zeros((HALF, CA), BF16)
        else:
            side = (1 - ds) // 2
            atom_buf[side] = jnp.zeros((ATOMS, CA), BF16)
            cot_buf[1 + ds] = jnp.zeros(cot_buf.shape[1:], BF16)
            for back in range(2):
                edge_recv[back, side] = jnp.zeros((CA, ATOMS), BF16)
            sums_recv[side] = jnp.zeros((TOK, ACT), BF16)

    for ds in (-2, -1, 1, 2):
        pl.when(jnp.logical_not(has[ds]))(functools.partial(close, ds))

    for copy in first_fetch:
        copy.wait()
    cond_buf[REACH, 0] = nn(single_ref[...], proj_ref[...])
    for copy in id_fetch:
        copy.wait()
    lane = iota((1, ATOMS), 1)
    own_first = jnp.zeros((1, ATOMS), jnp.int32)
    for b in range(ATOMS // QB):
        own_first = jnp.where(lane // QB == b, starts_ref[b], own_first)
    id_buf[REACH, 0:1] = ids_ref[...]
    id_buf[REACH, 1:2] = own_first
    places = has[-1].astype(jnp.int32) + has[1].astype(jnp.int32)
    pl.semaphore_wait(barrier, 3 + 4 * places)

    def tell():
        for ds in SIDES:
            pl.semaphore_signal(
                relay_sem.at[(ds + 1) // 2],
                inc=1,
                device_id=partner(ds, 0, 0),
                device_id_type=MESH,
            )

    pl.when(jnp.logical_and(has[-1], has[1]))(tell)

    def outward(reach):
        group = [
            (cond_buf.at[REACH, 0], cond_buf.at[REACH - ds, dr], ds, dr, dc)
            for ds, dr, dc in COND_PARTNERS
            if abs(ds) in reach
        ]
        group += [
            (id_buf.at[REACH], id_buf.at[REACH - ds], ds, 0, 0)
            for ds in (-1, 1, -2, 2)
            if abs(ds) in reach
        ]
        if REACH in reach:
            group += [
                (atom_hbm.at[near], halo_buf.at[near], -2, 0, 0),
                (atom_hbm.at[far], halo_buf.at[far], 2, 0, 0),
            ]
        else:
            group += [(atom_hbm, atom_buf.at[(ds + 1) // 2], ds, 0, 0) for ds in SIDES]
        return send_all(group)

    def outward_pairs(reach):
        return send_all(
            [
                (
                    pair_buf.at[REACH, pair_rows, pair_lanes],
                    pair_buf.at[REACH - ds, pair_rows, pair_lanes],
                    ds,
                    dr,
                    dc,
                )
                for ds, dr, dc in PARTNERS
                if abs(ds) in reach
            ]
        )

    cond_copies = outward((0, 1))
    for copy in pair_fetch:
        copy.wait()
    place_h = (iota((LAYERS * HEADS, CA), 1) == 8 * iota((LAYERS * HEADS, CA), 0)).astype(BF16)
    pp_high, pp_rest = split(pair_proj_ref[...])
    spread_high = tn(pp_high, place_h).astype(BF16)
    spread_rest = tn(pp_rest, place_h).astype(BF16)
    band = band_ref[...].astype(F32).reshape(PAIR_ROWS * PAIR_COLS, CA)
    centre = band - jnp.mean(band, axis=1, keepdims=True)
    normal = centre * lax.rsqrt(jnp.mean(centre * centre, axis=1, keepdims=True) + EPS)
    n_high, n_rest = split(normal)
    pairs = nn(n_high, spread_high) + nn(n_high, spread_rest) + nn(n_rest, spread_high)
    tile = pairs[:PAIR_COLS]
    for i in range(1, PAIR_ROWS):
        tile = tile + pltpu.roll(pairs[PAIR_COLS * i : PAIR_COLS * (i + 1)], i, 1)
    tile = jnp.concatenate([tile, jnp.zeros((PAIR_PAD - PAIR_COLS, CA), F32)], axis=0)
    pair_rows = pl.ds(pl.multiple_of(col * PAIR_PAD, 16), PAIR_PAD)
    pair_lanes = pl.ds(pl.multiple_of(row * CA, CA), CA)
    pair_buf[REACH, pair_rows, pair_lanes] = tile.astype(BF16)

    pair_copies = outward_pairs((0, 1))
    for ds in (-2, 2):
        toward(ds, functools.partial(pl.semaphore_wait, relay_sem.at[(2 - ds) // 4], 1))
    far_copies = outward((2,)) + outward_pairs((2,))

    for copy in atom_fetch + weight_fetch:
        copy.wait()
    for n in range(LAYERS):
        query_t[n] = flip(attn_in_ref[n, :, :CA])
        gate_t[n] = flip(attn_in_ref[n, :, 3 * CA :])
        out_t[n] = flip(attn_out_ref[n])
        in_t[n] = flip(trans_in_ref[n])
        down_t[n] = flip(trans_out_ref[n])

    token_base = TOK * (seq - 1)
    atom_base = seq * ATOMS
    low = lane < HALF

    def as_cols(ids):
        return flip(jnp.broadcast_to(ids.astype(F32), (CA, ATOMS))).astype(jnp.int32)

    own_ids = ids_ref[...] - token_base
    own_id_cols = as_cols(own_ids)
    atom_t = flip(atom_ref[...]).astype(F32)

    arrive(cond_copies)
    ids_at = {ds: id_buf[REACH + ds, 0:1] - token_base for ds in (-1, 0, 1)}
    halo_ids = jnp.where(low, ids_at[1], ids_at[-1])
    halo_id_cols = as_cols(halo_ids)

    def conditioning(slots):
        cond = (cond_buf[slots, 0] + cond_buf[slots, 1]).astype(BF16).reshape(-1, CA)
        return flip(cond)

    pick_ext = (iota((SPAN, EXT), 0) == jnp.concatenate([own_ids, halo_ids], axis=1)).astype(
        F32
    ).astype(BF16)
    beside_atoms = [flip(atom_buf[side]).astype(F32) for side in range(2)]
    stream_ext = jnp.concatenate([atom_t, jnp.where(low, *beside_atoms)], axis=1) + nn(
        conditioning(slice(1, 4)), pick_ext
    )
    pick = pick_ext[:, :ATOMS]

    position = iota((EXT, ATOMS), 0)
    position = jnp.where(position < ATOMS + HALF, position, position - EXT)

    def mask_of(tile):
        first = id_buf[REACH + tile, 1:2] - atom_base - tile * ATOMS
        out = jnp.where((position >= first) & (position < first + KW), 0.0, -1e30)
        return jnp.concatenate([out] * HEADS, axis=1)

    outside = mask_of(0)

    place = iota((2 * CA, ATOMS), 0)
    head_of = (place // PAIR_ROWS) % HEADS
    token_of = PAIR_ROWS * (place // (PAIR_ROWS * HEADS)) + place % PAIR_ROWS

    def take_of(id_cols):
        lanes = iota((id_cols.shape[0], CA), 1)
        column = jnp.where(
            lanes < PAIR_PAD,
            jnp.where(lanes < PAIR_COLS, lanes, -4096),
            jnp.where(lanes < PAIR_PAD + PAIR_COLS, lanes - (PAIR_PAD - PAIR_COLS), -4096),
        )
        return jnp.concatenate(
            [
                (id_cols + (2 - s) * TOK == column).astype(F32).astype(BF16)
                for s in range(3)
            ],
            axis=1,
        )

    def table_of(n, tile):
        part = PAIR_ROWS * HEADS
        none = jnp.zeros((CA, CA), BF16)
        blocks = []
        for s in range(3):
            at = 2 * part * (s % 2)
            here = pair_buf[REACH - 1 + tile + s].astype(F32)
            halves = []
            for r in range(2):
                shift = (at + part * r - part * n) % CA
                half = here[:, CA * r : CA * (r + 1)]
                halves.append(pltpu.roll(half, shift, 1) if shift else half)
            inside = lane - at
            piece = jnp.where(
                (inside >= 0) & (inside < part),
                halves[0],
                jnp.where((inside >= part) & (inside < 2 * part), halves[1], 0.0),
            ).astype(BF16)
            piece = jnp.concatenate([piece, none[: CA - 2 * PAIR_PAD]], axis=0)
            blocks.append(jnp.concatenate([piece, none] if s < 2 else [none, piece], axis=1))
        return jnp.concatenate(blocks, axis=0)

    def bias_picks(ids):
        hit = token_of == ids
        return jnp.concatenate(
            [(hit & (head_of == h)).astype(F32).astype(BF16) for h in range(HEADS)], axis=1
        )

    def bias_of(taken, n, tile, picks):
        return nn(nn(taken, table_of(n, tile)).astype(BF16), picks)

    def right_rows(values):
        return jnp.concatenate(
            [values[HALF:ATOMS], values[ATOMS : ATOMS + HALF], values[EXT : EXT + HALF]], axis=0
        )

    def left_rows(values):
        return jnp.concatenate(
            [values[:HALF], values[ATOMS + HALF : EXT], values[EXT + HALF :]], axis=0
        )

    low_all = jnp.concatenate([low] * HEADS, axis=1)

    def attend(kv_n, heads, bias_n):
        scores = nn(kv_n[:EXT, :CA], heads) * SCALE + bias_n
        values_t = flip(kv_n[:EXT, CA:])
        exps = jnp.exp(scores - jnp.max(scores, axis=0, keepdims=True))
        weights = exps * (1.0 / jnp.sum(exps, axis=0, keepdims=True))
        rounded = weights.astype(BF16)
        attended = jnp.concatenate(
            [
                nn(
                    values_t[width * h : width * (h + 1)],
                    rounded[:, ATOMS * h : ATOMS * (h + 1)],
                )
                for h in range(HEADS)
            ],
            axis=0,
        )
        return attended, weights, rounded

    def attend_own(n, kv_n, heads):
        attended, weights, rounded = attend(kv_n, heads, bias[n])
        soft[n] = weights
        soft_b[n] = rounded
        key_t[n] = flip(kv_n[:EXT, :CA])
        return attended

    def attend_rim(n, kv_n, heads):
        right_kv = right_rows(kv_n)
        left_kv = left_rows(kv_n)
        scores = jnp.where(
            low_all, nn(right_kv[:, :CA], heads), nn(left_kv[:, :CA], heads)
        )
        scores = scores * SCALE + bias_rim[...]
        most = jnp.maximum(jnp.max(scores, axis=0, keepdims=True), -1e29)
        exps = jnp.exp(scores - most)
        weights = exps * (1.0 / jnp.maximum(jnp.sum(exps, axis=0, keepdims=True), 1e-30))
        soft_rim[...] = weights
        rounded = weights.astype(BF16)
        near = weights[:HALF]
        soft_rim_own[:HALF] = jnp.where(low_all, 0.0, near).astype(BF16)
        soft_rim_own[HALF:] = jnp.where(low_all, near, 0.0).astype(BF16)
        right_t = flip(right_kv[:, CA:])
        left_t = flip(left_kv[:, CA:])
        parts = []
        for h in range(HEADS):
            here = rounded[:, ATOMS * h : ATOMS * (h + 1)]
            parts.append(
                jnp.where(
                    low,
                    nn(right_t[width * h : width * (h + 1)], here),
                    nn(left_t[width * h : width * (h + 1)], here),
                )
            )
        return jnp.concatenate(parts, axis=0)

    def transition(n, stream, gates, attended, lanes):
        gated = gates * attended
        x_mid = stream + nn(out_t[n], gated.astype(BF16))
        normal, scaling = norm_rows(x_mid)
        widened = nn(in_t[n], normal.astype(BF16))
        part_a = widened[:FFA]
        part_b = widened[FFA:]
        sig = jax.nn.sigmoid(part_a)
        act = part_a * sig
        if lanes:
            gating[n, :, :lanes] = gates
            gate_back[n] = gated[:, :ATOMS] * (1.0 - gates[:, :ATOMS])
            normal_m[n, :, :lanes] = normal
            scale_m[n, :, :lanes] = scaling
            silu_a[n, :, :lanes] = act
            back_a[n, :, :lanes] = part_b * (sig * (1.0 + part_a * (1.0 - sig)))
        return x_mid + nn(down_t[n], (act * part_b).astype(BF16))

    def local_layer(n, stream_ext):
        normal_ext, scale_ext = norm_rows(stream_ext)
        normal_x[n] = normal_ext
        scale_x[n] = scale_ext
        rows_ext = flip(normal_ext.astype(BF16))
        kv[n // 2] = nn(rows_ext, attn_in_ref[n, :, CA : 3 * CA]).astype(BF16)
        normed = normal_ext[:, :ATOMS].astype(BF16)
        heads = by_head(nn(query_t[n], normed).astype(BF16))
        q_heads[n] = flip(heads)
        gates = jax.nn.sigmoid(nn(gate_t[n], normed))
        if n == 0:
            own_picks[...] = bias_picks(own_ids)
            takes[:EXT] = take_of(jnp.concatenate([own_id_cols, halo_id_cols], axis=0))
            arrive(pair_copies)
            bias[0] = bias_of(takes[:EXT], 0, 0, own_picks[...]) + outside
        attended = attend_own(n, kv[n // 2], heads)
        return transition(n, stream_ext[:, :ATOMS], gates, attended, ATOMS)

    stream = local_layer(0, stream_ext)
    late_copies = send_all(
        [(cot_hbm, cot_buf.at[1 - ds, dr], ds, dr, dc) for ds, dr, dc in COND_PARTNERS if abs(ds) < REACH]
        + [(agg_hbm, agg_buf, 0, 1, 0)]
    )


    normal, scaling = norm_rows(stream)
    normal_x[1, :, :ATOMS] = normal
    scale_x[1, :, :ATOMS] = scaling
    normed = normal.astype(BF16)
    rows_own = flip(normed)
    kv_wide[:ATOMS] = nn(rows_own, attn_in_ref[1, :, CA : 3 * CA]).astype(BF16)
    own_heads = by_head(nn(query_t[1], normed).astype(BF16))
    q_heads[1] = flip(own_heads)
    own_gates = jax.nn.sigmoid(nn(gate_t[1], normed))
    outer_ids = pltpu.roll(jnp.where(low, ids_at[-1], ids_at[1]), HALF, 1)
    takes[EXT:] = take_of(as_cols(outer_ids))
    mixed = nn(takes[...], table_of(1, 0)).astype(BF16)
    bias[1] = nn(mixed[:EXT], own_picks[...]) + outside
    rim_full = nn(mixed, bias_picks(halo_ids))
    rim_rows = iota((3 * HALF, ATOMS), 0)
    left_position = jnp.where(
        rim_rows < HALF,
        rim_rows,
        jnp.where(rim_rows < ATOMS, rim_rows - ATOMS, rim_rows - EXT),
    )
    rim_position = jnp.where(low, HALF + rim_rows, left_position)
    rim_first = jnp.where(low, id_buf[REACH + 1, 1:2], id_buf[REACH - 1, 1:2]) - atom_base
    rim_outside = jnp.where(
        (rim_position >= rim_first) & (rim_position < rim_first + KW), 0.0, -1e30
    )
    bias_rim[...] = jnp.where(low_all, right_rows(rim_full), left_rows(rim_full)) + jnp.concatenate(
        [rim_outside] * HEADS, axis=1
    )
    bias[2] = bias_of(takes[:EXT], 2, 0, own_picks[...]) + outside
    at_token = jnp.concatenate([own_id_cols, halo_id_cols], axis=0) == iota((EXT, CA), 1)
    pick_t = at_token[:ATOMS].astype(F32).astype(BF16)[:, :SPAN]
    token_atoms = jnp.sum(at_token.astype(F32), axis=0, keepdims=True)
    atom_counts = jnp.sum(jnp.where(at_token[:ATOMS], token_atoms, 0.0), axis=1, keepdims=True)
    inverse = 1.0 / jnp.maximum(atom_counts, 1.0)

    arrive(far_copies)
    ids_at.update({ds: id_buf[REACH + ds, 0:1] - token_base for ds in (-2, 2)})
    side_ids = jnp.concatenate(
        [ids_at[1], ids_at[-1], jnp.where(low, ids_at[2], ids_at[-2])], axis=1
    )
    pick_side = (iota((SLOTS * TOK, 3 * ATOMS), 0) - TOK == side_ids).astype(F32).astype(BF16)
    stream_side = jnp.concatenate(beside_atoms + [flip(halo_buf[...]).astype(F32)], axis=1) + nn(
        conditioning(slice(0, SLOTS)), pick_side
    )
    normal_side, _ = norm_rows(stream_side)
    normed_side = normal_side.astype(BF16)
    rows_side = flip(normed_side)
    kv_side[...] = nn(rows_side, attn_in_ref[0, :, CA : 3 * CA]).astype(BF16)
    queries = nn(query_t[0], normed_side[:, :EXT]).astype(BF16)
    gates = jax.nn.sigmoid(nn(gate_t[0], normed_side[:, :EXT]))
    kv_of = {
        1: [kv_side[:ATOMS], kv_side[EXT : EXT + HALF], kv[0, HALF:ATOMS]],
        -1: [kv_side[ATOMS:EXT], kv[0, :HALF], kv_side[EXT + HALF :]],
    }
    attended = []
    for place, tile in enumerate((1, -1)):
        here = ids_at[tile] - TOK * tile
        there = jnp.where(low, ids_at[tile + 1], ids_at[tile - 1]) - TOK * tile
        taken = take_of(jnp.concatenate([as_cols(here), as_cols(there)], axis=0))
        bias_here = bias_of(taken, 0, tile, bias_picks(here)) + mask_of(tile)
        attended.append(
            attend(
                jnp.concatenate(kv_of[tile], axis=0),
                by_head(queries[:, ATOMS * place : ATOMS * (place + 1)]),
                bias_here,
            )[0]
        )
    stream_side = transition(
        0, stream_side[:, :EXT], gates, jnp.concatenate(attended, axis=1), 0
    )

    rows_side = flip(norm_rows(stream_side)[0].astype(BF16))
    rows_right, rows_left = rows_side[:ATOMS], rows_side[ATOMS:]
    rows_side = jnp.concatenate(
        [rows_right[:HALF], rows_left[HALF:], rows_right[HALF:], rows_left[:HALF]], axis=0
    )
    kv_wide[ATOMS:] = nn(rows_side, attn_in_ref[1, :, CA : 3 * CA]).astype(BF16)
    rim_heads = by_head(nt(query_t[1], rows_side[:ATOMS]).astype(BF16))
    q_rim[...] = flip(rim_heads)
    gates = jnp.concatenate(
        [own_gates, jax.nn.sigmoid(nt(gate_t[1], rows_side[:ATOMS]))], axis=1
    )
    attended = jnp.concatenate([attend_own(1, kv_wide, own_heads), attend_rim(1, kv_wide, rim_heads)], axis=1)
    stream_ext = jnp.concatenate(
        [stream, jnp.where(low, stream_side[:, :ATOMS], stream_side[:, ATOMS:])], axis=1
    )
    stream_ext = transition(1, stream_ext, gates, attended, EXT)

    stream = local_layer(2, stream_ext)

    final = flip(stream.astype(BF16))
    arrive(late_copies)
    gradient = None
    for part in range(2):
        weights = agg_ref[...] if part == 0 else agg_buf[...]
        pre = nn(final, weights)
        sig = jax.nn.sigmoid(pre)
        d_act = nn(pick_t, cot_buf[:, part].reshape(SPAN, ACT)) * inverse
        d_pre = (d_act * (sig * (1.0 + pre * (1.0 - sig)))).astype(BF16)
        term = nt(weights, d_pre)
        gradient = term if part == 0 else gradient + term
        if part == 0:
            high, rest = split(pre * sig)
            sums = nn(pick, high) + nn(pick, rest)
            sums_send[0] = sums[:TOK].astype(BF16)
            sums_send[1] = sums[2 * TOK :].astype(BF16)
            own_sums = sums[TOK : 2 * TOK]
            sums_copies = send_all(
                [
                    (sums_send.at[(ds + 1) // 2], sums_recv.at[(ds + 1) // 2], ds, 0, 0)
                    for ds in SIDES
                ]
            )

    def d_middle(n, upstream, lanes):
        d_transit = nn(trans_out_ref[n], upstream.astype(BF16))
        d_wide = jnp.concatenate(
            [
                (d_transit * back_a[n, :, :lanes]).astype(BF16),
                (d_transit * silu_a[n, :, :lanes]).astype(BF16),
            ],
            axis=0,
        )
        d_mid = upstream + norm_back(
            normal_m[n, :, :lanes], scale_m[n, :, :lanes], nn(trans_in_ref[n], d_wide)
        )
        return d_mid, nn(attn_out_ref[n], d_mid.astype(BF16))

    def d_own(n, kv_n, d_heads, d_att):
        own_d = nn(kv_n[:ATOMS, CA:], d_heads)
        halo_d = nn(kv_n[ATOMS:EXT, CA:], d_heads)
        own_prod = soft[n, :ATOMS] * own_d
        halo_prod = soft[n, ATOMS:] * halo_d
        inner = jnp.sum(own_prod, axis=0, keepdims=True) + jnp.sum(
            halo_prod, axis=0, keepdims=True
        )
        halo_ds = ((halo_prod - soft[n, ATOMS:] * inner) * SCALE).astype(BF16)
        own_ds = ((own_prod - soft[n, :ATOMS] * inner) * SCALE).astype(BF16)
        d_queries = jnp.concatenate(
            [
                nn(
                    key_t[n, width * h : width * (h + 1), :ATOMS],
                    own_ds[:, ATOMS * h : ATOMS * (h + 1)],
                )
                + nn(
                    key_t[n, width * h : width * (h + 1), ATOMS:],
                    halo_ds[:, ATOMS * h : ATOMS * (h + 1)],
                )
                for h in range(HEADS)
            ],
            axis=0,
        ).astype(BF16)
        return d_queries, nn(own_ds, q_heads[n]), nn(soft_b[n, :ATOMS], d_att), halo_ds

    def weigh_kv(n, d_keys, d_vals):
        return nt(attn_in_ref[n, :, CA : 2 * CA], d_keys) + nt(
            attn_in_ref[n, :, 2 * CA : 3 * CA], d_vals
        )

    def local_back(n, upstream):
        slot = n // 2
        d_mid, d_gated = d_middle(n, upstream, ATOMS)
        d_heads = by_head((d_gated * gating[n, :, :ATOMS]).astype(BF16))
        d_att = flip(d_heads)
        d_gate = (d_gated * gate_back[n]).astype(BF16)
        d_queries, d_keys, d_vals, halo_ds = d_own(n, kv[slot], d_heads, d_att)
        beside = norm_back(
            normal_x[n, :, ATOMS:],
            scale_x[n, :, ATOMS:],
            weigh_kv(
                n,
                nn(halo_ds, q_heads[n]).astype(BF16),
                nn(soft_b[n, ATOMS:], d_att).astype(BF16),
            ),
        )
        d_normed = (
            nn(attn_in_ref[n, :, :CA], d_queries)
            + nn(attn_in_ref[n, :, 3 * CA :], d_gate)
            + weigh_kv(n, d_keys.astype(BF16), d_vals.astype(BF16))
        )
        part = d_mid + norm_back(normal_x[n, :, :ATOMS], scale_x[n, :, :ATOMS], d_normed)
        edge_send[slot, 0] = jnp.where(low, part, beside).astype(BF16)
        edge_send[slot, 1] = jnp.where(low, beside, part).astype(BF16)
        arrive(
            send_all(
                [
                    (edge_send.at[slot, side], edge_recv.at[slot, side], ds, 0, 0)
                    for side, ds in enumerate(SIDES)
                ]
            )
        )
        from_right, from_left = edge_recv[slot, 0].astype(F32), edge_recv[slot, 1].astype(F32)
        return jnp.concatenate(
            [
                part + jnp.where(low, from_left, from_right),
                beside + jnp.where(low, from_right, from_left),
            ],
            axis=1,
        )

    gradient = local_back(2, gradient)

    d_mid, d_gated = d_middle(1, gradient, EXT)
    d_att_t = (d_gated * gating[1]).astype(BF16)
    d_heads = by_head(d_att_t[:, :ATOMS])
    d_att = flip(d_heads)
    d_heads_rim = by_head(d_att_t[:, ATOMS:])
    d_att_rim = flip(d_heads_rim)
    d_gate = (d_gated[:, :ATOMS] * gate_back[1]).astype(BF16)
    d_queries, d_keys, d_vals, _ = d_own(1, kv_wide, d_heads, d_att)
    rim_d = jnp.where(
        low_all,
        nn(right_rows(kv_wide[:, CA:]), d_heads_rim),
        nn(left_rows(kv_wide[:, CA:]), d_heads_rim),
    )
    rim_prod = soft_rim[...] * rim_d
    rim_inner = jnp.sum(rim_prod, axis=0, keepdims=True)
    rim_ds = (rim_prod[:HALF] - soft_rim[:HALF] * rim_inner) * SCALE
    rim_ds = jnp.concatenate(
        [jnp.where(low_all, 0.0, rim_ds), jnp.where(low_all, rim_ds, 0.0)], axis=0
    ).astype(BF16)
    d_keys = d_keys + nn(rim_ds, q_rim[...])
    d_vals = d_vals + nn(soft_rim_own[...], d_att_rim)
    d_normed = (
        nn(attn_in_ref[1, :, :CA], d_queries)
        + nn(attn_in_ref[1, :, 3 * CA :], d_gate)
        + weigh_kv(1, d_keys.astype(BF16), d_vals.astype(BF16))
    )
    gradient = d_mid[:, :ATOMS] + norm_back(
        normal_x[1, :, :ATOMS], scale_x[1, :, :ATOMS], d_normed
    )

    def per_token(picks, values):
        high, rest = split(values)
        return nt(picks, high) + nt(picks, rest)

    arrive(sums_copies)
    token_sums = own_sums + (sums_recv[0].astype(F32) + sums_recv[1].astype(F32))
    diagonal = iota((TOK, TOK), 0) == iota((TOK, TOK), 1)
    counts = jnp.sum(
        jnp.where(diagonal, counts_ref[...].astype(F32), 0.0), axis=1, keepdims=True
    )
    act_out[...] = (token_sums / counts).astype(BF16)
    gradient = local_back(0, gradient)
    grad_out[...] = flip(gradient[:, :ATOMS].astype(BF16))
    d_cond = per_token(pick_ext[TOK : 2 * TOK], gradient)
    high, rest = split(d_cond)
    single_out[...] = (nt(high, proj_ref[...]) + nt(rest, proj_ref[...])).astype(BF16)
    for side in (0, -1, 1, -2, 2):
        each(copies, side, side, lambda copy: copy.wait_send())


N_COPIES = 9 + 4 + 4 + 19 + 5 + 1 + 2 + 2 + 2


def hand_on(act, grad, single, act_out, grad_out, single_out):
    act_out[...] = act[...]
    grad_out[...] = grad[...]
    single_out[...] = single[...]


def local(
    atom_single,
    token_single,
    pair_band,
    token_counts,
    atom_token,
    window_starts,
    single_proj,
    pair_proj,
    attn_in,
    attn_out,
    trans_in,
    trans_out,
    agg_proj,
    token_cot,
):
    vmem = pl.BlockSpec(memory_space=pltpu.VMEM)
    hbm = pl.BlockSpec(memory_space=pltpu.HBM)

    def scratch(dtype, *shape):
        return pltpu.VMEM(shape, dtype)

    results = (
        jax.ShapeDtypeStruct((TOK, ACT), BF16),
        jax.ShapeDtypeStruct((ATOMS, CA), BF16),
        jax.ShapeDtypeStruct((TOK, COND), BF16),
    )
    results_here = pl.pallas_call(
        kernel,
        out_shape=results,
        in_specs=[hbm] * 14,
        out_specs=(vmem, vmem, vmem),
        scratch_shapes=[
            scratch(BF16, ATOMS, CA),
            scratch(BF16, TOK, COND),
            scratch(BF16, PAIR_ROWS, PAIR_COLS, CA),
            scratch(jnp.int32, 1, TOK),
            scratch(jnp.int32, 1, ATOMS),
            pltpu.SMEM((ATOMS // QB,), jnp.int32),
            scratch(BF16, COND, CA),
            scratch(F32, LAYERS * HEADS, CA),
            scratch(BF16, LAYERS, CA, 4 * CA),
            scratch(BF16, LAYERS, CA, CA),
            scratch(BF16, LAYERS, CA, 2 * FFA),
            scratch(BF16, LAYERS, FFA, CA),
            scratch(BF16, CA, ACT),
            scratch(jnp.int32, SLOTS, 2, ATOMS),
            scratch(BF16, ATOMS, CA),
            scratch(F32, SLOTS, 2, TOK, CA),
            scratch(BF16, SLOTS, 2 * PAIR_PAD, 2 * CA),
            scratch(BF16, 3, 2, TOK, ACT),
            scratch(BF16, CA, ACT),
            scratch(BF16, 2, ATOMS, CA),
            scratch(BF16, 3 * ATOMS, 2 * CA),
            scratch(BF16, 2, EXT, 2 * CA),
            scratch(BF16, 3 * ATOMS, 2 * CA),
            scratch(F32, LAYERS, EXT, ALL),
            scratch(F32, 3 * HALF, ALL),
            scratch(BF16, 3 * ATOMS, 3 * CA),
            scratch(BF16, LAYERS, CA, CA),
            scratch(BF16, LAYERS, CA, CA),
            scratch(BF16, LAYERS, CA, CA),
            scratch(BF16, LAYERS, 2 * FFA, CA),
            scratch(BF16, LAYERS, CA, FFA),
            scratch(F32, LAYERS, EXT, ALL),
            scratch(BF16, LAYERS, EXT, ALL),
            scratch(F32, 3 * HALF, ALL),
            scratch(BF16, ATOMS, ALL),
            scratch(BF16, LAYERS, ALL, CA),
            scratch(BF16, ALL, CA),
            scratch(BF16, LAYERS, CA, EXT),
            scratch(F32, LAYERS, CA, EXT),
            scratch(F32, LAYERS, 1, EXT),
            scratch(F32, LAYERS, CA, EXT),
            scratch(F32, LAYERS, 1, EXT),
            scratch(F32, LAYERS, CA, EXT),
            scratch(F32, LAYERS, CA, ATOMS),
            scratch(F32, LAYERS, FFA, EXT),
            scratch(F32, LAYERS, FFA, EXT),
            scratch(BF16, 2 * CA, ALL),
            scratch(BF16, 2, 2, CA, ATOMS),
            scratch(BF16, 2, 2, CA, ATOMS),
            scratch(BF16, 2, TOK, ACT),
            scratch(BF16, 2, TOK, ACT),
            pltpu.SemaphoreType.DMA((14,)),
            pltpu.SemaphoreType.REGULAR((2,)),
            pltpu.SemaphoreType.DMA((N_COPIES,)),
            pltpu.SemaphoreType.DMA((N_COPIES,)),
        ],
        compiler_params=pltpu.CompilerParams(
            collective_id=0, has_side_effects=True, vmem_limit_bytes=64 * 1024 * 1024
        ),
        cost_estimate=pl.CostEstimate(
            flops=2_000_000_000, bytes_accessed=2_000_000, transcendentals=1_000_000
        ),
        name="atoms",
    )(
        atom_single,
        token_single,
        pair_band,
        token_counts.reshape(1, TOK),
        atom_token.reshape(1, ATOMS),
        window_starts,
        single_proj,
        pair_proj.T,
        attn_in,
        attn_out,
        trans_in,
        trans_out,
        agg_proj,
        token_cot,
    )
    return pl.pallas_call(
        hand_on,
        out_shape=results,
        in_specs=[vmem] * 3,
        out_specs=(vmem,) * 3,
        name="results",
    )(*results_here)


def solution(mesh):
    return jax.shard_map(
        local,
        mesh=mesh,
        in_specs=(
            P("seq", None),
            P("seq", "row"),
            P(("seq", "row"), "col", None),
            P("seq"),
            P("seq"),
            P("seq"),
            P("row", None),
            P(),
            P(),
            P(),
            P(),
            P(),
            P(None, "row"),
            P("seq", "row"),
        ),
        out_specs=(P("seq", "row"), P("seq", None), P("seq", "row")),
        check_vma=False,
    )
```
